256 devices in a mesh: gx: 16 (over x, y), gy: 16 (over z, core).
Axes of the slice: x: 4, y: 4, z: 8, core: 2. Of those that a mesh axis runs over, the one named last changes fastest.
Arguments:
- source: float32 [8, 8, 32, 64, 256], P(None, None, 'gx', 'gy'), may hold values from -6 to 6
- geometry: float32 [3, 32, 64, 32], P(None, 'gx', 'gy'), may hold values from 0.5 to 2
- disc_mask: int32 [32, 64, 32], P('gx', 'gy'), may hold values 0 or 1
- thrust: float32 [32, 64, 32], P('gx', 'gy'), may hold values from 0.5 to 4
- xxt_factor: float32 [9, 32, 524288], P(None, None, ('gx', 'gy')), as said below
- col_count: int32 [9, 256], P(None, ('gx', 'gy')), may hold values from 8 to 32, as said below
Outputs:
- pressure: float32 [8, 8, 32, 64, 256], P(None, None, 'gx', 'gy')
The draws below stay inside these ranges and needn't reach their ends.
Inputs may be any that keep to these rules, and one draw needn't show every extreme that they name: `col_count`: equal on all devices of a level-l group (flat device index along gx+gy agreeing after the lowest l bits are dropped); at every level some group has exactly 32. `xxt_factor`: Real-valued entries of order one or below.
All inputs are finite; a program needn't handle non-finite values. No bound on the sum of `disc_mask` on one device may be relied on, other than what follows from the above.
Results may differ from the reference program's by a relative error of at most 0.00018.
Values sent between devices are 32-bit elements; how exact they have to be, the bound alone decides.
A program may use at most 128 MiB of HBM per device.

```python
import math
import jax
import jax.numpy as jnp
import numpy as np
from jax import lax

NODES = 8
EX = 2
EY = 4
EZ = 32
CYCLES = 2
CHEB_DEGREE = 2
XCOLS = 32
NEX = 32
NEY = 64
ZN = 256
RANKS = 256
SEP_LEVELS = 9
NC = 2048
COARSE = 524288
N_GX = 16
N_GY = 16


def draw_xxt_factor(key, part):
    full_shape = (SEP_LEVELS, XCOLS, COARSE)
    level_index = jnp.arange(SEP_LEVELS, dtype=jnp.float32)[:, None, None]
    level_scale = 1.4 * (XCOLS * NC * 2.0 ** level_index) ** (-0.25)
    noise_draw = jax.random.normal(key, full_shape, jnp.float32)
    return noise_draw * level_scale


def draw_col_count(key, part):
    level_index = jnp.arange(SEP_LEVELS, dtype=jnp.int32)[:, None]
    device = jnp.arange(RANKS, dtype=jnp.int32)[None, :]
    base_counts = jax.random.randint(key, (SEP_LEVELS, RANKS), XCOLS // 4, XCOLS + 1, dtype=jnp.int32)
    group_index = jnp.right_shift(device, level_index)
    counts = jnp.take_along_axis(base_counts, group_index, axis=1)
    chosen = jax.random.randint(jax.random.fold_in(key, 7), (SEP_LEVELS, 1), 0, RANKS, dtype=jnp.int32)
    counts = jnp.where(group_index == jnp.right_shift(chosen, level_index), XCOLS, counts)
    return counts.astype(jnp.int32)


def plant(entries, stream_key, low, largest):
    shape = entries.shape
    spot = [jax.random.randint(jax.random.fold_in(stream_key, axis), (), 0, shape[axis]) for axis in range(len(shape))]
    entries = entries.at[tuple(spot)].set(low)
    longest = shape.index(max(shape))
    spot[longest] = (spot[longest] + 1) % shape[longest]
    return entries.at[tuple(spot)].set(largest)


def block_scale(key, shape, cuts, low, high):
    level, own = 1.0, jax.random.fold_in(key, 6)
    for dim, parts in cuts:
        heights = jnp.exp(jax.random.uniform(jax.random.fold_in(own, dim), (parts,), jnp.float32, low / len(cuts), high / len(cuts)))
        level = level * jnp.repeat(heights, shape[dim] // parts).reshape([-1 if axis == dim else 1 for axis in range(len(shape))])
    return level


def centred(rng, shape, width, limit, split=(), held_as=jnp.bfloat16):
    entries = width * jax.random.normal(rng, shape, jnp.float32)
    if split:
        entries = entries * block_scale(rng, shape, split, -0.22, 0.18)
    return jnp.clip(entries, -limit, limit).astype(held_as)


def setup_inputs(seed: int = 0) -> dict:
    streams_of = jax.random.split(jax.random.key(seed), 7)
    source = centred(streams_of[0], (NODES, NODES, NEX, NEY, ZN), 1.0, 6.0, ((2, 16), (3, 16)), jnp.float32)
    geometry = jnp.clip(jnp.exp(math.log(2.0) - 1.3862944 * jax.random.uniform(streams_of[1], (3, NEX, NEY, EZ), jnp.float32) ** block_scale(streams_of[1], (3, NEX, NEY, EZ), ((1, 16), (2, 16)), -0.2, 0.2)), 0.5, 2.0)
    disc_mask = plant((jax.random.randint(streams_of[2], (NEX, NEY, EZ), 0, 8) < 1).astype(jnp.int32), jax.random.fold_in(streams_of[2], 1), 0, 1)
    thrust = jnp.clip(jnp.exp(math.log(4.0) - 2.0794415 * jax.random.uniform(streams_of[3], (NEX, NEY, EZ), jnp.float32) ** block_scale(streams_of[3], (NEX, NEY, EZ), ((0, 16), (1, 16)), -0.2, 0.2)), 0.5, 4.0)
    xxt_factor = draw_xxt_factor(jax.random.fold_in(streams_of[6], 71), 0)
    col_count = draw_col_count(jax.random.fold_in(streams_of[6], 71), 0)
    return dict(source=source, geometry=geometry, disc_mask=disc_mask, thrust=thrust, xxt_factor=xxt_factor, col_count=col_count)


highest = lax.Precision.HIGHEST
bound_low = 0.3
bound_high = 3.0
shift_ratio = 0.25

def legendre_table(points, poly_order):
    table = [points * 0.0 + 1.0, points]
    for degree in range(2, poly_order + 1):
        table.append(((2.0 * degree - 1.0) * points * table[-1] - (degree - 1.0) * table[-2]) / degree)
    return table

def jacobi_eigen(matrix):
    size_n = matrix.shape[0]
    current = matrix.copy()
    vectors = np.eye(size_n)
    for sweep_index in range(30):
        for first in range(size_n - 1):
            for second in range(first + 1, size_n):
                angle = 0.5 * math.atan2(2.0 * float(current[first, second]), float(current[second, second] - current[first, first]))
                rotation = np.eye(size_n)
                rotation[first, first] = math.cos(angle)
                rotation[second, second] = math.cos(angle)
                rotation[first, second] = math.sin(angle)
                rotation[second, first] = -math.sin(angle)
                current = rotation.T @ current @ rotation
                vectors = vectors @ rotation
    values = np.array([current[index, index] for index in range(size_n)])
    order = np.argsort(values)
    return (values[order], vectors[:, order])

def gll_tables(node_count):
    poly_order = node_count - 1
    points = np.cos(np.pi * np.arange(node_count) / poly_order)
    for newton_index in range(200):
        table = legendre_table(points, poly_order)
        points = points - (points * table[poly_order] - table[poly_order - 1]) / (node_count * table[poly_order])
    points = points[::-1].copy()
    legendre = legendre_table(points, poly_order)[poly_order]
    weights = 2.0 / (poly_order * (poly_order + 1) * legendre ** 2)
    identity = np.eye(node_count)
    gap_matrix = points[:, None] - points[None, :] + identity
    off_diagonal = legendre[:, None] / (legendre[None, :] * gap_matrix) * (1.0 - identity)
    end_value = poly_order * (poly_order + 1) / 4.0
    end_terms = np.concatenate([[-end_value], np.zeros(node_count - 2), [end_value]])
    derivative = off_diagonal + identity * end_terms[None, :]
    stiffness = derivative.T @ (weights[:, None] * derivative)
    root_inverse = 1.0 / np.sqrt(weights)
    symmetric = root_inverse[:, None] * stiffness * root_inverse[None, :]
    symmetric = 0.5 * (symmetric + symmetric.T)
    eigen_values, eigen_vectors = jacobi_eigen(symmetric)
    eigen_modes = root_inverse[:, None] * eigen_vectors
    vertex_interp = np.stack([(1.0 - points) / 2.0, (1.0 + points) / 2.0], axis=1)
    return (weights.astype(np.float32), stiffness.astype(np.float32), eigen_modes.astype(np.float32), eigen_values.astype(np.float32), vertex_interp.astype(np.float32))

def build_setup(geometry):
    weights, stiffness, eigen_modes, eigen_values, vertex_interp = gll_tables(NODES)
    elem_z = geometry.shape[3]
    z_count = elem_z * NODES
    lengths = jnp.repeat(geometry, NODES, axis=3)
    len_x = lengths[0][None, None]
    len_y = lengths[1][None, None]
    len_z = lengths[2][None, None]
    metric_x = len_y * len_z / (2.0 * len_x)
    metric_y = len_x * len_z / (2.0 * len_y)
    metric_z = len_x * len_y / (2.0 * len_z)
    node_weight = jnp.asarray(weights)
    weight_a = node_weight[:, None, None, None, None]
    weight_b = node_weight[None, :, None, None, None]
    weight_c = jnp.tile(node_weight, elem_z)
    coef_x = metric_x * weight_b * weight_c
    coef_y = metric_y * weight_a * weight_c
    coef_z = metric_z * weight_a * weight_b
    mass_diag = len_x * len_y * len_z / 8.0 * weight_a * weight_b * weight_c
    spectrum = jnp.asarray(eigen_values)
    denominator = metric_x * spectrum[:, None, None, None, None] + metric_y * spectrum[None, :, None, None, None] + metric_z * jnp.tile(spectrum, elem_z) + shift_ratio * (metric_x + metric_y + metric_z)
    inv_denom = 1.0 / denominator
    z_index = jnp.arange(z_count)
    z_node = z_index % NODES
    dirichlet = (z_index < z_count - 1).astype(jnp.float32)
    node_index = jnp.arange(NODES)
    edge_node = ((node_index == 0) | (node_index == NODES - 1)).astype(jnp.float32) + 1.0
    z_shared = 1.0 + ((z_node == 0) & (z_index > 0)).astype(jnp.float32) + ((z_node == NODES - 1) & (z_index < z_count - 1)).astype(jnp.float32)
    inv_mult = 1.0 / (edge_node[:, None, None, None, None] * edge_node[None, :, None, None, None] * z_shared)
    eye_z = jnp.eye(elem_z, dtype=jnp.float32)
    stiff_matrix = jnp.asarray(stiffness)
    mode_matrix = jnp.asarray(eigen_modes)
    interp = jnp.asarray(vertex_interp)
    z_stiff = jnp.kron(eye_z, stiff_matrix.T)
    z_modes = jnp.kron(eye_z, mode_matrix)
    z_modes_t = jnp.kron(eye_z, mode_matrix.T)
    z_restrict = jnp.kron(eye_z, interp)
    z_prolong = jnp.kron(eye_z, interp.T)
    link_up = (z_index[None, :] == z_index[:, None] + 1) & (z_node[:, None] == NODES - 1)
    link_down = (z_index[None, :] == z_index[:, None] - 1) & (z_node[:, None] == 0)
    z_sum = ((z_index[:, None] == z_index[None, :]) | link_up | link_down).astype(jnp.float32)
    return (coef_x, coef_y, coef_z, mass_diag, inv_denom, dirichlet, inv_mult, stiff_matrix, mode_matrix, z_stiff, z_modes, z_modes_t, z_restrict, z_prolong, z_sum, interp)

def pair_sum_x(data_field, prev_high, next_low):
    low_face = data_field[0]
    high_face = data_field[-1]
    before_faces = jnp.concatenate([prev_high[:, None], high_face[:, :-1]], axis=1)
    after_faces = jnp.concatenate([low_face[:, 1:], next_low[:, None]], axis=1)
    return jnp.concatenate([(low_face + before_faces)[None], data_field[1:-1], (high_face + after_faces)[None]], axis=0)

def pair_sum_y(data_field, prev_high, next_low):
    low_face = data_field[:, 0]
    high_face = data_field[:, -1]
    before_faces = jnp.concatenate([prev_high[:, :, None], high_face[:, :, :-1]], axis=2)
    after_faces = jnp.concatenate([low_face[:, :, 1:], next_low[:, :, None]], axis=2)
    return jnp.concatenate([(low_face + before_faces)[:, None], data_field[:, 1:-1], (high_face + after_faces)[:, None]], axis=1)

def assemble_wrap(data_field, z_sum):
    data_field = pair_sum_x(data_field, data_field[-1][:, -1], data_field[0][:, 0])
    data_field = pair_sum_y(data_field, data_field[:, -1][:, :, -1], data_field[:, 0][:, :, 0])
    return jnp.matmul(data_field, z_sum, precision=highest)

def chebyshev(solution, resid, apply_op, precond, keep_resid):
    center = 0.5 * (bound_high + bound_low)
    radius = 0.5 * (bound_high - bound_low)
    center_ratio = center / radius
    rho_old = 1.0 / center_ratio
    direction = precond(resid) / center
    for step_index in range(CHEB_DEGREE):
        solution = solution + direction
        if step_index < CHEB_DEGREE - 1 or keep_resid:
            resid = resid - apply_op(direction)
        if step_index < CHEB_DEGREE - 1:
            rho_new = 1.0 / (2.0 * center_ratio - rho_old)
            direction = rho_new * rho_old * direction + 2.0 * rho_new / radius * precond(resid)
            rho_old = rho_new
    return (solution, resid)

def pressure_solve(source, disc_mask, thrust, setup_tables, assembler, coarse_solve):
    coef_x, coef_y, coef_z, mass_diag, inv_denom, dirichlet, inv_mult, stiff_matrix, mode_matrix, z_stiff, z_modes, z_modes_t, z_restrict, z_prolong, z_sum, interp = setup_tables

    def apply_op(data_field):
        along_x = jnp.einsum('ac,cbxyz->abxyz', stiff_matrix, data_field, precision=highest)
        along_y = jnp.einsum('bc,acxyz->abxyz', stiff_matrix, data_field, precision=highest)
        along_z = jnp.matmul(data_field, z_stiff, precision=highest)
        return dirichlet * assembler(coef_x * along_x + coef_y * along_y + coef_z * along_z, z_sum)

    def precond(resid):
        spectral = jnp.einsum('ai,abxyz->ibxyz', mode_matrix, resid, precision=highest)
        spectral = jnp.einsum('bj,abxyz->ajxyz', mode_matrix, spectral, precision=highest)
        spectral = jnp.matmul(spectral, z_modes, precision=highest) * inv_denom
        spectral = jnp.einsum('ai,ibxyz->abxyz', mode_matrix, spectral, precision=highest)
        spectral = jnp.einsum('bj,ajxyz->abxyz', mode_matrix, spectral, precision=highest)
        return dirichlet * inv_mult * assembler(jnp.matmul(spectral, z_modes_t, precision=highest), z_sum)

    def restrict(resid):
        coarse = jnp.einsum('av,abxyz->vbxyz', interp, inv_mult * resid, precision=highest)
        coarse = jnp.einsum('bu,vbxyz->vuxyz', interp, coarse, precision=highest)
        return jnp.matmul(coarse, z_restrict, precision=highest)

    def prolong(coarse):
        fine_field = jnp.einsum('av,vuxyz->auxyz', interp, coarse, precision=highest)
        fine_field = jnp.einsum('bu,auxyz->abxyz', interp, fine_field, precision=highest)
        return jnp.matmul(fine_field, z_prolong, precision=highest)
    forcing = source + jnp.repeat(disc_mask.astype(jnp.float32) * thrust, NODES, axis=2)[None, None]
    rhs_field = dirichlet * assembler(mass_diag * forcing, z_sum)
    solution = jnp.zeros_like(rhs_field)
    for sweep_index in range(CYCLES):
        if sweep_index == 0:
            resid = rhs_field
        else:
            resid = rhs_field - apply_op(solution)
        solution, resid = chebyshev(solution, resid, apply_op, precond, True)
        correction = coarse_solve(restrict(resid))
        solution = solution + dirichlet * inv_mult * assembler(prolong(correction), z_sum)
        resid = rhs_field - apply_op(solution)
        solution, resid = chebyshev(solution, resid, apply_op, precond, False)
    return solution

def coarse_reference(coarse, xxt_factor, col_count):
    z_pairs = coarse.shape[4]
    split_rows = coarse.reshape(2, 2, N_GX, EX, N_GY, EY, z_pairs)
    by_rank = split_rows.transpose(2, 4, 0, 1, 3, 5, 6).reshape(RANKS, NC)
    blocks = xxt_factor.reshape(SEP_LEVELS, XCOLS, RANKS, NC)
    partial_value = jnp.einsum('lkdn,dn->ldk', blocks, by_rank, precision=highest)
    level_sums = []
    for level_index in range(SEP_LEVELS):
        width_group = 2 ** level_index
        summed = partial_value[level_index].reshape(RANKS // width_group, width_group, XCOLS).sum(axis=1)
        level_sums.append(jnp.repeat(summed, width_group, axis=0))
    totals = jnp.stack(level_sums)
    live_mask = (jnp.arange(XCOLS)[None, None, :] < col_count[:, :, None]).astype(jnp.float32)
    totals = totals * live_mask
    rank_rows = jnp.einsum('lkdn,ldk->dn', blocks, totals, precision=highest)
    return rank_rows.reshape(N_GX, N_GY, 2, 2, EX, EY, z_pairs).transpose(2, 3, 0, 4, 1, 5, 6).reshape(coarse.shape)

def reference(source, geometry, disc_mask, thrust, xxt_factor, col_count):
    setup_tables = build_setup(geometry)

    def coarse_solve(coarse):
        return coarse_reference(coarse, xxt_factor, col_count)
    return pressure_solve(source, disc_mask, thrust, setup_tables, assemble_wrap, coarse_solve)
```

```python
import functools
import math

import jax
import jax.numpy as jnp
import ml_dtypes
import numpy as np
from jax import lax
from jax.experimental import pallas as pl
from jax.experimental.pallas import tpu as pltpu
from jax.sharding import PartitionSpec as P

NODES = 8
CYCLES = 2
EX = 2
EY = 4
EZ = 32
LANES = EY * EZ
XCOLS = 32
SMOOTH = 5

bound_low = 0.3
bound_high = 3.0
shift_ratio = 0.25
MESH = pl.DeviceIdType.MESH


def legendre_table(points, poly_order):
    table = [points * 0.0 + 1.0, points]
    for degree in range(2, poly_order + 1):
        table.append(
            ((2.0 * degree - 1.0) * points * table[-1] - (degree - 1.0) * table[-2]) / degree
        )
    return table


def jacobi_eigen(matrix):
    size_n = matrix.shape[0]
    current = matrix.copy()
    vectors = np.eye(size_n)
    for sweep_index in range(30):
        for first in range(size_n - 1):
            for second in range(first + 1, size_n):
                angle = 0.5 * math.atan2(
                    2.0 * float(current[first, second]),
                    float(current[second, second] - current[first, first]),
                )
                rotation = np.eye(size_n)
                rotation[first, first] = math.cos(angle)
                rotation[second, second] = math.cos(angle)
                rotation[first, second] = math.sin(angle)
                rotation[second, first] = -math.sin(angle)
                current = rotation.T @ current @ rotation
                vectors = vectors @ rotation
    values = np.array([current[index, index] for index in range(size_n)])
    order = np.argsort(values)
    return (values[order], vectors[:, order])


def gll_tables(node_count):
    poly_order = node_count - 1
    points = np.cos(np.pi * np.arange(node_count) / poly_order)
    for newton_index in range(200):
        table = legendre_table(points, poly_order)
        points = points - (points * table[poly_order] - table[poly_order - 1]) / (
            node_count * table[poly_order]
        )
    points = points[::-1].copy()
    legendre = legendre_table(points, poly_order)[poly_order]
    weights = 2.0 / (poly_order * (poly_order + 1) * legendre**2)
    identity = np.eye(node_count)
    gap_matrix = points[:, None] - points[None, :] + identity
    off_diagonal = legendre[:, None] / (legendre[None, :] * gap_matrix) * (1.0 - identity)
    end_value = poly_order * (poly_order + 1) / 4.0
    end_terms = np.concatenate([[-end_value], np.zeros(node_count - 2), [end_value]])
    derivative = off_diagonal + identity * end_terms[None, :]
    stiffness = derivative.T @ (weights[:, None] * derivative)
    root_inverse = 1.0 / np.sqrt(weights)
    symmetric = root_inverse[:, None] * stiffness * root_inverse[None, :]
    symmetric = 0.5 * (symmetric + symmetric.T)
    eigen_values, eigen_vectors = jacobi_eigen(symmetric)
    eigen_modes = root_inverse[:, None] * eigen_vectors
    vertex_interp = np.stack([(1.0 - points) / 2.0, (1.0 + points) / 2.0], axis=1)
    return weights, eigen_modes, eigen_values, vertex_interp


def mode_order(modes):
    even = [i for i in range(NODES) if modes[0, i] * modes[NODES - 1, i] > 0.0]
    odd = [i for i in range(NODES) if i not in even]
    return even, odd


def split_pair(matrix):
    exact = matrix.astype(np.float32)
    high = exact.astype(ml_dtypes.bfloat16)
    low = (exact - high.astype(np.float32)).astype(ml_dtypes.bfloat16)
    return np.concatenate([high, high, low], axis=1)


def constant_tables():
    weights, modes, values, interp = gll_tables(NODES)
    even, odd = mode_order(modes)
    half = NODES // 2
    mats = []
    for chosen in (even, odd):
        inverse = np.kron(modes[:half][:, chosen], np.kron(modes, modes))
        mats.append((split_pair(inverse.T), split_pair(inverse)))
    matrices = np.stack([mats[0][0], mats[1][0], mats[0][1], mats[1][1]])
    full = np.ones((NODES, LANES))
    edge = np.ones(NODES)
    edge[0] = edge[-1] = 0.5
    ez = np.arange(LANES)[None, :] % EZ
    node = np.arange(NODES)[:, None]
    z_shared = 1.0 + ((node == 0) & (ez > 0)) + ((node == NODES - 1) & (ez < EZ - 1))
    free = 1.0 - ((node == NODES - 1) & (ez == EZ - 1))
    rows = [values[i] * full for i in even + odd]
    rows += [value * full for value in values]
    rows += [weight * full for weight in weights]
    rows += [value * full for value in edge]
    rows += [values[:, None] * full, weights[:, None] * full, free / z_shared, free * full]
    rows += [interp[:, 0:1] * full, interp[:, 1:2] * full]
    table = np.stack(rows).astype(np.float32)
    perm = np.zeros((2 * LANES, 2 * LANES), np.float32)
    for t in range(2):
        for element in range(LANES):
            perm[t * LANES + element, 2 * element + t] = 1.0
    perms = np.stack([perm, perm.T]).astype(ml_dtypes.bfloat16)
    return matrices, table, perms, interp.astype(np.float32)


def flipped(index, bits):
    out = index
    bit = 1
    while bit <= bits:
        if bits & bit:
            out = out + bit - 2 * bit * lax.rem(lax.div(index, bit), 2)
        bit *= 2
    return out


def exact_rows(value, perm):
    first = value.astype(jnp.bfloat16)
    rest = value - first.astype(jnp.float32)
    second = rest.astype(jnp.bfloat16)
    third = (rest - second.astype(jnp.float32)).astype(jnp.bfloat16)
    parts = [
        jnp.dot(part, perm, preferred_element_type=jnp.float32)
        for part in (first, second, third)
    ]
    return parts[0] + parts[1] + parts[2]


def kernel(
    n_gx,
    n_gy,
    levels,
    interp,
    source_ref,
    geom_ref,
    force_ref,
    live_ref,
    x_factor_ref,
    mat_ref,
    tab_ref,
    perm_ref,
    out_ref,
    u_ref,
    r_ref,
    d_ref,
    weight_ref,
    winv_ref,
    lam_ref,
    inv_ref,
    send_x,
    send_y,
    send_c,
    recv_x,
    recv_y,
    recv_c,
    send_one,
    recv_one,
    send_two,
    recv_two,
    send_sem,
    recv_sem,
    one_send_sem,
    one_recv_sem,
    two_send_sem,
    two_recv_sem,
):
    me_x = lax.axis_index("gx")
    me_y = lax.axis_index("gy")
    left = lax.rem(me_x + n_gx - 1, n_gx)
    right = lax.rem(me_x + 1, n_gx)
    down = lax.rem(me_y + n_gy - 1, n_gy)
    up = lax.rem(me_y + 1, n_gy)
    targets = [
        (left, me_y),
        (right, me_y),
        (me_x, down),
        (me_x, up),
        (left, down),
        (right, up),
        (left, up),
        (right, down),
    ]
    one_targets = [(me_x, flipped(me_y, off)) for off in range(1, n_gy)]
    two_targets = [(flipped(me_x, off), me_y) for off in range(1, n_gx)]
    barrier = pltpu.get_barrier_semaphore()
    everyone = targets + one_targets + two_targets
    for target in everyone:
        pl.semaphore_signal(barrier, inc=1, device_id=target, device_id_type=MESH)

    lane = lax.broadcasted_iota(jnp.int32, (1, 1, 1, LANES), 3)
    lane3 = lax.broadcasted_iota(jnp.int32, (1, 1, LANES), 2)
    lane2 = lax.broadcasted_iota(jnp.int32, (1, LANES), 1)
    ez = lax.rem(lane, EZ)

    def roll(value, shift):
        shift = shift % LANES
        return value if shift == 0 else pltpu.roll(value, shift, value.ndim - 1)

    lam_i = tab_ref[0:8]
    lam_j = tab_ref[8:16]
    w_node = tab_ref[16:24]
    edge = tab_ref[24:32]
    lam_k = tab_ref[32]
    w_c = tab_ref[33]
    zmask = tab_ref[34]
    free = tab_ref[35]
    weight_ref[...] = (w_node[:, None] * w_node[None] * w_c[None, None]).reshape(8, 64, LANES)
    winv_ref[...] = (edge[:, None] * edge[None] * zmask[None, None]).reshape(8, 64, LANES)
    for ex in range(EX):
        hx = geom_ref[0, ex : ex + 1]
        hy = geom_ref[1, ex : ex + 1]
        hz = geom_ref[2, ex : ex + 1]
        ax = hy * hz / (2.0 * hx)
        ay = hx * hz / (2.0 * hy)
        az = hx * hy / (2.0 * hz)
        in_x = lam_i * ax[None]
        in_y = lam_j * ay[None]
        in_z = lam_k * az
        spectrum = (in_x[:, None] + in_y[None] + in_z[None, None]).reshape(8, 64, LANES)
        shift = shift_ratio * (ax + ay + az)
        lam_ref[ex] = spectrum
        inv_ref[ex] = 1.0 / (spectrum + shift[None])
        mass = (hx * hy * hz / 8.0)[None] * weight_ref[...]
        u_ref[ex] = mass * (source_ref[ex] + force_ref[ex : ex + 1][None])

    def free_scaled(value):
        return (value.reshape(8, 8, 8, LANES) * free[None, None]).reshape(8, 64, LANES)

    for ex in range(EX):
        u_ref[ex] = free_scaled(u_ref[ex])

    pl.semaphore_wait(barrier, len(everyone))

    def assemble(slot):
        shared = u_ref[0, 7] + u_ref[1, 0]
        u_ref[0, 7] = shared
        u_ref[1, 0] = shared
        low = u_ref[:, :, 0:8]
        high = u_ref[:, :, 56:64]
        u_ref[:, :, 0:8] = low + jnp.where(lane >= EZ, roll(high, EZ), 0.0)
        u_ref[:, :, 56:64] = high + jnp.where(lane < LANES - EZ, roll(low, -EZ), 0.0)
        for ex in range(EX):
            for a in range(NODES):
                low = u_ref[ex, a, pl.ds(0, 8, stride=8)]
                high = u_ref[ex, a, pl.ds(7, 8, stride=8)]
                z2 = lax.rem(lane2, EZ)
                u_ref[ex, a, pl.ds(0, 8, stride=8)] = low + jnp.where(
                    z2 > 0, roll(high, 1), 0.0
                )
                u_ref[ex, a, pl.ds(7, 8, stride=8)] = high + jnp.where(
                    z2 < EZ - 1, roll(low, -1), 0.0
                )
        send_x[slot, 0] = u_ref[0, 0]
        send_x[slot, 1] = u_ref[1, 7]
        send_c[slot, 0] = u_ref[0, 0, 0:8]
        send_c[slot, 1] = u_ref[1, 7, 56:64]
        send_c[slot, 2] = u_ref[0, 0, 56:64]
        send_c[slot, 3] = u_ref[1, 7, 0:8]
        for ex in range(EX):
            for which, first, ey in ((0, 0, 0), (1, 56, EY - 1)):
                packed = None
                for s in range(4):
                    face = roll(
                        u_ref[ex, 2 * s : 2 * s + 2, first : first + 8], EZ * (s - ey)
                    )
                    packed = (
                        face if packed is None else jnp.where(lane3 >= EZ * s, face, packed)
                    )
                send_y[slot, which, ex] = packed
        pairs = (
            [(send_x.at[slot, i], recv_x.at[slot, i]) for i in range(2)]
            + [(send_y.at[slot, i], recv_y.at[slot, i]) for i in range(2)]
            + [(send_c.at[slot, i], recv_c.at[slot, i]) for i in range(4)]
        )
        copies = []
        for index, (source, landing) in enumerate(pairs):
            copy = pltpu.make_async_remote_copy(
                src_ref=source,
                dst_ref=landing,
                send_sem=send_sem.at[slot, index],
                recv_sem=recv_sem.at[slot, index],
                device_id=targets[index],
                device_id_type=MESH,
            )
            copy.start()
            copies.append(copy)
        for copy in copies:
            copy.wait()
        u_ref[1, 7] += recv_x[slot, 0]
        u_ref[0, 0] += recv_x[slot, 1]
        for ex in range(EX):
            for which, first, ey in ((0, 56, EY - 1), (1, 0, 0)):
                packed = recv_y[slot, which, ex]
                inside = (lane3 >= EZ * ey) & (lane3 < EZ * (ey + 1))
                for s in range(4):
                    u_ref[ex, 2 * s : 2 * s + 2, first : first + 8] += jnp.where(
                        inside, roll(packed, EZ * (ey - s)), 0.0
                    )
        for index, (ex, a, first, to_ey, from_ey) in enumerate(
            (
                (1, 7, 56, EY - 1, 0),
                (0, 0, 0, 0, EY - 1),
                (1, 7, 0, 0, EY - 1),
                (0, 0, 56, EY - 1, 0),
            )
        ):
            inside = (lane2 >= EZ * to_ey) & (lane2 < EZ * (to_ey + 1))
            u_ref[ex, a, first : first + 8] += jnp.where(
                inside, roll(recv_c[slot, index], EZ * (to_ey - from_ey)), 0.0
            )

    def product(which, value):
        high = value.astype(jnp.bfloat16)
        low = (value - high.astype(jnp.float32)).astype(jnp.bfloat16)
        return jnp.dot(
            mat_ref[which],
            jnp.concatenate([high, low, high], axis=0),
            preferred_element_type=jnp.float32,
        )

    def flat(parts):
        return jnp.concatenate([part.reshape(256, LANES) for part in parts], axis=1)

    def element_op(fields, diag_ref):
        even, odd = [], []
        for field in fields:
            low = field[0:4]
            high = jnp.concatenate([field[7:8], field[6:7], field[5:6], field[4:5]], axis=0)
            even.append(low + high)
            odd.append(low - high)
        even = product(0, flat(even)) * flat([diag_ref[ex, 0:4] for ex in range(EX)])
        odd = product(1, flat(odd)) * flat([diag_ref[ex, 4:8] for ex in range(EX)])
        even = product(2, even)
        odd = product(3, odd)
        out = []
        for ex in range(EX):
            at = slice(ex * LANES, (ex + 1) * LANES)
            e = even[:, at].reshape(4, 64, LANES)
            o = odd[:, at].reshape(4, 64, LANES)
            diff = e - o
            out.append(
                jnp.concatenate([e + o, diff[3:4], diff[2:3], diff[1:2], diff[0:1]], axis=0)
            )
        return out

    def stiffness():
        weight = weight_ref[...]
        out = element_op([d_ref[ex] * weight for ex in range(EX)], lam_ref)
        for ex in range(EX):
            u_ref[ex] = free_scaled(out[ex] * weight)

    def smoother():
        out = element_op([r_ref[ex] for ex in range(EX)], inv_ref)
        for ex in range(EX):
            u_ref[ex] = out[ex] * winv_ref[...]

    wide = (levels - 1) * XCOLS
    gy_bits = n_gy.bit_length() - 1
    split = gy_bits * XCOLS

    def exchange(cycle, send_ref, recv_ref, to, send_s, recv_s):
        copies = []
        for index, target in enumerate(to):
            copy = pltpu.make_async_remote_copy(
                src_ref=send_ref,
                dst_ref=recv_ref.at[cycle, index],
                send_sem=send_s.at[index],
                recv_sem=recv_s.at[cycle, index],
                device_id=target,
                device_id_type=MESH,
            )
            copy.start()
            copies.append(copy)
        for copy in copies:
            copy.wait()

    def level_sum(own, recv_ref, cycle, count, first_level_lane):
        which = lax.broadcasted_iota(jnp.int32, own.shape, 1)
        total = own
        start = 1
        bit = 0
        while start < count:
            part = recv_ref[cycle, start - 1]
            for index in range(start + 1, 2 * start):
                part = part + recv_ref[cycle, index - 1]
            total = total + jnp.where(which >= bit * XCOLS + first_level_lane, part, 0.0)
            start *= 2
            bit += 1
        return total

    def coarse(cycle):
        columns = []
        for t in range(2):
            to_t = tab_ref[36 + t]
            rows = []
            for v in range(2):
                for u in range(2):
                    for ex in range(EX):
                        rows.append((v, u, ex))
            columns.append(rows)
        sums = {}
        for ex in range(EX):
            scaled = r_ref[ex] * winv_ref[...]
            for v in range(2):
                by_v = scaled[0] * float(interp[0, v])
                for a in range(1, NODES):
                    by_v = by_v + scaled[a] * float(interp[a, v])
                by_v = by_v.reshape(8, 8, LANES)
                for u in range(2):
                    by_u = by_v[0] * float(interp[0, u])
                    for b in range(1, NODES):
                        by_u = by_u + by_v[b] * float(interp[b, u])
                    for t in range(2):
                        sums[v, u, ex, t] = jnp.sum(
                            by_u * tab_ref[36 + t], axis=0, keepdims=True
                        )
        order = [(v, u, ex) for v in range(2) for u in range(2) for ex in range(EX)]
        split_t = jnp.concatenate(
            [jnp.concatenate([sums[key + (t,)] for t in range(2)], axis=1) for key in order],
            axis=0,
        )
        vector = exact_rows(split_t, perm_ref[0])
        pieces = []
        for level in range(levels):
            rows = slice(level * XCOLS, (level + 1) * XCOLS)
            acc = None
            for q in range(8):
                term = x_factor_ref[rows, q * 256 : (q + 1) * 256] * vector[q : q + 1]
                acc = term if acc is None else acc + term
            pieces.append(acc[:, :LANES] + acc[:, LANES:])
        def row_of(parts):
            block = jnp.concatenate(parts, axis=0)
            missing = LANES - block.shape[0]
            if missing:
                block = jnp.concatenate([block, jnp.zeros((missing, LANES), jnp.float32)], axis=0)
            return jnp.sum(block.T, axis=0, keepdims=True)
        own = row_of(pieces[0:1])
        upper = jnp.concatenate(
            [row_of(pieces[i : i + 4]) for i in range(1, levels, 4)], axis=1
        )[:, :wide]
        send_one[...] = upper
        exchange(cycle, send_one, recv_one, one_targets, one_send_sem, one_recv_sem)
        upper = level_sum(upper, recv_one, cycle, n_gy, 0)
        send_two[...] = upper[:, split:]
        exchange(cycle, send_two, recv_two, two_targets, two_send_sem, two_recv_sem)
        top = level_sum(upper[:, split:], recv_two, cycle, n_gx, 0)
        upper = jnp.concatenate([upper[:, :split], top], axis=1)
        own = own * live_ref[:, 0:LANES]
        upper = upper * live_ref[:, LANES : LANES + wide]
        tail = (-wide) % LANES
        if tail:
            upper = jnp.concatenate([upper, jnp.zeros((1, tail), jnp.float32)], axis=1)
        cols = [jnp.broadcast_to(own, (LANES, LANES)).T[:XCOLS]]
        for first in range(0, wide, LANES):
            part = jnp.broadcast_to(upper[:, first : first + LANES], (LANES, LANES)).T
            cols += [part[k * XCOLS : (k + 1) * XCOLS] for k in range(LANES // XCOLS)]
        back = []
        for q in range(8):
            acc = None
            for level in range(levels):
                block = x_factor_ref[
                    level * XCOLS : (level + 1) * XCOLS, q * 256 : (q + 1) * 256
                ]
                col = cols[level]
                term = block * jnp.concatenate([col, col], axis=1)
                acc = term if acc is None else acc + term
            back.append(jnp.sum(acc, axis=0, keepdims=True))
        split_t = exact_rows(jnp.concatenate(back, axis=0), perm_ref[1])
        for ex in range(EX):
            by_v = []
            for v in range(2):
                by_u = []
                for u in range(2):
                    q = (v * 2 + u) * EX + ex
                    by_u.append(
                        split_t[q : q + 1, :LANES] * tab_ref[36]
                        + split_t[q : q + 1, LANES:] * tab_ref[37]
                    )
                by_v.append(
                    jnp.concatenate(
                        [
                            by_u[0] * float(interp[b, 0]) + by_u[1] * float(interp[b, 1])
                            for b in range(NODES)
                        ],
                        axis=0,
                    )
                )
            for a in range(NODES):
                u_ref[ex, a] = winv_ref[a] * (
                    by_v[0] * float(interp[a, 0]) + by_v[1] * float(interp[a, 1])
                )

    center = 0.5 * (bound_high + bound_low)
    radius = 0.5 * (bound_high - bound_low)
    ratio = center / radius
    rho_old = 1.0 / ratio
    rho_new = 1.0 / (2.0 * ratio - rho_old)

    assemble(1)
    r_ref[...] = u_ref[...]
    d_ref[...] = jnp.zeros_like(d_ref)
    out_ref[...] = jnp.zeros_like(out_ref)

    def step(index, carry):
        phase = lax.rem(index, SMOOTH)
        cycle = lax.div(index, SMOOTH)
        is_coarse = phase == 2
        second = (phase == 1) | (phase == 4)
        keep = jnp.where(second, rho_new * rho_old, 0.0)
        take = jnp.where(second, 2.0 * rho_new / radius, 1.0 / center)
        take = jnp.where(is_coarse, 1.0, take)

        @pl.when(is_coarse)
        def _():
            coarse(cycle)

        @pl.when(jnp.logical_not(is_coarse))
        def _():
            smoother()

        assemble(0)
        for ex in range(EX):
            direction = keep * d_ref[ex] + take * u_ref[ex]
            d_ref[ex] = direction
            out_ref[ex] += direction

        @pl.when(index < SMOOTH * CYCLES - 1)
        def _():
            stiffness()
            assemble(1)
            for ex in range(EX):
                r_ref[ex] -= u_ref[ex]

        return carry

    lax.fori_loop(0, SMOOTH * CYCLES, step, 0)


def per_device(source, geometry, disc_mask, thrust, xxt_factor, col_count):
    n_gx = lax.axis_size("gx")
    n_gy = lax.axis_size("gy")
    levels = xxt_factor.shape[0]
    wide = (levels - 1) * XCOLS
    split = (n_gy.bit_length() - 1) * XCOLS
    matrices, table, perms, interp = constant_tables()
    nodes = source.reshape(NODES, NODES, EX, EY, EZ, NODES)
    nodes = nodes.transpose(2, 0, 1, 5, 3, 4).reshape(EX, NODES, 64, LANES)
    geom = geometry.reshape(3, EX, LANES)
    force = (disc_mask.astype(jnp.float32) * thrust).reshape(EX, LANES)
    live = (jnp.arange(XCOLS)[None, :] < col_count).astype(jnp.float32)
    live = jnp.concatenate(
        [
            live[0:1],
            jnp.zeros((1, LANES - XCOLS), jnp.float32),
            live[1:].reshape(1, wide),
        ],
        axis=1,
    )
    field = (EX, NODES, 64, LANES)
    f32 = jnp.float32
    out = pl.pallas_call(
        functools.partial(kernel, n_gx, n_gy, levels, interp),
        out_shape=jax.ShapeDtypeStruct(field, f32),
        in_specs=[pl.BlockSpec(memory_space=pltpu.VMEM)] * 8,
        out_specs=pl.BlockSpec(memory_space=pltpu.VMEM),
        scratch_shapes=[
            pltpu.VMEM(field, f32),
            pltpu.VMEM(field, f32),
            pltpu.VMEM(field, f32),
            pltpu.VMEM(field[1:], f32),
            pltpu.VMEM(field[1:], f32),
            pltpu.VMEM(field, f32),
            pltpu.VMEM(field, f32),
            pltpu.VMEM((2, 2, 64, LANES), f32),
            pltpu.VMEM((2, 2, EX, 2, 8, LANES), f32),
            pltpu.VMEM((2, 4, 8, LANES), f32),
            pltpu.VMEM((2, 2, 64, LANES), f32),
            pltpu.VMEM((2, 2, EX, 2, 8, LANES), f32),
            pltpu.VMEM((2, 4, 8, LANES), f32),
            pltpu.VMEM((1, wide), f32),
            pltpu.VMEM((CYCLES, n_gy - 1, 1, wide), f32),
            pltpu.VMEM((1, wide - split), f32),
            pltpu.VMEM((CYCLES, n_gx - 1, 1, wide - split), f32),
            pltpu.SemaphoreType.DMA((2, 8)),
            pltpu.SemaphoreType.DMA((2, 8)),
            pltpu.SemaphoreType.DMA((n_gy - 1,)),
            pltpu.SemaphoreType.DMA((CYCLES, n_gy - 1)),
            pltpu.SemaphoreType.DMA((n_gx - 1,)),
            pltpu.SemaphoreType.DMA((CYCLES, n_gx - 1)),
        ],
        compiler_params=pltpu.CompilerParams(
            collective_id=0, has_side_effects=True, vmem_limit_bytes=48 * 1024 * 1024
        ),
    )(
        nodes,
        geom,
        force,
        live,
        xxt_factor.reshape(levels * XCOLS, xxt_factor.shape[2]),
        jnp.asarray(matrices),
        jnp.asarray(table),
        jnp.asarray(perms),
    )
    out = out.reshape(EX, NODES, NODES, NODES, EY, EZ).transpose(1, 2, 0, 4, 5, 3)
    return out.reshape(source.shape)


def solution(mesh):
    return jax.shard_map(
        per_device,
        mesh=mesh,
        in_specs=(
            P(None, None, "gx", "gy", None),
            P(None, "gx", "gy", None),
            P("gx", "gy", None),
            P("gx", "gy", None),
            P(None, None, ("gx", "gy")),
            P(None, ("gx", "gy")),
        ),
        out_specs=P(None, None, "gx", "gy", None),
        check_vma=False,
    )
```

```python
import functools
import math

import jax
import jax.numpy as jnp
import ml_dtypes
import numpy as np
from jax import lax
from jax.experimental import pallas as pl
from jax.experimental.pallas import tpu as pltpu
from jax.sharding import PartitionSpec as P

NODES = 8
CYCLES = 2
EX = 2
EY = 4
EZ = 32
LANES = EY * EZ
XCOLS = 32
SMOOTH = 5

bound_low = 0.3
bound_high = 3.0
shift_ratio = 0.25
MESH = pl.DeviceIdType.MESH


def legendre_table(points, poly_order):
    table = [points * 0.0 + 1.0, points]
    for degree in range(2, poly_order + 1):
        table.append(
            ((2.0 * degree - 1.0) * points * table[-1] - (degree - 1.0) * table[-2]) / degree
        )
    return table


def jacobi_eigen(matrix):
    size_n = matrix.shape[0]
    current = matrix.copy()
    vectors = np.eye(size_n)
    for sweep_index in range(30):
        for first in range(size_n - 1):
            for second in range(first + 1, size_n):
                angle = 0.5 * math.atan2(
                    2.0 * float(current[first, second]),
                    float(current[second, second] - current[first, first]),
                )
                rotation = np.eye(size_n)
                rotation[first, first] = math.cos(angle)
                rotation[second, second] = math.cos(angle)
                rotation[first, second] = math.sin(angle)
                rotation[second, first] = -math.sin(angle)
                current = rotation.T @ current @ rotation
                vectors = vectors @ rotation
    values = np.array([current[index, index] for index in range(size_n)])
    order = np.argsort(values)
    return (values[order], vectors[:, order])


def gll_tables(node_count):
    poly_order = node_count - 1
    points = np.cos(np.pi * np.arange(node_count) / poly_order)
    for newton_index in range(200):
        table = legendre_table(points, poly_order)
        points = points - (points * table[poly_order] - table[poly_order - 1]) / (
            node_count * table[poly_order]
        )
    points = points[::-1].copy()
    legendre = legendre_table(points, poly_order)[poly_order]
    weights = 2.0 / (poly_order * (poly_order + 1) * legendre**2)
    identity = np.eye(node_count)
    gap_matrix = points[:, None] - points[None, :] + identity
    off_diagonal = legendre[:, None] / (legendre[None, :] * gap_matrix) * (1.0 - identity)
    end_value = poly_order * (poly_order + 1) / 4.0
    end_terms = np.concatenate([[-end_value], np.zeros(node_count - 2), [end_value]])
    derivative = off_diagonal + identity * end_terms[None, :]
    stiffness = derivative.T @ (weights[:, None] * derivative)
    root_inverse = 1.0 / np.sqrt(weights)
    symmetric = root_inverse[:, None] * stiffness * root_inverse[None, :]
    symmetric = 0.5 * (symmetric + symmetric.T)
    eigen_values, eigen_vectors = jacobi_eigen(symmetric)
    eigen_modes = root_inverse[:, None] * eigen_vectors
    vertex_interp = np.stack([(1.0 - points) / 2.0, (1.0 + points) / 2.0], axis=1)
    return weights, stiffness, eigen_modes, eigen_values, vertex_interp


def mode_order(modes):
    even = [i for i in range(NODES) if modes[0, i] * modes[NODES - 1, i] > 0.0]
    odd = [i for i in range(NODES) if i not in even]
    return even, odd


def split_pair(matrix):
    exact = matrix.astype(np.float32)
    high = exact.astype(ml_dtypes.bfloat16)
    low = (exact - high.astype(np.float32)).astype(ml_dtypes.bfloat16)
    return np.concatenate([high, high, low], axis=1)


def constant_tables():
    weights, stiffness, modes, values, interp = gll_tables(NODES)
    even, odd = mode_order(modes)
    half = NODES // 2
    mats = []
    for chosen in (even, odd):
        inverse = np.kron(modes[:half][:, chosen], np.kron(modes, modes))
        mats.append((split_pair(inverse.T), split_pair(inverse)))
    matrices = np.stack([mats[0][0], mats[1][0], mats[0][1], mats[1][1]])
    plane = np.kron(modes, modes)
    plane_matrices = np.stack([split_pair(plane.T), split_pair(plane)])
    full = np.ones((NODES, LANES))
    edge = np.ones(NODES)
    edge[0] = edge[-1] = 0.5
    ez = np.arange(LANES)[None, :] % EZ
    node = np.arange(NODES)[:, None]
    z_shared = 1.0 + ((node == 0) & (ez > 0)) + ((node == NODES - 1) & (ez < EZ - 1))
    free = 1.0 - ((node == NODES - 1) & (ez == EZ - 1))
    rows = [values[i] * full for i in even + odd]
    rows += [value * full for value in values]
    rows += [weight * full for weight in weights]
    rows += [value * full for value in edge]
    rows += [values[:, None] * full, weights[:, None] * full, free / z_shared, free * full]
    rows += [interp[:, 0:1] * full, interp[:, 1:2] * full]
    rows += [stiffness[:, c : c + 1] * full for c in range(NODES)]
    table = np.stack(rows).astype(np.float32)
    perm = np.zeros((2 * LANES, 2 * LANES), np.float32)
    for t in range(2):
        for element in range(LANES):
            perm[t * LANES + element, 2 * element + t] = 1.0
    order = np.zeros((EZ * NODES, EZ * NODES), np.float32)
    for c in range(NODES):
        for element in range(EZ):
            order[element * NODES + c, c * EZ + element] = 1.0
    perms = np.stack([perm, perm.T, order, order.T]).astype(ml_dtypes.bfloat16)
    return (
        matrices,
        plane_matrices,
        table,
        perms,
        interp.astype(np.float32),
        stiffness.astype(np.float32),
        weights.astype(np.float32),
    )


def flipped(index, bits):
    out = index
    bit = 1
    while bit <= bits:
        if bits & bit:
            out = out + bit - 2 * bit * lax.rem(lax.div(index, bit), 2)
        bit *= 2
    return out


def exact_rows(value, perm):
    first = value.astype(jnp.bfloat16)
    rest = value - first.astype(jnp.float32)
    second = rest.astype(jnp.bfloat16)
    third = (rest - second.astype(jnp.float32)).astype(jnp.bfloat16)
    parts = [
        jnp.dot(part, perm, preferred_element_type=jnp.float32)
        for part in (first, second, third)
    ]
    return parts[0] + parts[1] + parts[2]


def kernel(
    n_gx,
    n_gy,
    levels,
    interp,
    stiff,
    weights,
    source_ref,
    geom_ref,
    force_ref,
    live_ref,
    x_hbm,
    mat_hbm,
    plane_ref,
    tab_ref,
    perm_ref,
    out_ref,
    u_ref,
    r_ref,
    d_ref,
    x_ref,
    weight_ref,
    winv_ref,
    lam_ref,
    inv_ref,
    face_lam,
    face_normal,
    line_tab,
    x_factor_ref,
    mat_ref,
    send_x,
    send_y,
    send_c,
    recv_x,
    recv_y,
    recv_c,
    recv_g,
    send_one,
    recv_one,
    send_two,
    recv_two,
    send_sem,
    recv_sem,
    g_send_sem,
    g_recv_sem,
    one_send_sem,
    one_recv_sem,
    two_send_sem,
    two_recv_sem,
    load_sem,
):
    loads = [
        pltpu.make_async_copy(mat_hbm, mat_ref, load_sem.at[0]),
        pltpu.make_async_copy(x_hbm, x_factor_ref, load_sem.at[1]),
    ]
    for load in loads:
        load.start()
    me_x = lax.axis_index("gx")
    me_y = lax.axis_index("gy")
    left = lax.rem(me_x + n_gx - 1, n_gx)
    right = lax.rem(me_x + 1, n_gx)
    down = lax.rem(me_y + n_gy - 1, n_gy)
    up = lax.rem(me_y + 1, n_gy)
    targets = [
        (left, me_y),
        (right, me_y),
        (me_x, down),
        (me_x, up),
        (left, down),
        (right, up),
        (left, up),
        (right, down),
    ]
    FROM_RIGHT, FROM_LEFT, FROM_UP, FROM_DOWN = 0, 1, 2, 3
    FROM_RIGHT_UP, FROM_LEFT_DOWN, FROM_RIGHT_DOWN, FROM_LEFT_UP = 4, 5, 6, 7
    one_targets = [(me_x, flipped(me_y, off)) for off in range(1, n_gy)]
    two_targets = [(flipped(me_x, off), me_y) for off in range(1, n_gx)]
    barrier = pltpu.get_barrier_semaphore()
    everyone = targets + one_targets + two_targets
    for target in everyone:
        pl.semaphore_signal(barrier, inc=1, device_id=target, device_id_type=MESH)

    lane = lax.broadcasted_iota(jnp.int32, (1, 1, 1, LANES), 3)
    lane3 = lax.broadcasted_iota(jnp.int32, (1, 1, LANES), 2)
    lane2 = lax.broadcasted_iota(jnp.int32, (1, LANES), 1)
    z2 = lax.rem(lane2, EZ)

    def roll(value, shift):
        shift = shift % LANES
        return value if shift == 0 else pltpu.roll(value, shift, value.ndim - 1)

    lam_i = tab_ref[0:8]
    lam_j = tab_ref[8:16]
    w_node = tab_ref[16:24]
    edge = tab_ref[24:32]
    lam_k = tab_ref[32]
    w_c = tab_ref[33]
    zmask = tab_ref[34]
    free = tab_ref[35]
    w_end = float(weights[0])
    k_end = float(stiff[0, 0])
    weight_ref[...] = (w_node[:, None] * w_node[None] * w_c[None, None]).reshape(8, 64, LANES)
    winv_ref[...] = (edge[:, None] * edge[None] * zmask[None, None]).reshape(8, 64, LANES)

    def metrics(hx, hy, hz):
        return hy * hz / (2.0 * hx), hx * hz / (2.0 * hy), hx * hy / (2.0 * hz)

    for half in range(2):
        at = slice(half * LANES, (half + 1) * LANES)
        d_ref[half] = source_ref[:, at].reshape(8, 64, LANES)
    by_node = exact_rows(
        jnp.concatenate(
            [
                jnp.concatenate(
                    [d_ref[half, a, pl.ds(k, 8, stride=8)] for half in range(2)], axis=1
                )
                for k in range(EX * EY)
                for a in range(NODES)
            ],
            axis=0,
        ),
        perm_ref[2],
    )
    for ex in range(EX):
        for c in range(NODES):
            at = slice(c // 4 * LANES, (c // 4 + 1) * LANES)
            joined = None
            for ey in range(EY):
                first = (ex * EY + ey) * 64
                part = roll(by_node[first : first + 64, at], EZ * (ey - c % 4))
                joined = part if ey == 0 else jnp.where(lane2 >= EZ * ey, part, joined)
            for a in range(NODES):
                u_ref[ex, a, pl.ds(c, 8, stride=8)] = joined[8 * a : 8 * a + 8]

    for ex in range(EX):
        hx = geom_ref[ex : ex + 1]
        hy = geom_ref[2 + ex : 3 + ex]
        hz = geom_ref[4 + ex : 5 + ex]
        ax, ay, az = metrics(hx, hy, hz)
        in_x = lam_i * ax[None]
        in_y = lam_j * ay[None]
        in_z = lam_k * az
        spectrum = (in_x[:, None] + in_y[None] + in_z[None, None]).reshape(8, 64, LANES)
        shift = shift_ratio * (ax + ay + az)
        lam_ref[ex] = spectrum
        inv_ref[ex] = 1.0 / (spectrum + shift[None])
        mass = (hx * hy * hz / 8.0)[None] * weight_ref[...]
        u_ref[ex] = mass * (u_ref[ex] + force_ref[ex : ex + 1][None])

    def free_scaled(value):
        return (value.reshape(8, 8, 8, LANES) * free[None, None]).reshape(8, 64, LANES)

    for ex in range(EX):
        u_ref[ex] = free_scaled(u_ref[ex])

    pl.semaphore_wait(barrier, len(everyone))

    geom_copies = []
    for index, target in enumerate(targets):
        copy = pltpu.make_async_remote_copy(
            src_ref=geom_ref,
            dst_ref=recv_g.at[index],
            send_sem=g_send_sem.at[index],
            recv_sem=g_recv_sem.at[index],
            device_id=target,
            device_id_type=MESH,
        )
        copy.start()
        geom_copies.append(copy)

    def own_pairs():
        shared = u_ref[0, 7] + u_ref[1, 0]
        u_ref[0, 7] = shared
        u_ref[1, 0] = shared
        low = u_ref[:, :, 0:8]
        high = u_ref[:, :, 56:64]
        u_ref[:, :, 0:8] = low + jnp.where(lane >= EZ, roll(high, EZ), 0.0)
        u_ref[:, :, 56:64] = high + jnp.where(lane < LANES - EZ, roll(low, -EZ), 0.0)
        for ex in range(EX):
            for a in range(NODES):
                low = u_ref[ex, a, pl.ds(0, 8, stride=8)]
                high = u_ref[ex, a, pl.ds(7, 8, stride=8)]
                u_ref[ex, a, pl.ds(0, 8, stride=8)] = low + jnp.where(
                    z2 > 0, roll(high, 1), 0.0
                )
                u_ref[ex, a, pl.ds(7, 8, stride=8)] = high + jnp.where(
                    z2 < EZ - 1, roll(low, -1), 0.0
                )

    def packed_y(down_faces, up_faces):
        return jnp.where(
            lane3 < EZ,
            down_faces[0],
            jnp.where(
                lane3 < 2 * EZ,
                roll(down_faces[1], EZ),
                jnp.where(lane3 < 3 * EZ, roll(up_faces[0], -EZ), up_faces[1]),
            ),
        )

    def y_faces():
        return packed_y(
            [u_ref[ex, :, 0:8] for ex in range(EX)], [u_ref[ex, :, 56:64] for ex in range(EX)]
        )

    def weighted(parts, row):
        total = None
        for index, part in parts:
            term = part * float(stiff[row, index])
            total = term if total is None else total + term
        return total

    def exchange_faces(slot, planes):
        send_x[slot, 0, 0] = u_ref[0, 0]
        send_x[slot, 1, 0] = u_ref[1, 7]
        send_y[slot, 0] = y_faces()
        send_c[slot, 0, 0] = u_ref[0, 0, 0:8]
        send_c[slot, 1, 0] = u_ref[1, 7, 56:64]
        send_c[slot, 2, 0] = u_ref[0, 0, 56:64]
        send_c[slot, 3, 0] = u_ref[1, 7, 0:8]
        if planes > 1:
            low = weighted([(a, u_ref[0, a]) for a in range(1, NODES)], 0)
            high = weighted([(a, u_ref[1, a]) for a in range(NODES - 1)], 7)
            send_x[slot, 0, 1] = low
            send_x[slot, 1, 1] = high
            send_c[slot, 0, 1] = low[0:8]
            send_c[slot, 1, 1] = high[56:64]
            send_c[slot, 2, 1] = low[56:64]
            send_c[slot, 3, 1] = high[0:8]
            down_normal, up_normal = [], []
            for ex in range(EX):
                rows = [u_ref[ex, :, 8 * b : 8 * b + 8] for b in range(NODES)]
                down_normal.append(weighted([(b, rows[b]) for b in range(1, NODES)], 0))
                up_normal.append(weighted([(b, rows[b]) for b in range(NODES - 1)], 7))
            normal = packed_y(down_normal, up_normal)
            send_y[slot, 1] = normal
            send_c[slot, 0, 2] = normal[0]
            send_c[slot, 1, 2] = normal[7]
            send_c[slot, 2, 2] = normal[0]
            send_c[slot, 3, 2] = normal[7]
        lines = 3 if planes > 1 else 1
        pairs = (
            [(send_x.at[slot, i, pl.ds(0, planes)], recv_x.at[slot, i, pl.ds(0, planes)]) for i in range(2)]
            + [(send_y.at[slot, pl.ds(0, planes)], recv_y.at[slot, i, pl.ds(0, planes)]) for i in range(2)]
            + [(send_c.at[slot, i, pl.ds(0, lines)], recv_c.at[slot, i, pl.ds(0, lines)]) for i in range(4)]
        )
        copies = []
        for index, (source, landing) in enumerate(pairs):
            copy = pltpu.make_async_remote_copy(
                src_ref=source,
                dst_ref=landing,
                send_sem=send_sem.at[slot, index],
                recv_sem=recv_sem.at[slot, index],
                device_id=targets[index],
                device_id_type=MESH,
            )
            copy.start()
            copies.append(copy)
        for copy in copies:
            copy.wait()
        u_ref[1, 7] += recv_x[slot, FROM_RIGHT, 0]
        u_ref[0, 0] += recv_x[slot, FROM_LEFT, 0]
        add_y(arrived_y(slot, 0))
        for index, (ex, a, first, to_ey, from_ey) in enumerate(
            (
                (1, 7, 56, EY - 1, 0),
                (0, 0, 0, 0, EY - 1),
                (1, 7, 0, 0, EY - 1),
                (0, 0, 56, EY - 1, 0),
            )
        ):
            inside = (lane2 >= EZ * to_ey) & (lane2 < EZ * (to_ey + 1))
            u_ref[ex, a, first : first + 8] += jnp.where(
                inside, roll(recv_c[slot, index, 0], EZ * (to_ey - from_ey)), 0.0
            )

    def arrived_y(slot, plane):
        from_up = recv_y[slot, FROM_UP - 2, plane]
        from_down = recv_y[slot, FROM_DOWN - 2, plane]
        return roll(jnp.where(lane3 >= 2 * EZ, from_down, from_up), 2 * EZ)

    def add_y(plane):
        for ex in range(EX):
            u_ref[ex, :, 0:8] += jnp.where(lane3 < EZ, roll(plane, -EZ * ex), 0.0)
            u_ref[ex, :, 56:64] += jnp.where(
                lane3 >= 3 * EZ, roll(plane, EZ * (1 - ex)), 0.0
            )

    def in_slot(value, slot):
        return jnp.where((lane2 >= EZ * slot) & (lane2 < EZ * (slot + 1)), value, 0.0)

    def outer_terms(slot):
        face = jnp.concatenate(
            [u_ref[0, 0], u_ref[1, 7], y_faces().reshape(64, LANES)], axis=1
        )
        from_left_down = recv_c[slot, FROM_LEFT_DOWN - 4]
        from_left_up = recv_c[slot, FROM_LEFT_UP - 4]
        from_right_down = recv_c[slot, FROM_RIGHT_DOWN - 4]
        from_right_up = recv_c[slot, FROM_RIGHT_UP - 4]
        sides = []
        for plane, low, high in (
            (recv_x[slot, FROM_LEFT, 1], from_left_down, from_left_up),
            (recv_x[slot, FROM_RIGHT, 1], from_right_down, from_right_up),
        ):
            sides.append(
                jnp.concatenate(
                    [
                        plane[0:8] + in_slot(roll(low[1], EZ), 0),
                        plane[8:56],
                        plane[56:64] + in_slot(roll(high[1], -EZ), 3),
                    ],
                    axis=0,
                )
            )
        normal_y = arrived_y(slot, 1)
        first = (
            normal_y[0]
            + in_slot(roll(from_left_down[2], EZ), 0)
            + in_slot(roll(from_left_up[2], EZ), 2)
        )
        last = (
            normal_y[7]
            + in_slot(roll(from_right_down[2], -EZ), 1)
            + in_slot(roll(from_right_up[2], -EZ), 3)
        )
        normal_y = jnp.concatenate([first[None], normal_y[1:7], last[None]], axis=0)
        normal = jnp.concatenate([sides[0], sides[1], normal_y.reshape(64, LANES)], axis=1)
        weight = weight_ref[0] * (1.0 / w_end)
        weight = jnp.concatenate([weight] * 3, axis=1)
        spread = small_product(1, face_lam[...] * small_product(0, weight * face))
        result = face_normal[...] * (normal + k_end * face) + w_end * weight * spread
        lines = []
        for side in range(2):
            plane = face[:, side * LANES : (side + 1) * LANES]
            value = jnp.where(lane2 < 2 * EZ, plane[0:8], plane[56:64])
            along_x = jnp.where(lane2 < 2 * EZ, sides[side][0:8], sides[side][56:64])
            edge_y = last if side else first
            along_y = jnp.where(
                lane2 < 2 * EZ,
                roll(edge_y, -EZ) if side else edge_y,
                edge_y if side else roll(edge_y, EZ),
            )
            along_z = None
            for c in range(NODES):
                term = tab_ref[38 + c] * value[c : c + 1]
                along_z = term if along_z is None else along_z + term
            lines.append(
                line_tab[side, 0] * (along_x + k_end * value)
                + line_tab[side, 1] * (along_y + k_end * value)
                + line_tab[side, 2] * along_z
            )
        return result, lines

    def add_outer(result, lines):
        for side, (ex, a) in enumerate(((0, 0), (1, 7))):
            u_ref[ex, a] += result[:, side * LANES : (side + 1) * LANES]
            u_ref[ex, a, 0:8] += in_slot(lines[side], 0)
            u_ref[ex, a, 56:64] += in_slot(lines[side], 3)
        add_y(result[:, 2 * LANES :].reshape(8, 8, LANES))

    def small_product(which, value):
        high = value.astype(jnp.bfloat16)
        low = (value - high.astype(jnp.float32)).astype(jnp.bfloat16)
        return jnp.dot(
            plane_ref[which],
            jnp.concatenate([high, low, high], axis=0),
            preferred_element_type=jnp.float32,
        )

    def product(which, value):
        high = value.astype(jnp.bfloat16)
        low = (value - high.astype(jnp.float32)).astype(jnp.bfloat16)
        return jnp.dot(
            mat_ref[which],
            jnp.concatenate([high, low, high], axis=0),
            preferred_element_type=jnp.float32,
        )

    def flat(parts):
        return jnp.concatenate([part.reshape(256, LANES) for part in parts], axis=1)

    def element_op(fields, diag_ref):
        even, odd = [], []
        for field in fields:
            low = field[0:4]
            high = jnp.concatenate([field[7:8], field[6:7], field[5:6], field[4:5]], axis=0)
            even.append(low + high)
            odd.append(low - high)
        even = product(0, flat(even)) * flat([diag_ref[ex, 0:4] for ex in range(EX)])
        odd = product(1, flat(odd)) * flat([diag_ref[ex, 4:8] for ex in range(EX)])
        even = product(2, even)
        odd = product(3, odd)
        out = []
        for ex in range(EX):
            at = slice(ex * LANES, (ex + 1) * LANES)
            e = even[:, at].reshape(4, 64, LANES)
            o = odd[:, at].reshape(4, 64, LANES)
            diff = e - o
            out.append(
                jnp.concatenate([e + o, diff[3:4], diff[2:3], diff[1:2], diff[0:1]], axis=0)
            )
        return out

    def stiffness():
        weight = weight_ref[...]
        out = element_op([u_ref[ex] * weight for ex in range(EX)], lam_ref)
        for ex in range(EX):
            u_ref[ex] = out[ex] * weight

    def smoother(keep, take):
        out = element_op([r_ref[ex] for ex in range(EX)], inv_ref)
        for ex in range(EX):
            u_ref[ex] = (take * out[ex] + keep * d_ref[ex]) * winv_ref[...]

    wide = (levels - 1) * XCOLS
    gy_bits = n_gy.bit_length() - 1
    split = gy_bits * XCOLS

    def exchange(cycle, send_ref, recv_ref, to, send_s, recv_s):
        copies = []
        for index, target in enumerate(to):
            copy = pltpu.make_async_remote_copy(
                src_ref=send_ref,
                dst_ref=recv_ref.at[cycle, index],
                send_sem=send_s.at[index],
                recv_sem=recv_s.at[cycle, index],
                device_id=target,
                device_id_type=MESH,
            )
            copy.start()
            copies.append(copy)
        for copy in copies:
            copy.wait()

    def level_sum(own, recv_ref, cycle, count, first_level_lane):
        which = lax.broadcasted_iota(jnp.int32, own.shape, 1)
        total = own
        start = 1
        bit = 0
        while start < count:
            part = recv_ref[cycle, start - 1]
            for index in range(start + 1, 2 * start):
                part = part + recv_ref[cycle, index - 1]
            total = total + jnp.where(which >= bit * XCOLS + first_level_lane, part, 0.0)
            start *= 2
            bit += 1
        return total

    def coarse(cycle):
        sums = {}
        for ex in range(EX):
            scaled = r_ref[ex] * winv_ref[...]
            for v in range(2):
                by_v = scaled[0] * float(interp[0, v])
                for a in range(1, NODES):
                    by_v = by_v + scaled[a] * float(interp[a, v])
                by_v = by_v.reshape(8, 8, LANES)
                for u in range(2):
                    by_u = by_v[0] * float(interp[0, u])
                    for b in range(1, NODES):
                        by_u = by_u + by_v[b] * float(interp[b, u])
                    for t in range(2):
                        sums[v, u, ex, t] = jnp.sum(
                            by_u * tab_ref[36 + t], axis=0, keepdims=True
                        )
        order = [(v, u, ex) for v in range(2) for u in range(2) for ex in range(EX)]
        split_t = jnp.concatenate(
            [jnp.concatenate([sums[key + (t,)] for t in range(2)], axis=1) for key in order],
            axis=0,
        )
        vector = exact_rows(split_t, perm_ref[0])
        pieces = []
        for level in range(levels):
            rows = slice(level * XCOLS, (level + 1) * XCOLS)
            acc = None
            for q in range(8):
                term = x_factor_ref[rows, q * 256 : (q + 1) * 256] * vector[q : q + 1]
                acc = term if acc is None else acc + term
            pieces.append(acc[:, :LANES] + acc[:, LANES:])
        def row_of(parts):
            block = jnp.concatenate(parts, axis=0)
            missing = LANES - block.shape[0]
            if missing:
                block = jnp.concatenate([block, jnp.zeros((missing, LANES), jnp.float32)], axis=0)
            return jnp.sum(block.T, axis=0, keepdims=True)
        own = row_of(pieces[0:1])
        upper = jnp.concatenate(
            [row_of(pieces[i : i + 4]) for i in range(1, levels, 4)], axis=1
        )[:, :wide]
        send_one[...] = upper
        exchange(cycle, send_one, recv_one, one_targets, one_send_sem, one_recv_sem)
        upper = level_sum(upper, recv_one, cycle, n_gy, 0)
        send_two[...] = upper[:, split:]
        exchange(cycle, send_two, recv_two, two_targets, two_send_sem, two_recv_sem)
        top = level_sum(upper[:, split:], recv_two, cycle, n_gx, 0)
        upper = jnp.concatenate([upper[:, :split], top], axis=1)
        own = own * live_ref[:, 0:LANES]
        upper = upper * live_ref[:, LANES : LANES + wide]
        tail = (-wide) % LANES
        if tail:
            upper = jnp.concatenate([upper, jnp.zeros((1, tail), jnp.float32)], axis=1)
        cols = [jnp.broadcast_to(own, (LANES, LANES)).T[:XCOLS]]
        for first in range(0, wide, LANES):
            part = jnp.broadcast_to(upper[:, first : first + LANES], (LANES, LANES)).T
            cols += [part[k * XCOLS : (k + 1) * XCOLS] for k in range(LANES // XCOLS)]
        back = []
        for q in range(8):
            acc = None
            for level in range(levels):
                block = x_factor_ref[
                    level * XCOLS : (level + 1) * XCOLS, q * 256 : (q + 1) * 256
                ]
                col = cols[level]
                term = block * jnp.concatenate([col, col], axis=1)
                acc = term if acc is None else acc + term
            back.append(jnp.sum(acc, axis=0, keepdims=True))
        split_t = exact_rows(jnp.concatenate(back, axis=0), perm_ref[1])
        for ex in range(EX):
            by_v = []
            for v in range(2):
                by_u = []
                for u in range(2):
                    q = (v * 2 + u) * EX + ex
                    by_u.append(
                        split_t[q : q + 1, :LANES] * tab_ref[36]
                        + split_t[q : q + 1, LANES:] * tab_ref[37]
                    )
                by_v.append(
                    jnp.concatenate(
                        [
                            by_u[0] * float(interp[b, 0]) + by_u[1] * float(interp[b, 1])
                            for b in range(NODES)
                        ],
                        axis=0,
                    )
                )
            for a in range(NODES):
                u_ref[ex, a] = winv_ref[a] * (
                    by_v[0] * float(interp[a, 0]) + by_v[1] * float(interp[a, 1])
                )

    center = 0.5 * (bound_high + bound_low)
    radius = 0.5 * (bound_high - bound_low)
    ratio = center / radius
    rho_old = 1.0 / ratio
    rho_new = 1.0 / (2.0 * ratio - rho_old)

    own_pairs()
    exchange_faces(1, 1)
    r_ref[...] = u_ref[...]
    d_ref[...] = jnp.zeros_like(d_ref)
    x_ref[...] = jnp.zeros_like(x_ref)

    for copy in geom_copies:
        copy.wait()
    slots = lambda values: jnp.where(
        lane2 < EZ,
        values[0],
        jnp.where(lane2 < 2 * EZ, values[1], jnp.where(lane2 < 3 * EZ, values[2], values[3])),
    )

    def ghost(source, dim, ex):
        return recv_g[source, 2 * dim + ex : 2 * dim + ex + 1]

    outer = []
    for dim in range(3):
        y_side = slots(
            [
                roll(ghost(FROM_DOWN, dim, 0), EZ),
                roll(ghost(FROM_DOWN, dim, 1), 2 * EZ),
                roll(ghost(FROM_UP, dim, 0), 2 * EZ),
                roll(ghost(FROM_UP, dim, 1), 3 * EZ),
            ]
        )
        outer.append([ghost(FROM_LEFT, dim, 1), ghost(FROM_RIGHT, dim, 0), y_side])
    for part in range(3):
        ax, ay, az = metrics(*[outer[dim][part] for dim in range(3)])
        at = slice(part * LANES, (part + 1) * LANES)
        normal, along = (ay, ax) if part == 2 else (ax, ay)
        face_lam[:, at] = ((lam_j * along[None]) + (lam_k * az)[None]).reshape(64, LANES)
        face_normal[:, at] = (w_node * w_c[None] * normal[None]).reshape(64, LANES)
    for side, (low, high, ex) in enumerate(
        ((FROM_LEFT_DOWN, FROM_LEFT_UP, 1), (FROM_RIGHT_DOWN, FROM_RIGHT_UP, 0))
    ):
        lengths = [
            jnp.where(
                lane2 < 2 * EZ,
                roll(ghost(low, dim, ex), EZ),
                roll(ghost(high, dim, ex), -EZ),
            )
            for dim in range(3)
        ]
        ax, ay, az = metrics(*lengths)
        line_tab[side, 0] = w_end * w_c * ax
        line_tab[side, 1] = w_end * w_c * ay
        line_tab[side, 2] = jnp.broadcast_to(w_end * w_end * az, (8, LANES))

    for load in loads:
        load.wait()

    def step(index, carry):
        phase = lax.rem(index, SMOOTH)
        cycle = lax.div(index, SMOOTH)
        slot = lax.rem(index, 2)
        is_coarse = phase == 2
        second = (phase == 1) | (phase == 4)

        @pl.when(is_coarse)
        def _():
            coarse(cycle)

        @pl.when(jnp.logical_not(is_coarse))
        def _():
            keep = jnp.where(second, rho_new * rho_old, 0.0)
            take = jnp.where(second, 2.0 * rho_new / radius, 1.0 / center)
            smoother(keep, take)

        own_pairs()
        exchange_faces(slot, 2)
        for ex in range(EX):
            d_ref[ex] = u_ref[ex]
            x_ref[ex] += u_ref[ex]

        @pl.when(index < SMOOTH * CYCLES - 1)
        def _():
            result, lines = outer_terms(slot)
            stiffness()
            add_outer(result, lines)
            own_pairs()
            for ex in range(EX):
                r_ref[ex] -= free_scaled(u_ref[ex])

        return carry

    lax.fori_loop(0, SMOOTH * CYCLES, step, 0)

    by_node = [
        [
            jnp.concatenate(
                [x_ref[ex, a, pl.ds(c, 8, stride=8)] for a in range(NODES)], axis=0
            )
            for c in range(NODES)
        ]
        for ex in range(EX)
    ]
    rows = []
    for ex in range(EX):
        for ey in range(EY):
            halves = []
            for half in range(2):
                joined = None
                for s in range(4):
                    part = roll(by_node[ex][half * 4 + s], EZ * (s - ey))
                    joined = part if s == 0 else jnp.where(lane2 >= EZ * s, part, joined)
                halves.append(joined)
            rows.append(jnp.concatenate(halves, axis=1))
    result = exact_rows(jnp.concatenate(rows, axis=0), perm_ref[3])
    for half in range(2):
        at = slice(half * LANES, (half + 1) * LANES)
        for k in range(EX * EY):
            for a in range(NODES):
                first = k * 64 + a * 8
                d_ref[half, a, pl.ds(k, 8, stride=8)] = result[first : first + 8, at]
    for half in range(2):
        at = slice(half * LANES, (half + 1) * LANES)
        out_ref[:, at] = d_ref[half].reshape(512, LANES)


def per_device(source, geometry, disc_mask, thrust, xxt_factor, col_count):
    n_gx = lax.axis_size("gx")
    n_gy = lax.axis_size("gy")
    levels = xxt_factor.shape[0]
    wide = (levels - 1) * XCOLS
    split = (n_gy.bit_length() - 1) * XCOLS
    matrices, plane, table, perms, interp, stiff, weights = constant_tables()
    geom = jnp.concatenate(
        [geometry.reshape(3 * EX, LANES), jnp.ones((8 - 3 * EX, LANES), jnp.float32)], axis=0
    )
    force = (disc_mask.astype(jnp.float32) * thrust).reshape(EX, LANES)
    live = (jnp.arange(XCOLS)[None, :] < col_count).astype(jnp.float32)
    live = jnp.concatenate(
        [
            live[0:1],
            jnp.zeros((1, LANES - XCOLS), jnp.float32),
            live[1:].reshape(1, wide),
        ],
        axis=1,
    )
    field = (EX, NODES, 64, LANES)
    f32 = jnp.float32
    out = pl.pallas_call(
        functools.partial(kernel, n_gx, n_gy, levels, interp, stiff, weights),
        out_shape=jax.ShapeDtypeStruct((512, 256), f32),
        in_specs=[pl.BlockSpec(memory_space=pltpu.VMEM)] * 4
        + [pl.BlockSpec(memory_space=pl.ANY)] * 2
        + [pl.BlockSpec(memory_space=pltpu.VMEM)] * 3,
        out_specs=pl.BlockSpec(memory_space=pltpu.VMEM),
        scratch_shapes=[
            pltpu.VMEM(field, f32),
            pltpu.VMEM(field, f32),
            pltpu.VMEM(field, f32),
            pltpu.VMEM(field, f32),
            pltpu.VMEM(field[1:], f32),
            pltpu.VMEM(field[1:], f32),
            pltpu.VMEM(field, f32),
            pltpu.VMEM(field, f32),
            pltpu.VMEM((64, 3 * LANES), f32),
            pltpu.VMEM((64, 3 * LANES), f32),
            pltpu.VMEM((2, 3, 8, LANES), f32),
            pltpu.VMEM((levels * XCOLS, xxt_factor.shape[2]), f32),
            pltpu.VMEM(matrices.shape, jnp.bfloat16),
            pltpu.VMEM((2, 2, 2, 64, LANES), f32),
            pltpu.VMEM((2, 2, 8, 8, LANES), f32),
            pltpu.VMEM((2, 4, 3, 8, LANES), f32),
            pltpu.VMEM((2, 2, 2, 64, LANES), f32),
            pltpu.VMEM((2, 2, 2, 8, 8, LANES), f32),
            pltpu.VMEM((2, 4, 3, 8, LANES), f32),
            pltpu.VMEM((8, 8, LANES), f32),
            pltpu.VMEM((1, wide), f32),
            pltpu.VMEM((CYCLES, n_gy - 1, 1, wide), f32),
            pltpu.VMEM((1, wide - split), f32),
            pltpu.VMEM((CYCLES, n_gx - 1, 1, wide - split), f32),
            pltpu.SemaphoreType.DMA((2, 8)),
            pltpu.SemaphoreType.DMA((2, 8)),
            pltpu.SemaphoreType.DMA((8,)),
            pltpu.SemaphoreType.DMA((8,)),
            pltpu.SemaphoreType.DMA((n_gy - 1,)),
            pltpu.SemaphoreType.DMA((CYCLES, n_gy - 1)),
            pltpu.SemaphoreType.DMA((n_gx - 1,)),
            pltpu.SemaphoreType.DMA((CYCLES, n_gx - 1)),
            pltpu.SemaphoreType.DMA((2,)),
        ],
        compiler_params=pltpu.CompilerParams(
            collective_id=0, has_side_effects=True, vmem_limit_bytes=48 * 1024 * 1024
        ),
    )(
        source.reshape(NODES * NODES * EX * EY, EZ * NODES),
        geom,
        force,
        live,
        xxt_factor.reshape(levels * XCOLS, xxt_factor.shape[2]),
        jnp.asarray(matrices),
        jnp.asarray(plane),
        jnp.asarray(table),
        jnp.asarray(perms),
    )
    return out.reshape(source.shape)


def solution(mesh):
    return jax.shard_map(
        per_device,
        mesh=mesh,
        in_specs=(
            P(None, None, "gx", "gy", None),
            P(None, "gx", "gy", None),
            P("gx", "gy", None),
            P("gx", "gy", None),
            P(None, None, ("gx", "gy")),
            P(None, ("gx", "gy")),
        ),
        out_specs=P(None, None, "gx", "gy", None),
        check_vma=False,
    )
```

```python
import functools
import math

import jax
import jax.numpy as jnp
import ml_dtypes
import numpy as np
from jax import lax
from jax.experimental import pallas as pl
from jax.experimental.pallas import tpu as pltpu
from jax.sharding import PartitionSpec as P

NODES = 8
CYCLES = 2
EX = 2
EY = 4
EZ = 32
LANES = EY * EZ
XCOLS = 32
SMOOTH = 5

bound_low = 0.3
bound_high = 3.0
shift_ratio = 0.25
MESH = pl.DeviceIdType.MESH


def legendre_table(points, poly_order):
    table = [points * 0.0 + 1.0, points]
    for degree in range(2, poly_order + 1):
        table.append(
            ((2.0 * degree - 1.0) * points * table[-1] - (degree - 1.0) * table[-2]) / degree
        )
    return table


def jacobi_eigen(matrix):
    size_n = matrix.shape[0]
    current = matrix.copy()
    vectors = np.eye(size_n)
    for sweep_index in range(30):
        for first in range(size_n - 1):
            for second in range(first + 1, size_n):
                angle = 0.5 * math.atan2(
                    2.0 * float(current[first, second]),
                    float(current[second, second] - current[first, first]),
                )
                rotation = np.eye(size_n)
                rotation[first, first] = math.cos(angle)
                rotation[second, second] = math.cos(angle)
                rotation[first, second] = math.sin(angle)
                rotation[second, first] = -math.sin(angle)
                current = rotation.T @ current @ rotation
                vectors = vectors @ rotation
    values = np.array([current[index, index] for index in range(size_n)])
    order = np.argsort(values)
    return (values[order], vectors[:, order])


def gll_tables(node_count):
    poly_order = node_count - 1
    points = np.cos(np.pi * np.arange(node_count) / poly_order)
    for newton_index in range(200):
        table = legendre_table(points, poly_order)
        points = points - (points * table[poly_order] - table[poly_order - 1]) / (
            node_count * table[poly_order]
        )
    points = points[::-1].copy()
    legendre = legendre_table(points, poly_order)[poly_order]
    weights = 2.0 / (poly_order * (poly_order + 1) * legendre**2)
    identity = np.eye(node_count)
    gap_matrix = points[:, None] - points[None, :] + identity
    off_diagonal = legendre[:, None] / (legendre[None, :] * gap_matrix) * (1.0 - identity)
    end_value = poly_order * (poly_order + 1) / 4.0
    end_terms = np.concatenate([[-end_value], np.zeros(node_count - 2), [end_value]])
    derivative = off_diagonal + identity * end_terms[None, :]
    stiffness = derivative.T @ (weights[:, None] * derivative)
    root_inverse = 1.0 / np.sqrt(weights)
    symmetric = root_inverse[:, None] * stiffness * root_inverse[None, :]
    symmetric = 0.5 * (symmetric + symmetric.T)
    eigen_values, eigen_vectors = jacobi_eigen(symmetric)
    eigen_modes = root_inverse[:, None] * eigen_vectors
    vertex_interp = np.stack([(1.0 - points) / 2.0, (1.0 + points) / 2.0], axis=1)
    return weights, stiffness, eigen_modes, eigen_values, vertex_interp


def mode_order(modes):
    even = [i for i in range(NODES) if modes[0, i] * modes[NODES - 1, i] > 0.0]
    odd = [i for i in range(NODES) if i not in even]
    return even, odd


def split_pair(matrix):
    exact = matrix.astype(np.float32)
    high = exact.astype(ml_dtypes.bfloat16)
    low = (exact - high.astype(np.float32)).astype(ml_dtypes.bfloat16)
    return np.concatenate([high, high, low], axis=1)


def constant_tables():
    weights, stiffness, modes, values, interp = gll_tables(NODES)
    even, odd = mode_order(modes)
    half = NODES // 2
    mats = []
    for chosen in (even, odd):
        inverse = np.kron(modes[:half][:, chosen], np.kron(modes, modes))
        mats.append((split_pair(inverse.T), split_pair(inverse)))
    matrices = np.stack([mats[0][0], mats[1][0], mats[0][1], mats[1][1]])
    plane = np.kron(modes, modes)
    plane_matrices = np.stack([split_pair(plane.T), split_pair(plane)])
    full = np.ones((NODES, LANES))
    edge = np.ones(NODES)
    edge[0] = edge[-1] = 0.5
    ez = np.arange(LANES)[None, :] % EZ
    node = np.arange(NODES)[:, None]
    z_shared = 1.0 + ((node == 0) & (ez > 0)) + ((node == NODES - 1) & (ez < EZ - 1))
    free = 1.0 - ((node == NODES - 1) & (ez == EZ - 1))
    rows = [values[i] * full for i in even + odd]
    rows += [value * full for value in values]
    rows += [weight * full for weight in weights]
    rows += [value * full for value in edge]
    rows += [values[:, None] * full, weights[:, None] * full, free / z_shared, free * full]
    rows += [interp[:, 0:1] * full, interp[:, 1:2] * full]
    rows += [stiffness[:, c : c + 1] * full for c in range(NODES)]
    table = np.stack(rows).astype(np.float32)
    perm = np.zeros((2 * LANES, 2 * LANES), np.float32)
    for t in range(2):
        for element in range(LANES):
            perm[t * LANES + element, 2 * element + t] = 1.0
    order = np.zeros((EZ * NODES, EZ * NODES), np.float32)
    for c in range(NODES):
        for element in range(EZ):
            order[element * NODES + c, c * EZ + element] = 1.0
    perms = np.stack([perm, perm.T, order, order.T]).astype(ml_dtypes.bfloat16)
    return (
        matrices,
        plane_matrices,
        table,
        perms,
        interp.astype(np.float32),
        stiffness.astype(np.float32),
        weights.astype(np.float32),
    )


def flipped(index, bits):
    out = index
    bit = 1
    while bit <= bits:
        if bits & bit:
            out = out + bit - 2 * bit * lax.rem(lax.div(index, bit), 2)
        bit *= 2
    return out


def exact_rows(value, perm):
    first = value.astype(jnp.bfloat16)
    rest = value - first.astype(jnp.float32)
    second = rest.astype(jnp.bfloat16)
    third = (rest - second.astype(jnp.float32)).astype(jnp.bfloat16)
    parts = [
        jnp.dot(part, perm, preferred_element_type=jnp.float32)
        for part in (first, second, third)
    ]
    return parts[0] + parts[1] + parts[2]


def kernel(
    n_gx,
    n_gy,
    levels,
    interp,
    stiff,
    weights,
    source_hbm,
    lengths_hbm,
    disc_hbm,
    thrust_hbm,
    count_hbm,
    x_hbm,
    mat_hbm,
    plane_hbm,
    tab_hbm,
    perm_hbm,
    out_ref,
    source_ref,
    lengths_ref,
    disc_ref,
    thrust_ref,
    count_ref,
    plane_ref,
    tab_ref,
    perm_ref,
    geom_ref,
    live_ref,
    u_ref,
    r_ref,
    d_ref,
    x_ref,
    weight_ref,
    winv_ref,
    lam_ref,
    inv_ref,
    face_lam,
    face_normal,
    line_tab,
    x_factor_ref,
    mat_ref,
    send_x,
    send_y,
    send_c,
    recv_x,
    recv_y,
    recv_c,
    recv_g,
    send_one,
    recv_one,
    send_two,
    recv_two,
    send_sem,
    recv_sem,
    g_send_sem,
    g_recv_sem,
    one_send_sem,
    one_recv_sem,
    two_send_sem,
    two_recv_sem,
    load_sem,
):
    me_x = lax.axis_index("gx")
    me_y = lax.axis_index("gy")
    left = lax.rem(me_x + n_gx - 1, n_gx)
    right = lax.rem(me_x + 1, n_gx)
    down = lax.rem(me_y + n_gy - 1, n_gy)
    up = lax.rem(me_y + 1, n_gy)
    targets = [
        (left, me_y),
        (right, me_y),
        (me_x, down),
        (me_x, up),
        (left, down),
        (right, up),
        (left, up),
        (right, down),
    ]
    FROM_RIGHT, FROM_LEFT, FROM_UP, FROM_DOWN = 0, 1, 2, 3
    FROM_RIGHT_UP, FROM_LEFT_DOWN, FROM_RIGHT_DOWN, FROM_LEFT_UP = 4, 5, 6, 7
    one_targets = [(me_x, flipped(me_y, off)) for off in range(1, n_gy)]
    two_targets = [(flipped(me_x, off), me_y) for off in range(1, n_gx)]
    barrier = pltpu.get_barrier_semaphore()
    everyone = targets + one_targets + two_targets
    for target in everyone:
        pl.semaphore_signal(barrier, inc=1, device_id=target, device_id_type=MESH)
    loads = [
        pltpu.make_async_copy(src, dst, load_sem.at[index])
        for index, (src, dst) in enumerate(
            (
                (tab_hbm, tab_ref),
                (source_hbm, source_ref),
                (perm_hbm, perm_ref),
                (lengths_hbm, lengths_ref),
                (disc_hbm, disc_ref),
                (thrust_hbm, thrust_ref),
                (count_hbm, count_ref),
                (mat_hbm, mat_ref),
                (plane_hbm, plane_ref),
                (x_hbm, x_factor_ref),
            )
        )
    ]
    for load in loads:
        load.start()
    first_loads, later_loads = loads[:7], loads[7:]

    lane = lax.broadcasted_iota(jnp.int32, (1, 1, 1, LANES), 3)
    lane3 = lax.broadcasted_iota(jnp.int32, (1, 1, LANES), 2)
    lane2 = lax.broadcasted_iota(jnp.int32, (1, LANES), 1)
    z2 = lax.rem(lane2, EZ)

    def roll(value, shift):
        shift = shift % LANES
        return value if shift == 0 else pltpu.roll(value, shift, value.ndim - 1)

    for load in first_loads:
        load.wait()
    for dim in range(3):
        for ex in range(EX):
            geom_ref[2 * dim + ex : 2 * dim + ex + 1] = jnp.concatenate(
                [lengths_ref[dim, ex, ey : ey + 1] for ey in range(EY)], axis=1
            )
    geom_ref[6:8] = jnp.ones((2, LANES), jnp.float32)
    forces = []
    for ex in range(EX):
        element = disc_ref[ex].astype(jnp.float32) * thrust_ref[ex]
        forces.append(
            jnp.concatenate([element[ey : ey + 1] for ey in range(EY)], axis=1)
        )
    column = lax.rem(lane2, XCOLS)
    for first in range(0, levels, LANES // XCOLS):
        chosen = [0] * 4 if first == 0 else range(first - 3, first + 1)
        count = None
        for place, level in enumerate(chosen):
            one = jnp.broadcast_to(count_ref[level : level + 1], (1, LANES))
            count = one if count is None else jnp.where(lane2 >= XCOLS * place, one, count)
        at = slice(first // 4 * LANES, (first // 4 + 1) * LANES)
        live_ref[:, at] = (column < count).astype(jnp.float32)
    lam_i = tab_ref[0:8]
    lam_j = tab_ref[8:16]
    w_node = tab_ref[16:24]
    edge = tab_ref[24:32]
    lam_k = tab_ref[32]
    w_c = tab_ref[33]
    zmask = tab_ref[34]
    free = tab_ref[35]
    w_end = float(weights[0])
    k_end = float(stiff[0, 0])
    weight_ref[...] = (w_node[:, None] * w_node[None] * w_c[None, None]).reshape(8, 64, LANES)
    winv_ref[...] = (edge[:, None] * edge[None] * zmask[None, None]).reshape(8, 64, LANES)

    def metrics(hx, hy, hz):
        return hy * hz / (2.0 * hx), hx * hz / (2.0 * hy), hx * hy / (2.0 * hz)

    for half in range(2):
        at = slice(half * LANES, (half + 1) * LANES)
        d_ref[half] = source_ref[:, at].reshape(8, 64, LANES)
    by_node = exact_rows(
        jnp.concatenate(
            [
                jnp.concatenate(
                    [d_ref[half, a, pl.ds(k, 8, stride=8)] for half in range(2)], axis=1
                )
                for k in range(EX * EY)
                for a in range(NODES)
            ],
            axis=0,
        ),
        perm_ref[2],
    )
    for ex in range(EX):
        for c in range(NODES):
            at = slice(c // 4 * LANES, (c // 4 + 1) * LANES)
            joined = None
            for ey in range(EY):
                first = (ex * EY + ey) * 64
                part = roll(by_node[first : first + 64, at], EZ * (ey - c % 4))
                joined = part if ey == 0 else jnp.where(lane2 >= EZ * ey, part, joined)
            for a in range(NODES):
                u_ref[ex, a, pl.ds(c, 8, stride=8)] = joined[8 * a : 8 * a + 8]

    for ex in range(EX):
        hx = geom_ref[ex : ex + 1]
        hy = geom_ref[2 + ex : 3 + ex]
        hz = geom_ref[4 + ex : 5 + ex]
        ax, ay, az = metrics(hx, hy, hz)
        in_x = lam_i * ax[None]
        in_y = lam_j * ay[None]
        in_z = lam_k * az
        spectrum = (in_x[:, None] + in_y[None] + in_z[None, None]).reshape(8, 64, LANES)
        shift = shift_ratio * (ax + ay + az)
        lam_ref[ex] = spectrum
        inv_ref[ex] = 1.0 / (spectrum + shift[None])
        mass = (hx * hy * hz / 8.0)[None] * weight_ref[...]
        u_ref[ex] = mass * (u_ref[ex] + forces[ex][None])

    def free_scaled(value):
        return (value.reshape(8, 8, 8, LANES) * free[None, None]).reshape(8, 64, LANES)

    for ex in range(EX):
        u_ref[ex] = free_scaled(u_ref[ex])

    pl.semaphore_wait(barrier, len(everyone))

    geom_copies = []
    for index, target in enumerate(targets):
        copy = pltpu.make_async_remote_copy(
            src_ref=geom_ref,
            dst_ref=recv_g.at[index],
            send_sem=g_send_sem.at[index],
            recv_sem=g_recv_sem.at[index],
            device_id=target,
            device_id_type=MESH,
        )
        copy.start()
        geom_copies.append(copy)

    def own_pairs():
        shared = u_ref[0, 7] + u_ref[1, 0]
        u_ref[0, 7] = shared
        u_ref[1, 0] = shared
        low = u_ref[:, :, 0:8]
        high = u_ref[:, :, 56:64]
        u_ref[:, :, 0:8] = low + jnp.where(lane >= EZ, roll(high, EZ), 0.0)
        u_ref[:, :, 56:64] = high + jnp.where(lane < LANES - EZ, roll(low, -EZ), 0.0)
        for ex in range(EX):
            for a in range(NODES):
                low = u_ref[ex, a, pl.ds(0, 8, stride=8)]
                high = u_ref[ex, a, pl.ds(7, 8, stride=8)]
                u_ref[ex, a, pl.ds(0, 8, stride=8)] = low + jnp.where(
                    z2 > 0, roll(high, 1), 0.0
                )
                u_ref[ex, a, pl.ds(7, 8, stride=8)] = high + jnp.where(
                    z2 < EZ - 1, roll(low, -1), 0.0
                )

    def packed_y(down_faces, up_faces):
        return jnp.where(
            lane3 < EZ,
            down_faces[0],
            jnp.where(
                lane3 < 2 * EZ,
                roll(down_faces[1], EZ),
                jnp.where(lane3 < 3 * EZ, roll(up_faces[0], -EZ), up_faces[1]),
            ),
        )

    def y_faces():
        return packed_y(
            [u_ref[ex, :, 0:8] for ex in range(EX)], [u_ref[ex, :, 56:64] for ex in range(EX)]
        )

    def weighted(parts, row):
        total = None
        for index, part in parts:
            term = part * float(stiff[row, index])
            total = term if total is None else total + term
        return total

    def exchange_faces(slot, planes):
        send_x[slot, 0, 0] = u_ref[0, 0]
        send_x[slot, 1, 0] = u_ref[1, 7]
        send_y[slot, 0] = y_faces()
        corners = (
            (u_ref[0, 0, 0:8], 0),
            (u_ref[1, 7, 56:64], EY - 1),
            (u_ref[0, 0, 56:64], EY - 1),
            (u_ref[1, 7, 0:8], 0),
        )
        lines = [roll(value, -EZ * ey) for value, ey in corners]
        if planes > 1:
            low = weighted([(a, u_ref[0, a]) for a in range(1, NODES)], 0)
            high = weighted([(a, u_ref[1, a]) for a in range(NODES - 1)], 7)
            send_x[slot, 0, 1] = low
            send_x[slot, 1, 1] = high
            down_normal, up_normal = [], []
            for ex in range(EX):
                rows = [u_ref[ex, :, 8 * b : 8 * b + 8] for b in range(NODES)]
                down_normal.append(weighted([(b, rows[b]) for b in range(1, NODES)], 0))
                up_normal.append(weighted([(b, rows[b]) for b in range(NODES - 1)], 7))
            normal = packed_y(down_normal, up_normal)
            send_y[slot, 1] = normal
            along_x = (low[0:8], high[56:64], low[56:64], high[0:8])
            along_y = ((normal[0], 0), (normal[7], 3), (normal[0], 2), (normal[7], 1))
            lines = [
                jnp.where(
                    lane2 < EZ,
                    lines[i],
                    jnp.where(
                        lane2 < 2 * EZ,
                        roll(along_x[i], EZ * (1 - corners[i][1])),
                        roll(along_y[i][0], EZ * (2 - along_y[i][1])),
                    ),
                )
                for i in range(4)
            ]
        for i in range(4):
            send_c[slot, i] = lines[i]
        pairs = (
            [
                (send_x.at[slot, i, pl.ds(0, planes)], recv_x.at[slot, i, pl.ds(0, planes)])
                for i in range(2)
            ]
            + [
                (send_y.at[slot, pl.ds(0, planes)], recv_y.at[slot, i, pl.ds(0, planes)])
                for i in range(2)
            ]
            + [(send_c.at[slot, i], recv_c.at[slot, i]) for i in range(4)]
        )
        copies = []
        for index in (4, 5, 6, 7, 0, 1, 2, 3):
            source, landing = pairs[index]
            copy = pltpu.make_async_remote_copy(
                src_ref=source,
                dst_ref=landing,
                send_sem=send_sem.at[slot, index],
                recv_sem=recv_sem.at[slot, index],
                device_id=targets[index],
                device_id_type=MESH,
            )
            copy.start()
            copies.append(copy)
        for copy in copies:
            copy.wait()
        u_ref[1, 7] += recv_x[slot, FROM_RIGHT, 0]
        u_ref[0, 0] += recv_x[slot, FROM_LEFT, 0]
        add_y(arrived_y(slot, 0))
        for index, (ex, a, first, to_ey) in enumerate(
            ((1, 7, 56, EY - 1), (0, 0, 0, 0), (1, 7, 0, 0), (0, 0, 56, EY - 1))
        ):
            u_ref[ex, a, first : first + 8] += in_slot(
                roll(recv_c[slot, index], EZ * to_ey), to_ey
            )

    def arrived_y(slot, plane):
        from_up = recv_y[slot, FROM_UP - 2, plane]
        from_down = recv_y[slot, FROM_DOWN - 2, plane]
        return roll(jnp.where(lane3 >= 2 * EZ, from_down, from_up), 2 * EZ)

    def add_y(plane):
        for ex in range(EX):
            u_ref[ex, :, 0:8] += jnp.where(lane3 < EZ, roll(plane, -EZ * ex), 0.0)
            u_ref[ex, :, 56:64] += jnp.where(
                lane3 >= 3 * EZ, roll(plane, EZ * (1 - ex)), 0.0
            )

    def in_slot(value, slot):
        return jnp.where((lane2 >= EZ * slot) & (lane2 < EZ * (slot + 1)), value, 0.0)

    def outer_terms(slot):
        face = jnp.concatenate(
            [u_ref[0, 0], u_ref[1, 7], y_faces().reshape(64, LANES)], axis=1
        )
        from_left_down = recv_c[slot, FROM_LEFT_DOWN - 4]
        from_left_up = recv_c[slot, FROM_LEFT_UP - 4]
        from_right_down = recv_c[slot, FROM_RIGHT_DOWN - 4]
        from_right_up = recv_c[slot, FROM_RIGHT_UP - 4]
        sides = []
        for plane, low, high in (
            (recv_x[slot, FROM_LEFT, 1], from_left_down, from_left_up),
            (recv_x[slot, FROM_RIGHT, 1], from_right_down, from_right_up),
        ):
            sides.append(
                jnp.concatenate(
                    [
                        plane[0:8] + in_slot(roll(low, -EZ), 0),
                        plane[8:56],
                        plane[56:64] + in_slot(roll(high, 2 * EZ), 3),
                    ],
                    axis=0,
                )
            )
        normal_y = arrived_y(slot, 1)
        first = (
            normal_y[0]
            + in_slot(roll(from_left_down, -2 * EZ), 0)
            + in_slot(from_left_up, 2)
        )
        last = (
            normal_y[7]
            + in_slot(roll(from_right_down, -EZ), 1)
            + in_slot(roll(from_right_up, EZ), 3)
        )
        normal_y = jnp.concatenate([first[None], normal_y[1:7], last[None]], axis=0)
        normal = jnp.concatenate([sides[0], sides[1], normal_y.reshape(64, LANES)], axis=1)
        weight = weight_ref[0] * (1.0 / w_end)
        weight = jnp.concatenate([weight] * 3, axis=1)
        spread = small_product(1, face_lam[...] * small_product(0, weight * face))
        result = face_normal[...] * (normal + k_end * face) + w_end * weight * spread
        lines = []
        for side in range(2):
            plane = face[:, side * LANES : (side + 1) * LANES]
            value = jnp.where(lane2 < 2 * EZ, plane[0:8], plane[56:64])
            along_x = jnp.where(lane2 < 2 * EZ, sides[side][0:8], sides[side][56:64])
            edge_y = last if side else first
            along_y = jnp.where(
                lane2 < 2 * EZ,
                roll(edge_y, -EZ) if side else edge_y,
                edge_y if side else roll(edge_y, EZ),
            )
            along_z = None
            for c in range(NODES):
                term = tab_ref[38 + c] * value[c : c + 1]
                along_z = term if along_z is None else along_z + term
            lines.append(
                line_tab[side, 0] * (along_x + k_end * value)
                + line_tab[side, 1] * (along_y + k_end * value)
                + line_tab[side, 2] * along_z
            )
        return result, lines

    def add_outer(result, lines):
        for side, (ex, a) in enumerate(((0, 0), (1, 7))):
            u_ref[ex, a] += result[:, side * LANES : (side + 1) * LANES]
            u_ref[ex, a, 0:8] += in_slot(lines[side], 0)
            u_ref[ex, a, 56:64] += in_slot(lines[side], 3)
        add_y(result[:, 2 * LANES :].reshape(8, 8, LANES))

    def small_product(which, value):
        high = value.astype(jnp.bfloat16)
        low = (value - high.astype(jnp.float32)).astype(jnp.bfloat16)
        return jnp.dot(
            plane_ref[which],
            jnp.concatenate([high, low, high], axis=0),
            preferred_element_type=jnp.float32,
        )

    def product(which, value):
        high = value.astype(jnp.bfloat16)
        low = (value - high.astype(jnp.float32)).astype(jnp.bfloat16)
        return jnp.dot(
            mat_ref[which],
            jnp.concatenate([high, low, high], axis=0),
            preferred_element_type=jnp.float32,
        )

    def flat(parts):
        return jnp.concatenate([part.reshape(256, LANES) for part in parts], axis=1)

    def element_op(fields, diag_ref):
        even, odd = [], []
        for field in fields:
            low = field[0:4]
            high = jnp.concatenate([field[7:8], field[6:7], field[5:6], field[4:5]], axis=0)
            even.append(low + high)
            odd.append(low - high)
        even = product(0, flat(even)) * flat([diag_ref[ex, 0:4] for ex in range(EX)])
        odd = product(1, flat(odd)) * flat([diag_ref[ex, 4:8] for ex in range(EX)])
        even = product(2, even)
        odd = product(3, odd)
        out = []
        for ex in range(EX):
            at = slice(ex * LANES, (ex + 1) * LANES)
            e = even[:, at].reshape(4, 64, LANES)
            o = odd[:, at].reshape(4, 64, LANES)
            diff = e - o
            out.append(
                jnp.concatenate([e + o, diff[3:4], diff[2:3], diff[1:2], diff[0:1]], axis=0)
            )
        return out

    def stiffness():
        weight = weight_ref[...]
        out = element_op([u_ref[ex] * weight for ex in range(EX)], lam_ref)
        for ex in range(EX):
            u_ref[ex] = out[ex] * weight

    def smoother(keep, take):
        out = element_op([r_ref[ex] for ex in range(EX)], inv_ref)
        for ex in range(EX):
            u_ref[ex] = (take * out[ex] + keep * d_ref[ex]) * winv_ref[...]

    wide = (levels - 1) * XCOLS
    gy_bits = n_gy.bit_length() - 1
    split = gy_bits * XCOLS

    def exchange(cycle, send_ref, recv_ref, to, send_s, recv_s):
        copies = []
        for index, target in enumerate(to):
            copy = pltpu.make_async_remote_copy(
                src_ref=send_ref,
                dst_ref=recv_ref.at[cycle, index],
                send_sem=send_s.at[index],
                recv_sem=recv_s.at[cycle, index],
                device_id=target,
                device_id_type=MESH,
            )
            copy.start()
            copies.append(copy)
        for copy in copies:
            copy.wait()

    def level_sum(own, recv_ref, cycle, count, first_level_lane):
        which = lax.broadcasted_iota(jnp.int32, own.shape, 1)
        total = own
        start = 1
        bit = 0
        while start < count:
            part = recv_ref[cycle, start - 1]
            for index in range(start + 1, 2 * start):
                part = part + recv_ref[cycle, index - 1]
            total = total + jnp.where(which >= bit * XCOLS + first_level_lane, part, 0.0)
            start *= 2
            bit += 1
        return total

    def coarse(cycle):
        sums = {}
        for ex in range(EX):
            scaled = r_ref[ex] * winv_ref[...]
            for v in range(2):
                by_v = scaled[0] * float(interp[0, v])
                for a in range(1, NODES):
                    by_v = by_v + scaled[a] * float(interp[a, v])
                by_v = by_v.reshape(8, 8, LANES)
                for u in range(2):
                    by_u = by_v[0] * float(interp[0, u])
                    for b in range(1, NODES):
                        by_u = by_u + by_v[b] * float(interp[b, u])
                    for t in range(2):
                        sums[v, u, ex, t] = jnp.sum(
                            by_u * tab_ref[36 + t], axis=0, keepdims=True
                        )
        order = [(v, u, ex) for v in range(2) for u in range(2) for ex in range(EX)]
        split_t = jnp.concatenate(
            [jnp.concatenate([sums[key + (t,)] for t in range(2)], axis=1) for key in order],
            axis=0,
        )
        vector = exact_rows(split_t, perm_ref[0])
        pieces = []
        for level in range(levels):
            rows = slice(level * XCOLS, (level + 1) * XCOLS)
            acc = None
            for q in range(8):
                term = x_factor_ref[rows, q * 256 : (q + 1) * 256] * vector[q : q + 1]
                acc = term if acc is None else acc + term
            pieces.append(acc[:, :LANES] + acc[:, LANES:])
        def row_of(parts):
            block = jnp.concatenate(parts, axis=0)
            missing = LANES - block.shape[0]
            if missing:
                block = jnp.concatenate([block, jnp.zeros((missing, LANES), jnp.float32)], axis=0)
            return jnp.sum(block.T, axis=0, keepdims=True)
        own = row_of(pieces[0:1])
        upper = jnp.concatenate(
            [row_of(pieces[i : i + 4]) for i in range(1, levels, 4)], axis=1
        )[:, :wide]
        send_one[...] = upper
        exchange(cycle, send_one, recv_one, one_targets, one_send_sem, one_recv_sem)
        upper = level_sum(upper, recv_one, cycle, n_gy, 0)
        send_two[...] = upper[:, split:]
        exchange(cycle, send_two, recv_two, two_targets, two_send_sem, two_recv_sem)
        top = level_sum(upper[:, split:], recv_two, cycle, n_gx, 0)
        upper = jnp.concatenate([upper[:, :split], top], axis=1)
        own = own * live_ref[:, 0:LANES]
        upper = upper * live_ref[:, LANES : LANES + wide]
        tail = (-wide) % LANES
        if tail:
            upper = jnp.concatenate([upper, jnp.zeros((1, tail), jnp.float32)], axis=1)
        cols = [jnp.broadcast_to(own, (LANES, LANES)).T[:XCOLS]]
        for first in range(0, wide, LANES):
            part = jnp.broadcast_to(upper[:, first : first + LANES], (LANES, LANES)).T
            cols += [part[k * XCOLS : (k + 1) * XCOLS] for k in range(LANES // XCOLS)]
        back = []
        for q in range(8):
            acc = None
            for level in range(levels):
                block = x_factor_ref[
                    level * XCOLS : (level + 1) * XCOLS, q * 256 : (q + 1) * 256
                ]
                col = cols[level]
                term = block * jnp.concatenate([col, col], axis=1)
                acc = term if acc is None else acc + term
            back.append(jnp.sum(acc, axis=0, keepdims=True))
        split_t = exact_rows(jnp.concatenate(back, axis=0), perm_ref[1])
        for ex in range(EX):
            by_v = []
            for v in range(2):
                by_u = []
                for u in range(2):
                    q = (v * 2 + u) * EX + ex
                    by_u.append(
                        split_t[q : q + 1, :LANES] * tab_ref[36]
                        + split_t[q : q + 1, LANES:] * tab_ref[37]
                    )
                by_v.append(
                    jnp.concatenate(
                        [
                            by_u[0] * float(interp[b, 0]) + by_u[1] * float(interp[b, 1])
                            for b in range(NODES)
                        ],
                        axis=0,
                    )
                )
            for a in range(NODES):
                u_ref[ex, a] = winv_ref[a] * (
                    by_v[0] * float(interp[a, 0]) + by_v[1] * float(interp[a, 1])
                )

    center = 0.5 * (bound_high + bound_low)
    radius = 0.5 * (bound_high - bound_low)
    ratio = center / radius
    rho_old = 1.0 / ratio
    rho_new = 1.0 / (2.0 * ratio - rho_old)

    own_pairs()
    exchange_faces(1, 1)
    r_ref[...] = u_ref[...]
    d_ref[...] = jnp.zeros_like(d_ref)
    x_ref[...] = jnp.zeros_like(x_ref)

    for copy in geom_copies:
        copy.wait()
    slots = lambda values: jnp.where(
        lane2 < EZ,
        values[0],
        jnp.where(lane2 < 2 * EZ, values[1], jnp.where(lane2 < 3 * EZ, values[2], values[3])),
    )

    def ghost(source, dim, ex):
        return recv_g[source, 2 * dim + ex : 2 * dim + ex + 1]

    outer = []
    for dim in range(3):
        y_side = slots(
            [
                roll(ghost(FROM_DOWN, dim, 0), EZ),
                roll(ghost(FROM_DOWN, dim, 1), 2 * EZ),
                roll(ghost(FROM_UP, dim, 0), 2 * EZ),
                roll(ghost(FROM_UP, dim, 1), 3 * EZ),
            ]
        )
        outer.append([ghost(FROM_LEFT, dim, 1), ghost(FROM_RIGHT, dim, 0), y_side])
    for part in range(3):
        ax, ay, az = metrics(*[outer[dim][part] for dim in range(3)])
        at = slice(part * LANES, (part + 1) * LANES)
        normal, along = (ay, ax) if part == 2 else (ax, ay)
        face_lam[:, at] = ((lam_j * along[None]) + (lam_k * az)[None]).reshape(64, LANES)
        face_normal[:, at] = (w_node * w_c[None] * normal[None]).reshape(64, LANES)
    for side, (low, high, ex) in enumerate(
        ((FROM_LEFT_DOWN, FROM_LEFT_UP, 1), (FROM_RIGHT_DOWN, FROM_RIGHT_UP, 0))
    ):
        lengths = [
            jnp.where(
                lane2 < 2 * EZ,
                roll(ghost(low, dim, ex), EZ),
                roll(ghost(high, dim, ex), -EZ),
            )
            for dim in range(3)
        ]
        ax, ay, az = metrics(*lengths)
        line_tab[side, 0] = w_end * w_c * ax
        line_tab[side, 1] = w_end * w_c * ay
        line_tab[side, 2] = jnp.broadcast_to(w_end * w_end * az, (8, LANES))

    for load in later_loads:
        load.wait()

    def step(index, carry):
        phase = lax.rem(index, SMOOTH)
        cycle = lax.div(index, SMOOTH)
        slot = lax.rem(index, 2)
        is_coarse = phase == 2
        second = (phase == 1) | (phase == 4)

        @pl.when(is_coarse)
        def _():
            coarse(cycle)

        @pl.when(jnp.logical_not(is_coarse))
        def _():
            keep = jnp.where(second, rho_new * rho_old, 0.0)
            take = jnp.where(second, 2.0 * rho_new / radius, 1.0 / center)
            smoother(keep, take)

        own_pairs()
        exchange_faces(slot, 2)
        for ex in range(EX):
            d_ref[ex] = u_ref[ex]
            x_ref[ex] += u_ref[ex]

        @pl.when(index < SMOOTH * CYCLES - 1)
        def _():
            result, lines = outer_terms(slot)
            stiffness()
            add_outer(result, lines)
            own_pairs()
            for ex in range(EX):
                r_ref[ex] -= free_scaled(u_ref[ex])

        return carry

    lax.fori_loop(0, SMOOTH * CYCLES, step, 0)

    by_node = [
        [
            jnp.concatenate(
                [x_ref[ex, a, pl.ds(c, 8, stride=8)] for a in range(NODES)], axis=0
            )
            for c in range(NODES)
        ]
        for ex in range(EX)
    ]
    rows = []
    for ex in range(EX):
        for ey in range(EY):
            halves = []
            for half in range(2):
                joined = None
                for s in range(4):
                    part = roll(by_node[ex][half * 4 + s], EZ * (s - ey))
                    joined = part if s == 0 else jnp.where(lane2 >= EZ * s, part, joined)
                halves.append(joined)
            rows.append(jnp.concatenate(halves, axis=1))
    result = exact_rows(jnp.concatenate(rows, axis=0), perm_ref[3])
    for half in range(2):
        at = slice(half * LANES, (half + 1) * LANES)
        for k in range(EX * EY):
            for a in range(NODES):
                first = k * 64 + a * 8
                d_ref[half, a, pl.ds(k, 8, stride=8)] = result[first : first + 8, at]
    for half in range(2):
        at = slice(half * LANES, (half + 1) * LANES)
        out_ref[:, at] = d_ref[half].reshape(512, LANES)


def per_device(source, geometry, disc_mask, thrust, xxt_factor, col_count):
    n_gx = lax.axis_size("gx")
    n_gy = lax.axis_size("gy")
    levels = xxt_factor.shape[0]
    wide = (levels - 1) * XCOLS
    split = (n_gy.bit_length() - 1) * XCOLS
    matrices, plane, table, perms, interp, stiff, weights = constant_tables()
    field = (EX, NODES, 64, LANES)
    f32 = jnp.float32
    out = pl.pallas_call(
        functools.partial(kernel, n_gx, n_gy, levels, interp, stiff, weights),
        out_shape=jax.ShapeDtypeStruct((512, 256), f32),
        in_specs=[pl.BlockSpec(memory_space=pl.ANY)] * 10,
        out_specs=pl.BlockSpec(memory_space=pltpu.VMEM),
        scratch_shapes=[
            pltpu.VMEM((NODES * NODES * EX * EY, EZ * NODES), f32),
            pltpu.VMEM(geometry.shape, f32),
            pltpu.VMEM(disc_mask.shape, jnp.int32),
            pltpu.VMEM(thrust.shape, f32),
            pltpu.VMEM(col_count.shape, jnp.int32),
            pltpu.VMEM(plane.shape, jnp.bfloat16),
            pltpu.VMEM(table.shape, f32),
            pltpu.VMEM(perms.shape, jnp.bfloat16),
            pltpu.VMEM((8, LANES), f32),
            pltpu.VMEM((1, LANES + wide), f32),
            pltpu.VMEM(field, f32),
            pltpu.VMEM(field, f32),
            pltpu.VMEM(field, f32),
            pltpu.VMEM(field, f32),
            pltpu.VMEM(field[1:], f32),
            pltpu.VMEM(field[1:], f32),
            pltpu.VMEM(field, f32),
            pltpu.VMEM(field, f32),
            pltpu.VMEM((64, 3 * LANES), f32),
            pltpu.VMEM((64, 3 * LANES), f32),
            pltpu.VMEM((2, 3, 8, LANES), f32),
            pltpu.VMEM((levels * XCOLS, xxt_factor.shape[2]), f32),
            pltpu.VMEM(matrices.shape, jnp.bfloat16),
            pltpu.VMEM((2, 2, 2, 64, LANES), f32),
            pltpu.VMEM((2, 2, 8, 8, LANES), f32),
            pltpu.VMEM((2, 4, 8, LANES), f32),
            pltpu.VMEM((2, 2, 2, 64, LANES), f32),
            pltpu.VMEM((2, 2, 2, 8, 8, LANES), f32),
            pltpu.VMEM((2, 4, 8, LANES), f32),
            pltpu.VMEM((8, 8, LANES), f32),
            pltpu.VMEM((1, wide), f32),
            pltpu.VMEM((CYCLES, n_gy - 1, 1, wide), f32),
            pltpu.VMEM((1, wide - split), f32),
            pltpu.VMEM((CYCLES, n_gx - 1, 1, wide - split), f32),
            pltpu.SemaphoreType.DMA((2, 8)),
            pltpu.SemaphoreType.DMA((2, 8)),
            pltpu.SemaphoreType.DMA((8,)),
            pltpu.SemaphoreType.DMA((8,)),
            pltpu.SemaphoreType.DMA((n_gy - 1,)),
            pltpu.SemaphoreType.DMA((CYCLES, n_gy - 1)),
            pltpu.SemaphoreType.DMA((n_gx - 1,)),
            pltpu.SemaphoreType.DMA((CYCLES, n_gx - 1)),
            pltpu.SemaphoreType.DMA((10,)),
        ],
        compiler_params=pltpu.CompilerParams(
            collective_id=0, has_side_effects=True, vmem_limit_bytes=56 * 1024 * 1024
        ),
    )(
        source.reshape(NODES * NODES * EX * EY, EZ * NODES),
        geometry,
        disc_mask,
        thrust,
        col_count,
        xxt_factor.reshape(levels * XCOLS, xxt_factor.shape[2]),
        jnp.asarray(matrices),
        jnp.asarray(plane),
        jnp.asarray(table),
        jnp.asarray(perms),
    )
    return out.reshape(source.shape)


def solution(mesh):
    return jax.shard_map(
        per_device,
        mesh=mesh,
        in_specs=(
            P(None, None, "gx", "gy", None),
            P(None, "gx", "gy", None),
            P("gx", "gy", None),
            P("gx", "gy", None),
            P(None, None, ("gx", "gy")),
            P(None, ("gx", "gy")),
        ),
        out_specs=P(None, None, "gx", "gy", None),
        check_vma=False,
    )
```

```python
import functools
import math

import jax
import jax.numpy as jnp
import ml_dtypes
import numpy as np
from jax import lax
from jax.experimental import pallas as pl
from jax.experimental.pallas import tpu as pltpu
from jax.sharding import PartitionSpec as P

NODES = 8
CYCLES = 2
EX = 2
EY = 4
EZ = 32
LANES = EY * EZ
XCOLS = 32
SMOOTH = 5

bound_low = 0.3
bound_high = 3.0
shift_ratio = 0.25
MESH = pl.DeviceIdType.MESH


def legendre_table(points, poly_order):
    table = [points * 0.0 + 1.0, points]
    for degree in range(2, poly_order + 1):
        table.append(
            ((2.0 * degree - 1.0) * points * table[-1] - (degree - 1.0) * table[-2]) / degree
        )
    return table


def jacobi_eigen(matrix):
    size_n = matrix.shape[0]
    current = matrix.copy()
    vectors = np.eye(size_n)
    for sweep_index in range(30):
        for first in range(size_n - 1):
            for second in range(first + 1, size_n):
                angle = 0.5 * math.atan2(
                    2.0 * float(current[first, second]),
                    float(current[second, second] - current[first, first]),
                )
                rotation = np.eye(size_n)
                rotation[first, first] = math.cos(angle)
                rotation[second, second] = math.cos(angle)
                rotation[first, second] = math.sin(angle)
                rotation[second, first] = -math.sin(angle)
                current = rotation.T @ current @ rotation
                vectors = vectors @ rotation
    values = np.array([current[index, index] for index in range(size_n)])
    order = np.argsort(values)
    return (values[order], vectors[:, order])


def gll_tables(node_count):
    poly_order = node_count - 1
    points = np.cos(np.pi * np.arange(node_count) / poly_order)
    for newton_index in range(200):
        table = legendre_table(points, poly_order)
        points = points - (points * table[poly_order] - table[poly_order - 1]) / (
            node_count * table[poly_order]
        )
    points = points[::-1].copy()
    legendre = legendre_table(points, poly_order)[poly_order]
    weights = 2.0 / (poly_order * (poly_order + 1) * legendre**2)
    identity = np.eye(node_count)
    gap_matrix = points[:, None] - points[None, :] + identity
    off_diagonal = legendre[:, None] / (legendre[None, :] * gap_matrix) * (1.0 - identity)
    end_value = poly_order * (poly_order + 1) / 4.0
    end_terms = np.concatenate([[-end_value], np.zeros(node_count - 2), [end_value]])
    derivative = off_diagonal + identity * end_terms[None, :]
    stiffness = derivative.T @ (weights[:, None] * derivative)
    root_inverse = 1.0 / np.sqrt(weights)
    symmetric = root_inverse[:, None] * stiffness * root_inverse[None, :]
    symmetric = 0.5 * (symmetric + symmetric.T)
    eigen_values, eigen_vectors = jacobi_eigen(symmetric)
    eigen_modes = root_inverse[:, None] * eigen_vectors
    vertex_interp = np.stack([(1.0 - points) / 2.0, (1.0 + points) / 2.0], axis=1)
    return weights, stiffness, eigen_modes, eigen_values, vertex_interp


def mode_order(modes):
    even = [i for i in range(NODES) if modes[0, i] * modes[NODES - 1, i] > 0.0]
    odd = [i for i in range(NODES) if i not in even]
    return even, odd


def split_pair(matrix):
    exact = matrix.astype(np.float32)
    high = exact.astype(ml_dtypes.bfloat16)
    low = (exact - high.astype(np.float32)).astype(ml_dtypes.bfloat16)
    return np.concatenate([high, high, low], axis=1)


def constant_tables():
    weights, stiffness, modes, values, interp = gll_tables(NODES)
    even, odd = mode_order(modes)
    half = NODES // 2
    mats = []
    for chosen in (even, odd):
        inverse = np.kron(modes[:half][:, chosen], np.kron(modes, modes))
        mats.append((split_pair(inverse.T), split_pair(inverse)))
    matrices = np.stack([mats[0][0], mats[1][0], mats[0][1], mats[1][1]])
    plane = np.kron(modes, modes)
    plane_matrices = np.stack([split_pair(plane.T), split_pair(plane)])
    full = np.ones((NODES, LANES))
    edge = np.ones(NODES)
    edge[0] = edge[-1] = 0.5
    ez = np.arange(LANES)[None, :] % EZ
    node = np.arange(NODES)[:, None]
    z_shared = 1.0 + ((node == 0) & (ez > 0)) + ((node == NODES - 1) & (ez < EZ - 1))
    free = 1.0 - ((node == NODES - 1) & (ez == EZ - 1))
    rows = [values[i] * full for i in even + odd]
    rows += [value * full for value in values]
    rows += [weight * full for weight in weights]
    rows += [value * full for value in edge]
    rows += [values[:, None] * full, weights[:, None] * full, free / z_shared, free * full]
    rows += [interp[:, 0:1] * full, interp[:, 1:2] * full]
    rows += [stiffness[:, c : c + 1] * full for c in range(NODES)]
    low_side = np.arange(LANES)[None, :] < LANES // 2
    rows += [
        np.where(low_side, stiffness[b, 0], stiffness[b, NODES - 1]) * full for b in range(NODES)
    ]
    table = np.stack(rows).astype(np.float32)
    perm = np.zeros((2 * LANES, 2 * LANES), np.float32)
    for t in range(2):
        for element in range(LANES):
            perm[t * LANES + element, 2 * element + t] = 1.0
    order = np.zeros((EZ * NODES, EZ * NODES), np.float32)
    for c in range(NODES):
        for element in range(EZ):
            order[element * NODES + c, c * EZ + element] = 1.0
    perms = np.stack([perm, perm.T, order, order.T]).astype(ml_dtypes.bfloat16)
    return (
        matrices,
        plane_matrices,
        table,
        perms,
        interp.astype(np.float32),
        stiffness.astype(np.float32),
        weights.astype(np.float32),
    )


def flipped(index, bits):
    out = index
    bit = 1
    while bit <= bits:
        if bits & bit:
            out = out + bit - 2 * bit * lax.rem(lax.div(index, bit), 2)
        bit *= 2
    return out


def exact_rows(value, perm):
    first = value.astype(jnp.bfloat16)
    rest = value - first.astype(jnp.float32)
    second = rest.astype(jnp.bfloat16)
    third = (rest - second.astype(jnp.float32)).astype(jnp.bfloat16)
    parts = [
        jnp.dot(part, perm, preferred_element_type=jnp.float32)
        for part in (first, second, third)
    ]
    return parts[0] + parts[1] + parts[2]


def kernel(
    n_gx,
    n_gy,
    levels,
    interp,
    stiff,
    weights,
    source_hbm,
    lengths_hbm,
    disc_hbm,
    thrust_hbm,
    count_hbm,
    x_hbm,
    mat_hbm,
    plane_hbm,
    tab_hbm,
    perm_hbm,
    out_ref,
    source_ref,
    lengths_ref,
    disc_ref,
    thrust_ref,
    count_ref,
    plane_ref,
    tab_ref,
    perm_ref,
    geom_ref,
    live_ref,
    u_ref,
    r_ref,
    w_ref,
    x_ref,
    weight_ref,
    winv_ref,
    lam_ref,
    inv_ref,
    face_lam,
    face_normal,
    own_lam,
    own_normal,
    line_tab,
    x_factor_ref,
    mat_ref,
    send_x,
    send_y,
    send_c,
    recv_x,
    recv_y,
    recv_c,
    recv_g,
    send_one,
    recv_one,
    send_two,
    recv_two,
    send_sem,
    recv_sem,
    g_send_sem,
    g_recv_sem,
    one_send_sem,
    one_recv_sem,
    two_send_sem,
    two_recv_sem,
    load_sem,
):
    me_x = lax.axis_index("gx")
    me_y = lax.axis_index("gy")
    left = lax.rem(me_x + n_gx - 1, n_gx)
    right = lax.rem(me_x + 1, n_gx)
    down = lax.rem(me_y + n_gy - 1, n_gy)
    up = lax.rem(me_y + 1, n_gy)
    targets = [
        (left, me_y),
        (right, me_y),
        (me_x, down),
        (me_x, up),
        (left, down),
        (right, up),
        (left, up),
        (right, down),
    ]
    FROM_RIGHT, FROM_LEFT, FROM_UP, FROM_DOWN = 0, 1, 2, 3
    FROM_RIGHT_UP, FROM_LEFT_DOWN, FROM_RIGHT_DOWN, FROM_LEFT_UP = 4, 5, 6, 7
    one_targets = [(me_x, flipped(me_y, off)) for off in range(1, n_gy)]
    two_targets = [(flipped(me_x, off), me_y) for off in range(1, n_gx)]
    barrier = pltpu.get_barrier_semaphore()
    everyone = targets + one_targets + two_targets
    for target in everyone:
        pl.semaphore_signal(barrier, inc=1, device_id=target, device_id_type=MESH)
    loads = [
        pltpu.make_async_copy(src, dst, load_sem.at[index])
        for index, (src, dst) in enumerate(
            (
                (tab_hbm, tab_ref),
                (source_hbm, source_ref),
                (perm_hbm, perm_ref),
                (lengths_hbm, lengths_ref),
                (disc_hbm, disc_ref),
                (thrust_hbm, thrust_ref),
                (count_hbm, count_ref),
                (mat_hbm, mat_ref),
                (plane_hbm, plane_ref),
                (x_hbm, x_factor_ref),
            )
        )
    ]
    for load in loads:
        load.start()
    first_loads, later_loads = loads[:7], loads[7:]

    lane = lax.broadcasted_iota(jnp.int32, (1, 1, 1, LANES), 3)
    lane3 = lax.broadcasted_iota(jnp.int32, (1, 1, LANES), 2)
    lane2 = lax.broadcasted_iota(jnp.int32, (1, LANES), 1)
    z2 = lax.rem(lane2, EZ)

    def roll(value, shift):
        shift = shift % LANES
        return value if shift == 0 else pltpu.roll(value, shift, value.ndim - 1)

    for load in first_loads:
        load.wait()
    for dim in range(3):
        for ex in range(EX):
            geom_ref[2 * dim + ex : 2 * dim + ex + 1] = jnp.concatenate(
                [lengths_ref[dim, ex, ey : ey + 1] for ey in range(EY)], axis=1
            )
    geom_ref[6:8] = jnp.ones((2, LANES), jnp.float32)
    forces = []
    for ex in range(EX):
        element = disc_ref[ex].astype(jnp.float32) * thrust_ref[ex]
        forces.append(
            jnp.concatenate([element[ey : ey + 1] for ey in range(EY)], axis=1)
        )
    column = lax.rem(lane2, XCOLS)
    for first in range(0, levels, LANES // XCOLS):
        chosen = [0] * 4 if first == 0 else range(first - 3, first + 1)
        count = None
        for place, level in enumerate(chosen):
            one = jnp.broadcast_to(count_ref[level : level + 1], (1, LANES))
            count = one if count is None else jnp.where(lane2 >= XCOLS * place, one, count)
        at = slice(first // 4 * LANES, (first // 4 + 1) * LANES)
        live_ref[:, at] = (column < count).astype(jnp.float32)
    lam_i = tab_ref[0:8]
    lam_j = tab_ref[8:16]
    w_node = tab_ref[16:24]
    edge = tab_ref[24:32]
    lam_k = tab_ref[32]
    w_c = tab_ref[33]
    zmask = tab_ref[34]
    free = tab_ref[35]
    w_end = float(weights[0])
    k_end = float(stiff[0, 0])
    weight_ref[...] = (w_node[:, None] * w_node[None] * w_c[None, None]).reshape(8, 64, LANES)
    winv_ref[...] = (edge[:, None] * edge[None] * zmask[None, None]).reshape(8, 64, LANES)

    def metrics(hx, hy, hz):
        return hy * hz / (2.0 * hx), hx * hz / (2.0 * hy), hx * hy / (2.0 * hz)

    for half in range(2):
        at = slice(half * LANES, (half + 1) * LANES)
        w_ref[half] = source_ref[:, at].reshape(8, 64, LANES)
    by_node = exact_rows(
        jnp.concatenate(
            [
                jnp.concatenate(
                    [w_ref[half, a, pl.ds(k, 8, stride=8)] for half in range(2)], axis=1
                )
                for k in range(EX * EY)
                for a in range(NODES)
            ],
            axis=0,
        ),
        perm_ref[2],
    )
    for ex in range(EX):
        for c in range(NODES):
            at = slice(c // 4 * LANES, (c // 4 + 1) * LANES)
            joined = None
            for ey in range(EY):
                first = (ex * EY + ey) * 64
                part = roll(by_node[first : first + 64, at], EZ * (ey - c % 4))
                joined = part if ey == 0 else jnp.where(lane2 >= EZ * ey, part, joined)
            for a in range(NODES):
                u_ref[ex, a, pl.ds(c, 8, stride=8)] = joined[8 * a : 8 * a + 8]

    for ex in range(EX):
        hx = geom_ref[ex : ex + 1]
        hy = geom_ref[2 + ex : 3 + ex]
        hz = geom_ref[4 + ex : 5 + ex]
        ax, ay, az = metrics(hx, hy, hz)
        in_x = lam_i * ax[None]
        in_y = lam_j * ay[None]
        in_z = lam_k * az
        spectrum = (in_x[:, None] + in_y[None] + in_z[None, None]).reshape(8, 64, LANES)
        shift = shift_ratio * (ax + ay + az)
        lam_ref[ex] = spectrum
        inv_ref[ex] = 1.0 / (spectrum + shift[None])
        mass = (hx * hy * hz / 8.0)[None] * weight_ref[...]
        u_ref[ex] = mass * (u_ref[ex] + forces[ex][None])

    def free_scaled(value):
        return (value.reshape(8, 8, 8, LANES) * free[None, None]).reshape(8, 64, LANES)

    for ex in range(EX):
        u_ref[ex] = free_scaled(u_ref[ex])

    pl.semaphore_wait(barrier, len(everyone))

    geom_copies = []
    for index, target in enumerate(targets):
        copy = pltpu.make_async_remote_copy(
            src_ref=geom_ref,
            dst_ref=recv_g.at[index],
            send_sem=g_send_sem.at[index],
            recv_sem=g_recv_sem.at[index],
            device_id=target,
            device_id_type=MESH,
        )
        copy.start()
        geom_copies.append(copy)

    def own_pairs(ref):
        shared = ref[0, 7] + ref[1, 0]
        ref[0, 7] = shared
        ref[1, 0] = shared
        low = ref[:, :, 0:8]
        high = ref[:, :, 56:64]
        ref[:, :, 0:8] = low + jnp.where(lane >= EZ, roll(high, EZ), 0.0)
        ref[:, :, 56:64] = high + jnp.where(lane < LANES - EZ, roll(low, -EZ), 0.0)
        for ex in range(EX):
            for a in range(NODES):
                low = ref[ex, a, pl.ds(0, 8, stride=8)]
                high = ref[ex, a, pl.ds(7, 8, stride=8)]
                ref[ex, a, pl.ds(0, 8, stride=8)] = low + jnp.where(
                    z2 > 0, roll(high, 1), 0.0
                )
                ref[ex, a, pl.ds(7, 8, stride=8)] = high + jnp.where(
                    z2 < EZ - 1, roll(low, -1), 0.0
                )

    def packed_y(down_faces, up_faces):
        return jnp.where(
            lane3 < EZ,
            down_faces[0],
            jnp.where(
                lane3 < 2 * EZ,
                roll(down_faces[1], EZ),
                jnp.where(lane3 < 3 * EZ, roll(up_faces[0], -EZ), up_faces[1]),
            ),
        )

    def y_faces():
        return packed_y(
            [u_ref[ex, :, 0:8] for ex in range(EX)], [u_ref[ex, :, 56:64] for ex in range(EX)]
        )

    def weighted(parts, row):
        total = None
        for index, part in parts:
            term = part * float(stiff[row, index])
            total = term if total is None else total + term
        return total

    def send_faces(slot, planes):
        send_x[slot, 0, 0] = u_ref[0, 0]
        send_x[slot, 1, 0] = u_ref[1, 7]
        send_y[slot, 0] = y_faces()
        corners = (
            (u_ref[0, 0, 0:8], 0),
            (u_ref[1, 7, 56:64], EY - 1),
            (u_ref[0, 0, 56:64], EY - 1),
            (u_ref[1, 7, 0:8], 0),
        )
        lines = [roll(value, -EZ * ey) for value, ey in corners]
        if planes > 1:
            low = weighted([(a, u_ref[0, a]) for a in range(1, NODES)], 0)
            high = weighted([(a, u_ref[1, a]) for a in range(NODES - 1)], 7)
            send_x[slot, 0, 1] = low
            send_x[slot, 1, 1] = high
            down_normal, up_normal = [], []
            for ex in range(EX):
                rows = [u_ref[ex, :, 8 * b : 8 * b + 8] for b in range(NODES)]
                down_normal.append(weighted([(b, rows[b]) for b in range(1, NODES)], 0))
                up_normal.append(weighted([(b, rows[b]) for b in range(NODES - 1)], 7))
            normal = packed_y(down_normal, up_normal)
            send_y[slot, 1] = normal
            along_x = (low[0:8], high[56:64], low[56:64], high[0:8])
            along_y = ((normal[0], 0), (normal[7], 3), (normal[0], 2), (normal[7], 1))
            lines = [
                jnp.where(
                    lane2 < EZ,
                    lines[i],
                    jnp.where(
                        lane2 < 2 * EZ,
                        roll(along_x[i], EZ * (1 - corners[i][1])),
                        roll(along_y[i][0], EZ * (2 - along_y[i][1])),
                    ),
                )
                for i in range(4)
            ]
        for i in range(4):
            send_c[slot, i] = lines[i]
        pairs = (
            [
                (send_x.at[slot, i, pl.ds(0, planes)], recv_x.at[slot, i, pl.ds(0, planes)])
                for i in range(2)
            ]
            + [
                (send_y.at[slot, pl.ds(0, planes)], recv_y.at[slot, i, pl.ds(0, planes)])
                for i in range(2)
            ]
            + [(send_c.at[slot, i], recv_c.at[slot, i]) for i in range(4)]
        )
        copies = []
        for index in (4, 5, 6, 7, 0, 1, 2, 3):
            source, landing = pairs[index]
            copy = pltpu.make_async_remote_copy(
                src_ref=source,
                dst_ref=landing,
                send_sem=send_sem.at[slot, index],
                recv_sem=recv_sem.at[slot, index],
                device_id=targets[index],
                device_id_type=MESH,
            )
            copy.start()
            copies.append(copy)
        return copies

    def receive_faces(slot, copies):
        for copy in copies:
            copy.wait()
        u_ref[1, 7] += recv_x[slot, FROM_RIGHT, 0]
        u_ref[0, 0] += recv_x[slot, FROM_LEFT, 0]
        add_y(u_ref, arrived_y(slot, 0))
        for index, (ex, a, first, to_ey) in enumerate(
            ((1, 7, 56, EY - 1), (0, 0, 0, 0), (1, 7, 0, 0), (0, 0, 56, EY - 1))
        ):
            u_ref[ex, a, first : first + 8] += in_slot(
                roll(recv_c[slot, index], EZ * to_ey), to_ey
            )

    def arrived_y(slot, plane):
        from_up = recv_y[slot, FROM_UP - 2, plane]
        from_down = recv_y[slot, FROM_DOWN - 2, plane]
        return roll(jnp.where(lane3 >= 2 * EZ, from_down, from_up), 2 * EZ)

    def add_y(ref, plane):
        for ex in range(EX):
            ref[ex, :, 0:8] += jnp.where(lane3 < EZ, roll(plane, -EZ * ex), 0.0)
            ref[ex, :, 56:64] += jnp.where(
                lane3 >= 3 * EZ, roll(plane, EZ * (1 - ex)), 0.0
            )

    def in_slot(value, slot):
        return jnp.where((lane2 >= EZ * slot) & (lane2 < EZ * (slot + 1)), value, 0.0)

    def outer_terms(slot):
        face = jnp.concatenate(
            [u_ref[0, 0], u_ref[1, 7], y_faces().reshape(64, LANES)], axis=1
        )
        from_left_down = recv_c[slot, FROM_LEFT_DOWN - 4]
        from_left_up = recv_c[slot, FROM_LEFT_UP - 4]
        from_right_down = recv_c[slot, FROM_RIGHT_DOWN - 4]
        from_right_up = recv_c[slot, FROM_RIGHT_UP - 4]
        sides = []
        for plane, low, high in (
            (recv_x[slot, FROM_LEFT, 1], from_left_down, from_left_up),
            (recv_x[slot, FROM_RIGHT, 1], from_right_down, from_right_up),
        ):
            sides.append(
                jnp.concatenate(
                    [
                        plane[0:8] + in_slot(roll(low, -EZ), 0),
                        plane[8:56],
                        plane[56:64] + in_slot(roll(high, 2 * EZ), 3),
                    ],
                    axis=0,
                )
            )
        normal_y = arrived_y(slot, 1)
        first = (
            normal_y[0]
            + in_slot(roll(from_left_down, -2 * EZ), 0)
            + in_slot(from_left_up, 2)
        )
        last = (
            normal_y[7]
            + in_slot(roll(from_right_down, -EZ), 1)
            + in_slot(roll(from_right_up, EZ), 3)
        )
        normal_y = jnp.concatenate([first[None], normal_y[1:7], last[None]], axis=0)
        normal = jnp.concatenate([sides[0], sides[1], normal_y.reshape(64, LANES)], axis=1)
        weight = weight_ref[0] * (1.0 / w_end)
        weight = jnp.concatenate([weight] * 3, axis=1)
        odd_ex = lax.rem(lax.div(lane2, EZ), 2) == 1
        arrived = y_faces() - send_y[slot, 0]
        arrived = jnp.concatenate(
            [
                jnp.where(odd_ex, arrived[0], 0.0)[None],
                arrived[1:7],
                jnp.where(odd_ex, 0.0, arrived[7])[None],
            ],
            axis=0,
        )
        arrived = jnp.concatenate(
            [
                u_ref[0, 0] - send_x[slot, 0, 0],
                u_ref[1, 7] - send_x[slot, 1, 0],
                arrived.reshape(64, LANES),
            ],
            axis=1,
        )
        modes = small_product(
            0, jnp.concatenate([weight * face, weight * arrived], axis=1)
        )
        width = 3 * LANES
        modes = face_lam[...] * modes[:, :width] + own_lam[...] * modes[:, width:]
        spread = small_product(1, modes)
        inward = own_normal[...] * arrived
        result = face_normal[...] * (normal + k_end * face) + w_end * weight * spread
        lines = []
        for side in range(2):
            plane = face[:, side * LANES : (side + 1) * LANES]
            value = jnp.where(lane2 < 2 * EZ, plane[0:8], plane[56:64])
            along_x = jnp.where(lane2 < 2 * EZ, sides[side][0:8], sides[side][56:64])
            edge_y = last if side else first
            along_y = jnp.where(
                lane2 < 2 * EZ,
                roll(edge_y, -EZ) if side else edge_y,
                edge_y if side else roll(edge_y, EZ),
            )
            along_z = None
            for c in range(NODES):
                term = tab_ref[38 + c] * value[c : c + 1]
                along_z = term if along_z is None else along_z + term
            lines.append(
                line_tab[side, 0] * (along_x + k_end * value)
                + line_tab[side, 1] * (along_y + k_end * value)
                + line_tab[side, 2] * along_z
            )
        return result, lines, inward

    def add_outer(result, lines, inward):
        inward_y = inward[:, 2 * LANES :].reshape(8, 8, LANES)
        for ex in range(EX):
            inward_x = inward[:, ex * LANES : (ex + 1) * LANES]
            along = jnp.where(
                lane3 < EZ,
                roll(inward_y, -EZ * ex),
                jnp.where(lane3 >= 3 * EZ, roll(inward_y, EZ * (1 - ex)), 0.0),
            )
            for a in range(NODES):
                terms = (along[a][None] * tab_ref[46:54]).reshape(64, LANES)
                w_ref[ex, a] += terms + inward_x * float(stiff[a, 7 * ex])
        for side, (ex, a) in enumerate(((0, 0), (1, 7))):
            w_ref[ex, a] += result[:, side * LANES : (side + 1) * LANES]
            w_ref[ex, a, 0:8] += in_slot(lines[side], 0)
            w_ref[ex, a, 56:64] += in_slot(lines[side], 3)
        add_y(w_ref, result[:, 2 * LANES :].reshape(8, 8, LANES))

    def small_product(which, value):
        high = value.astype(jnp.bfloat16)
        low = (value - high.astype(jnp.float32)).astype(jnp.bfloat16)
        return jnp.dot(
            plane_ref[which],
            jnp.concatenate([high, low, high], axis=0),
            preferred_element_type=jnp.float32,
        )

    def product(which, value):
        high = value.astype(jnp.bfloat16)
        low = (value - high.astype(jnp.float32)).astype(jnp.bfloat16)
        return jnp.dot(
            mat_ref[which],
            jnp.concatenate([high, low, high], axis=0),
            preferred_element_type=jnp.float32,
        )

    def flat(parts):
        return jnp.concatenate([part.reshape(256, LANES) for part in parts], axis=1)

    def element_op(fields, diag_ref):
        even, odd = [], []
        for field in fields:
            low = field[0:4]
            high = jnp.concatenate([field[7:8], field[6:7], field[5:6], field[4:5]], axis=0)
            even.append(low + high)
            odd.append(low - high)
        even = product(0, flat(even)) * flat([diag_ref[ex, 0:4] for ex in range(EX)])
        odd = product(1, flat(odd)) * flat([diag_ref[ex, 4:8] for ex in range(EX)])
        even = product(2, even)
        odd = product(3, odd)
        out = []
        for ex in range(EX):
            at = slice(ex * LANES, (ex + 1) * LANES)
            e = even[:, at].reshape(4, 64, LANES)
            o = odd[:, at].reshape(4, 64, LANES)
            diff = e - o
            out.append(
                jnp.concatenate([e + o, diff[3:4], diff[2:3], diff[1:2], diff[0:1]], axis=0)
            )
        return out

    def stiffness():
        weight = weight_ref[...]
        out = element_op([u_ref[ex] * weight for ex in range(EX)], lam_ref)
        for ex in range(EX):
            w_ref[ex] = out[ex] * weight

    def smoother(keep, take):
        out = element_op([r_ref[ex] for ex in range(EX)], inv_ref)
        for ex in range(EX):
            u_ref[ex] = (take * out[ex] + keep * u_ref[ex]) * winv_ref[...]

    wide = (levels - 1) * XCOLS
    gy_bits = n_gy.bit_length() - 1
    split = gy_bits * XCOLS

    def exchange(cycle, send_ref, recv_ref, to, send_s, recv_s):
        copies = []
        for index, target in enumerate(to):
            copy = pltpu.make_async_remote_copy(
                src_ref=send_ref,
                dst_ref=recv_ref.at[cycle, index],
                send_sem=send_s.at[index],
                recv_sem=recv_s.at[cycle, index],
                device_id=target,
                device_id_type=MESH,
            )
            copy.start()
            copies.append(copy)
        for copy in copies:
            copy.wait()

    def level_sum(own, recv_ref, cycle, count, first_level_lane):
        which = lax.broadcasted_iota(jnp.int32, own.shape, 1)
        total = own
        start = 1
        bit = 0
        while start < count:
            part = recv_ref[cycle, start - 1]
            for index in range(start + 1, 2 * start):
                part = part + recv_ref[cycle, index - 1]
            total = total + jnp.where(which >= bit * XCOLS + first_level_lane, part, 0.0)
            start *= 2
            bit += 1
        return total

    def coarse(cycle):
        sums = {}
        for ex in range(EX):
            scaled = r_ref[ex] * winv_ref[...]
            for v in range(2):
                by_v = scaled[0] * float(interp[0, v])
                for a in range(1, NODES):
                    by_v = by_v + scaled[a] * float(interp[a, v])
                by_v = by_v.reshape(8, 8, LANES)
                for u in range(2):
                    by_u = by_v[0] * float(interp[0, u])
                    for b in range(1, NODES):
                        by_u = by_u + by_v[b] * float(interp[b, u])
                    for t in range(2):
                        sums[v, u, ex, t] = jnp.sum(
                            by_u * tab_ref[36 + t], axis=0, keepdims=True
                        )
        order = [(v, u, ex) for v in range(2) for u in range(2) for ex in range(EX)]
        split_t = jnp.concatenate(
            [jnp.concatenate([sums[key + (t,)] for t in range(2)], axis=1) for key in order],
            axis=0,
        )
        vector = exact_rows(split_t, perm_ref[0])
        pieces = []
        for level in range(levels):
            rows = slice(level * XCOLS, (level + 1) * XCOLS)
            acc = None
            for q in range(8):
                term = x_factor_ref[rows, q * 256 : (q + 1) * 256] * vector[q : q + 1]
                acc = term if acc is None else acc + term
            pieces.append(acc[:, :LANES] + acc[:, LANES:])
        def row_of(parts):
            block = jnp.concatenate(parts, axis=0)
            missing = LANES - block.shape[0]
            if missing:
                block = jnp.concatenate([block, jnp.zeros((missing, LANES), jnp.float32)], axis=0)
            return jnp.sum(block.T, axis=0, keepdims=True)
        own = row_of(pieces[0:1])
        upper = jnp.concatenate(
            [row_of(pieces[i : i + 4]) for i in range(1, levels, 4)], axis=1
        )[:, :wide]
        send_one[...] = upper
        exchange(cycle, send_one, recv_one, one_targets, one_send_sem, one_recv_sem)
        upper = level_sum(upper, recv_one, cycle, n_gy, 0)
        send_two[...] = upper[:, split:]
        exchange(cycle, send_two, recv_two, two_targets, two_send_sem, two_recv_sem)
        top = level_sum(upper[:, split:], recv_two, cycle, n_gx, 0)
        upper = jnp.concatenate([upper[:, :split], top], axis=1)
        own = own * live_ref[:, 0:LANES]
        upper = upper * live_ref[:, LANES : LANES + wide]
        tail = (-wide) % LANES
        if tail:
            upper = jnp.concatenate([upper, jnp.zeros((1, tail), jnp.float32)], axis=1)
        cols = [jnp.broadcast_to(own, (LANES, LANES)).T[:XCOLS]]
        for first in range(0, wide, LANES):
            part = jnp.broadcast_to(upper[:, first : first + LANES], (LANES, LANES)).T
            cols += [part[k * XCOLS : (k + 1) * XCOLS] for k in range(LANES // XCOLS)]
        back = []
        for q in range(8):
            acc = None
            for level in range(levels):
                block = x_factor_ref[
                    level * XCOLS : (level + 1) * XCOLS, q * 256 : (q + 1) * 256
                ]
                col = cols[level]
                term = block * jnp.concatenate([col, col], axis=1)
                acc = term if acc is None else acc + term
            back.append(jnp.sum(acc, axis=0, keepdims=True))
        split_t = exact_rows(jnp.concatenate(back, axis=0), perm_ref[1])
        for ex in range(EX):
            by_v = []
            for v in range(2):
                by_u = []
                for u in range(2):
                    q = (v * 2 + u) * EX + ex
                    by_u.append(
                        split_t[q : q + 1, :LANES] * tab_ref[36]
                        + split_t[q : q + 1, LANES:] * tab_ref[37]
                    )
                by_v.append(
                    jnp.concatenate(
                        [
                            by_u[0] * float(interp[b, 0]) + by_u[1] * float(interp[b, 1])
                            for b in range(NODES)
                        ],
                        axis=0,
                    )
                )
            for a in range(NODES):
                u_ref[ex, a] = winv_ref[a] * (
                    by_v[0] * float(interp[a, 0]) + by_v[1] * float(interp[a, 1])
                )

    center = 0.5 * (bound_high + bound_low)
    radius = 0.5 * (bound_high - bound_low)
    ratio = center / radius
    rho_old = 1.0 / ratio
    rho_new = 1.0 / (2.0 * ratio - rho_old)

    own_pairs(u_ref)
    receive_faces(1, send_faces(1, 1))
    r_ref[...] = u_ref[...]
    x_ref[...] = jnp.zeros_like(x_ref)

    for copy in geom_copies:
        copy.wait()
    slots = lambda values: jnp.where(
        lane2 < EZ,
        values[0],
        jnp.where(lane2 < 2 * EZ, values[1], jnp.where(lane2 < 3 * EZ, values[2], values[3])),
    )

    def ghost(source, dim, ex):
        return recv_g[source, 2 * dim + ex : 2 * dim + ex + 1]

    outer = []
    for dim in range(3):
        y_side = slots(
            [
                roll(ghost(FROM_DOWN, dim, 0), EZ),
                roll(ghost(FROM_DOWN, dim, 1), 2 * EZ),
                roll(ghost(FROM_UP, dim, 0), 2 * EZ),
                roll(ghost(FROM_UP, dim, 1), 3 * EZ),
            ]
        )
        outer.append([ghost(FROM_LEFT, dim, 1), ghost(FROM_RIGHT, dim, 0), y_side])
    for part in range(3):
        ax, ay, az = metrics(*[outer[dim][part] for dim in range(3)])
        at = slice(part * LANES, (part + 1) * LANES)
        normal, along = (ay, ax) if part == 2 else (ax, ay)
        face_lam[:, at] = ((lam_j * along[None]) + (lam_k * az)[None]).reshape(64, LANES)
        face_normal[:, at] = (w_node * w_c[None] * normal[None]).reshape(64, LANES)
    own = []
    for dim in range(3):
        low, high = (geom_ref[2 * dim + ex : 2 * dim + ex + 1] for ex in range(EX))
        own.append([low, high, slots([low, roll(high, EZ), roll(low, -EZ), high])])
    for part in range(3):
        ax, ay, az = metrics(*[own[dim][part] for dim in range(3)])
        at = slice(part * LANES, (part + 1) * LANES)
        normal, along = (ay, ax) if part == 2 else (ax, ay)
        own_lam[:, at] = ((lam_j * along[None]) + (lam_k * az)[None]).reshape(64, LANES)
        own_normal[:, at] = (w_node * w_c[None] * normal[None]).reshape(64, LANES)
    for side, (low, high, ex) in enumerate(
        ((FROM_LEFT_DOWN, FROM_LEFT_UP, 1), (FROM_RIGHT_DOWN, FROM_RIGHT_UP, 0))
    ):
        lengths = [
            jnp.where(
                lane2 < 2 * EZ,
                roll(ghost(low, dim, ex), EZ),
                roll(ghost(high, dim, ex), -EZ),
            )
            for dim in range(3)
        ]
        ax, ay, az = metrics(*lengths)
        line_tab[side, 0] = w_end * w_c * ax
        line_tab[side, 1] = w_end * w_c * ay
        line_tab[side, 2] = jnp.broadcast_to(w_end * w_end * az, (8, LANES))

    for load in later_loads:
        load.wait()

    def step(index, carry):
        phase = lax.rem(index, SMOOTH)
        cycle = lax.div(index, SMOOTH)
        slot = lax.rem(index, 2)
        is_coarse = phase == 2
        second = (phase == 1) | (phase == 4)

        @pl.when(is_coarse)
        def _():
            coarse(cycle)

        @pl.when(jnp.logical_not(is_coarse))
        def _():
            keep = jnp.where(second, rho_new * rho_old, 0.0)
            take = jnp.where(second, 2.0 * rho_new / radius, 1.0 / center)
            smoother(keep, take)

        own_pairs(u_ref)
        copies = send_faces(slot, 2)

        @pl.when(index < SMOOTH * CYCLES - 1)
        def _():
            stiffness()

        receive_faces(slot, copies)
        for ex in range(EX):
            x_ref[ex] += u_ref[ex]

        @pl.when(index < SMOOTH * CYCLES - 1)
        def _():
            add_outer(*outer_terms(slot))
            own_pairs(w_ref)
            for ex in range(EX):
                r_ref[ex] -= free_scaled(w_ref[ex])

        return carry

    lax.fori_loop(0, SMOOTH * CYCLES, step, 0)

    by_node = [
        [
            jnp.concatenate(
                [x_ref[ex, a, pl.ds(c, 8, stride=8)] for a in range(NODES)], axis=0
            )
            for c in range(NODES)
        ]
        for ex in range(EX)
    ]
    rows = []
    for ex in range(EX):
        for ey in range(EY):
            halves = []
            for half in range(2):
                joined = None
                for s in range(4):
                    part = roll(by_node[ex][half * 4 + s], EZ * (s - ey))
                    joined = part if s == 0 else jnp.where(lane2 >= EZ * s, part, joined)
                halves.append(joined)
            rows.append(jnp.concatenate(halves, axis=1))
    result = exact_rows(jnp.concatenate(rows, axis=0), perm_ref[3])
    for half in range(2):
        at = slice(half * LANES, (half + 1) * LANES)
        for k in range(EX * EY):
            for a in range(NODES):
                first = k * 64 + a * 8
                w_ref[half, a, pl.ds(k, 8, stride=8)] = result[first : first + 8, at]
    for half in range(2):
        at = slice(half * LANES, (half + 1) * LANES)
        out_ref[:, at] = w_ref[half].reshape(512, LANES)


def per_device(source, geometry, disc_mask, thrust, xxt_factor, col_count):
    n_gx = lax.axis_size("gx")
    n_gy = lax.axis_size("gy")
    levels = xxt_factor.shape[0]
    wide = (levels - 1) * XCOLS
    split = (n_gy.bit_length() - 1) * XCOLS
    matrices, plane, table, perms, interp, stiff, weights = constant_tables()
    field = (EX, NODES, 64, LANES)
    f32 = jnp.float32
    out = pl.pallas_call(
        functools.partial(kernel, n_gx, n_gy, levels, interp, stiff, weights),
        out_shape=jax.ShapeDtypeStruct((512, 256), f32),
        in_specs=[pl.BlockSpec(memory_space=pl.ANY)] * 10,
        out_specs=pl.BlockSpec(memory_space=pltpu.VMEM),
        scratch_shapes=[
            pltpu.VMEM((NODES * NODES * EX * EY, EZ * NODES), f32),
            pltpu.VMEM(geometry.shape, f32),
            pltpu.VMEM(disc_mask.shape, jnp.int32),
            pltpu.VMEM(thrust.shape, f32),
            pltpu.VMEM(col_count.shape, jnp.int32),
            pltpu.VMEM(plane.shape, jnp.bfloat16),
            pltpu.VMEM(table.shape, f32),
            pltpu.VMEM(perms.shape, jnp.bfloat16),
            pltpu.VMEM((8, LANES), f32),
            pltpu.VMEM((1, LANES + wide), f32),
            pltpu.VMEM(field, f32),
            pltpu.VMEM(field, f32),
            pltpu.VMEM(field, f32),
            pltpu.VMEM(field, f32),
            pltpu.VMEM(field[1:], f32),
            pltpu.VMEM(field[1:], f32),
            pltpu.VMEM(field, f32),
            pltpu.VMEM(field, f32),
            pltpu.VMEM((64, 3 * LANES), f32),
            pltpu.VMEM((64, 3 * LANES), f32),
            pltpu.VMEM((64, 3 * LANES), f32),
            pltpu.VMEM((64, 3 * LANES), f32),
            pltpu.VMEM((2, 3, 8, LANES), f32),
            pltpu.VMEM((levels * XCOLS, xxt_factor.shape[2]), f32),
            pltpu.VMEM(matrices.shape, jnp.bfloat16),
            pltpu.VMEM((2, 2, 2, 64, LANES), f32),
            pltpu.VMEM((2, 2, 8, 8, LANES), f32),
            pltpu.VMEM((2, 4, 8, LANES), f32),
            pltpu.VMEM((2, 2, 2, 64, LANES), f32),
            pltpu.VMEM((2, 2, 2, 8, 8, LANES), f32),
            pltpu.VMEM((2, 4, 8, LANES), f32),
            pltpu.VMEM((8, 8, LANES), f32),
            pltpu.VMEM((1, wide), f32),
            pltpu.VMEM((CYCLES, n_gy - 1, 1, wide), f32),
            pltpu.VMEM((1, wide - split), f32),
            pltpu.VMEM((CYCLES, n_gx - 1, 1, wide - split), f32),
            pltpu.SemaphoreType.DMA((2, 8)),
            pltpu.SemaphoreType.DMA((2, 8)),
            pltpu.SemaphoreType.DMA((8,)),
            pltpu.SemaphoreType.DMA((8,)),
            pltpu.SemaphoreType.DMA((n_gy - 1,)),
            pltpu.SemaphoreType.DMA((CYCLES, n_gy - 1)),
            pltpu.SemaphoreType.DMA((n_gx - 1,)),
            pltpu.SemaphoreType.DMA((CYCLES, n_gx - 1)),
            pltpu.SemaphoreType.DMA((10,)),
        ],
        compiler_params=pltpu.CompilerParams(
            collective_id=0, has_side_effects=True, vmem_limit_bytes=56 * 1024 * 1024
        ),
    )(
        source.reshape(NODES * NODES * EX * EY, EZ * NODES),
        geometry,
        disc_mask,
        thrust,
        col_count,
        xxt_factor.reshape(levels * XCOLS, xxt_factor.shape[2]),
        jnp.asarray(matrices),
        jnp.asarray(plane),
        jnp.asarray(table),
        jnp.asarray(perms),
    )
    return out.reshape(source.shape)


def solution(mesh):
    return jax.shard_map(
        per_device,
        mesh=mesh,
        in_specs=(
            P(None, None, "gx", "gy", None),
            P(None, "gx", "gy", None),
            P("gx", "gy", None),
            P("gx", "gy", None),
            P(None, None, ("gx", "gy")),
            P(None, ("gx", "gy")),
        ),
        out_specs=P(None, None, "gx", "gy", None),
        check_vma=False,
    )
```

```python
import functools
import math

import jax
import jax.numpy as jnp
import ml_dtypes
import numpy as np
from jax import lax
from jax.experimental import pallas as pl
from jax.experimental.pallas import tpu as pltpu
from jax.sharding import PartitionSpec as P

NODES = 8
CYCLES = 2
EX = 2
EY = 4
EZ = 32
LANES = EY * EZ
XCOLS = 32
SMOOTH = 5

bound_low = 0.3
bound_high = 3.0
shift_ratio = 0.25
MESH = pl.DeviceIdType.MESH


def legendre_table(points, poly_order):
    table = [points * 0.0 + 1.0, points]
    for degree in range(2, poly_order + 1):
        table.append(
            ((2.0 * degree - 1.0) * points * table[-1] - (degree - 1.0) * table[-2]) / degree
        )
    return table


def jacobi_eigen(matrix):
    size_n = matrix.shape[0]
    current = matrix.copy()
    vectors = np.eye(size_n)
    for sweep_index in range(30):
        for first in range(size_n - 1):
            for second in range(first + 1, size_n):
                angle = 0.5 * math.atan2(
                    2.0 * float(current[first, second]),
                    float(current[second, second] - current[first, first]),
                )
                rotation = np.eye(size_n)
                rotation[first, first] = math.cos(angle)
                rotation[second, second] = math.cos(angle)
                rotation[first, second] = math.sin(angle)
                rotation[second, first] = -math.sin(angle)
                current = rotation.T @ current @ rotation
                vectors = vectors @ rotation
    values = np.array([current[index, index] for index in range(size_n)])
    order = np.argsort(values)
    return (values[order], vectors[:, order])


def gll_tables(node_count):
    poly_order = node_count - 1
    points = np.cos(np.pi * np.arange(node_count) / poly_order)
    for newton_index in range(200):
        table = legendre_table(points, poly_order)
        points = points - (points * table[poly_order] - table[poly_order - 1]) / (
            node_count * table[poly_order]
        )
    points = points[::-1].copy()
    legendre = legendre_table(points, poly_order)[poly_order]
    weights = 2.0 / (poly_order * (poly_order + 1) * legendre**2)
    identity = np.eye(node_count)
    gap_matrix = points[:, None] - points[None, :] + identity
    off_diagonal = legendre[:, None] / (legendre[None, :] * gap_matrix) * (1.0 - identity)
    end_value = poly_order * (poly_order + 1) / 4.0
    end_terms = np.concatenate([[-end_value], np.zeros(node_count - 2), [end_value]])
    derivative = off_diagonal + identity * end_terms[None, :]
    stiffness = derivative.T @ (weights[:, None] * derivative)
    root_inverse = 1.0 / np.sqrt(weights)
    symmetric = root_inverse[:, None] * stiffness * root_inverse[None, :]
    symmetric = 0.5 * (symmetric + symmetric.T)
    eigen_values, eigen_vectors = jacobi_eigen(symmetric)
    eigen_modes = root_inverse[:, None] * eigen_vectors
    vertex_interp = np.stack([(1.0 - points) / 2.0, (1.0 + points) / 2.0], axis=1)
    return weights, stiffness, eigen_modes, eigen_values, vertex_interp


def mode_order(modes):
    even = [i for i in range(NODES) if modes[0, i] * modes[NODES - 1, i] > 0.0]
    odd = [i for i in range(NODES) if i not in even]
    return even, odd


def split_pair(matrix):
    exact = matrix.astype(np.float32)
    high = exact.astype(ml_dtypes.bfloat16)
    low = (exact - high.astype(np.float32)).astype(ml_dtypes.bfloat16)
    return np.concatenate([high, high, low], axis=1)


def constant_tables():
    weights, stiffness, modes, values, interp = gll_tables(NODES)
    even, odd = mode_order(modes)
    half = NODES // 2
    mats = []
    for chosen in (even, odd):
        inverse = np.kron(modes[:half][:, chosen], np.kron(modes, modes))
        mats.append((split_pair(inverse.T), split_pair(inverse)))
    matrices = np.stack([mats[0][0], mats[1][0], mats[0][1], mats[1][1]])
    plane = np.kron(modes, modes)
    plane_matrices = np.stack([split_pair(plane.T), split_pair(plane)])
    full = np.ones((NODES, LANES))
    edge = np.ones(NODES)
    edge[0] = edge[-1] = 0.5
    ez = np.arange(LANES)[None, :] % EZ
    node = np.arange(NODES)[:, None]
    z_shared = 1.0 + ((node == 0) & (ez > 0)) + ((node == NODES - 1) & (ez < EZ - 1))
    free = 1.0 - ((node == NODES - 1) & (ez == EZ - 1))
    rows = [values[i] * full for i in even + odd]
    rows += [value * full for value in values]
    rows += [weight * full for weight in weights]
    rows += [value * full for value in edge]
    rows += [values[:, None] * full, weights[:, None] * full, free / z_shared, free * full]
    rows += [interp[:, 0:1] * full, interp[:, 1:2] * full]
    rows += [stiffness[:, c : c + 1] * full for c in range(NODES)]
    low_side = np.arange(LANES)[None, :] < LANES // 2
    rows += [
        np.where(low_side, stiffness[b, 0], stiffness[b, NODES - 1]) * full for b in range(NODES)
    ]
    table = np.stack(rows).astype(np.float32)
    perm = np.zeros((2 * LANES, 2 * LANES), np.float32)
    for t in range(2):
        for element in range(LANES):
            perm[t * LANES + element, 2 * element + t] = 1.0
    order = np.zeros((EZ * NODES, EZ * NODES), np.float32)
    for c in range(NODES):
        for element in range(EZ):
            order[element * NODES + c, c * EZ + element] = 1.0
    perms = np.stack([perm, perm.T, order, order.T]).astype(ml_dtypes.bfloat16)
    return (
        matrices,
        plane_matrices,
        table,
        perms,
        interp.astype(np.float32),
        stiffness.astype(np.float32),
        weights.astype(np.float32),
    )


def flipped(index, bits):
    out = index
    bit = 1
    while bit <= bits:
        if bits & bit:
            out = out + bit - 2 * bit * lax.rem(lax.div(index, bit), 2)
        bit *= 2
    return out


def exact_rows(value, perm):
    first = value.astype(jnp.bfloat16)
    rest = value - first.astype(jnp.float32)
    second = rest.astype(jnp.bfloat16)
    third = (rest - second.astype(jnp.float32)).astype(jnp.bfloat16)
    parts = [
        jnp.dot(part, perm, preferred_element_type=jnp.float32)
        for part in (first, second, third)
    ]
    return parts[0] + parts[1] + parts[2]


def kernel(
    n_gx,
    n_gy,
    levels,
    interp,
    stiff,
    weights,
    source_hbm,
    lengths_hbm,
    disc_hbm,
    thrust_hbm,
    count_hbm,
    x_hbm,
    mat_hbm,
    plane_hbm,
    tab_hbm,
    perm_hbm,
    out_ref,
    source_ref,
    lengths_ref,
    disc_ref,
    thrust_ref,
    count_ref,
    plane_ref,
    tab_ref,
    perm_ref,
    geom_ref,
    live_ref,
    u_ref,
    r_ref,
    w_ref,
    x_ref,
    weight_ref,
    winv_ref,
    lam_ref,
    inv_ref,
    face_lam,
    face_normal,
    own_lam,
    own_normal,
    line_tab,
    x_factor_ref,
    mat_ref,
    send_x,
    send_y,
    send_c,
    recv_x,
    recv_y,
    recv_c,
    recv_g,
    send_one,
    recv_one,
    send_two,
    recv_two,
    send_sem,
    recv_sem,
    g_send_sem,
    g_recv_sem,
    one_send_sem,
    one_recv_sem,
    two_send_sem,
    two_recv_sem,
    load_sem,
):
    me_x = lax.axis_index("gx")
    me_y = lax.axis_index("gy")
    left = lax.rem(me_x + n_gx - 1, n_gx)
    right = lax.rem(me_x + 1, n_gx)
    down = lax.rem(me_y + n_gy - 1, n_gy)
    up = lax.rem(me_y + 1, n_gy)
    targets = [
        (left, me_y),
        (right, me_y),
        (me_x, down),
        (me_x, up),
        (left, down),
        (right, up),
        (left, up),
        (right, down),
    ]
    FROM_RIGHT, FROM_LEFT, FROM_UP, FROM_DOWN = 0, 1, 2, 3
    FROM_RIGHT_UP, FROM_LEFT_DOWN, FROM_RIGHT_DOWN, FROM_LEFT_UP = 4, 5, 6, 7
    one_targets = [(me_x, flipped(me_y, off)) for off in range(1, n_gy)]
    two_targets = [(flipped(me_x, off), me_y) for off in range(1, n_gx)]
    barrier = pltpu.get_barrier_semaphore()
    everyone = targets + one_targets + two_targets
    for target in everyone:
        pl.semaphore_signal(barrier, inc=1, device_id=target, device_id_type=MESH)
    loads = [
        pltpu.make_async_copy(src, dst, load_sem.at[index])
        for index, (src, dst) in enumerate(
            (
                (tab_hbm, tab_ref),
                (source_hbm, source_ref),
                (perm_hbm, perm_ref),
                (lengths_hbm, lengths_ref),
                (disc_hbm, disc_ref),
                (thrust_hbm, thrust_ref),
                (count_hbm, count_ref),
                (mat_hbm, mat_ref),
                (plane_hbm, plane_ref),
                (x_hbm, x_factor_ref),
            )
        )
    ]
    for load in loads:
        load.start()
    first_loads, later_loads = loads[:7], loads[7:]

    lane = lax.broadcasted_iota(jnp.int32, (1, 1, 1, LANES), 3)
    lane3 = lax.broadcasted_iota(jnp.int32, (1, 1, LANES), 2)
    lane2 = lax.broadcasted_iota(jnp.int32, (1, LANES), 1)
    z2 = lax.rem(lane2, EZ)

    def roll(value, shift):
        shift = shift % LANES
        return value if shift == 0 else pltpu.roll(value, shift, value.ndim - 1)

    for load in first_loads:
        load.wait()
    for dim in range(3):
        for ex in range(EX):
            geom_ref[2 * dim + ex : 2 * dim + ex + 1] = jnp.concatenate(
                [lengths_ref[dim, ex, ey : ey + 1] for ey in range(EY)], axis=1
            )
    geom_ref[6:8] = jnp.ones((2, LANES), jnp.float32)
    forces = []
    for ex in range(EX):
        element = disc_ref[ex].astype(jnp.float32) * thrust_ref[ex]
        forces.append(
            jnp.concatenate([element[ey : ey + 1] for ey in range(EY)], axis=1)
        )
    column = lax.rem(lane2, XCOLS)
    for first in range(0, levels, LANES // XCOLS):
        chosen = [0] * 4 if first == 0 else range(first - 3, first + 1)
        count = None
        for place, level in enumerate(chosen):
            one = jnp.broadcast_to(count_ref[:, level : level + 1], (1, LANES))
            count = one if count is None else jnp.where(lane2 >= XCOLS * place, one, count)
        at = slice(first // 4 * LANES, (first // 4 + 1) * LANES)
        live_ref[:, at] = (column < count).astype(jnp.float32)
    lam_i = tab_ref[0:8]
    lam_j = tab_ref[8:16]
    w_node = tab_ref[16:24]
    edge = tab_ref[24:32]
    lam_k = tab_ref[32]
    w_c = tab_ref[33]
    zmask = tab_ref[34]
    free = tab_ref[35]
    w_end = float(weights[0])
    k_end = float(stiff[0, 0])
    weight_ref[...] = (w_node[:, None] * w_node[None] * w_c[None, None]).reshape(8, 64, LANES)

    def metrics(hx, hy, hz):
        return hy * hz / (2.0 * hx), hx * hz / (2.0 * hy), hx * hy / (2.0 * hz)

    for half in range(2):
        at = slice(half * LANES, (half + 1) * LANES)
        w_ref[half] = source_ref[:, :, at].reshape(8, 64, LANES)
    by_node = exact_rows(
        jnp.concatenate(
            [
                jnp.concatenate(
                    [w_ref[half, a, pl.ds(k, 8, stride=8)] for half in range(2)], axis=1
                )
                for k in range(EX * EY)
                for a in range(NODES)
            ],
            axis=0,
        ),
        perm_ref[2],
    )
    for ex in range(EX):
        for c in range(NODES):
            at = slice(c // 4 * LANES, (c // 4 + 1) * LANES)
            joined = None
            for ey in range(EY):
                first = (ex * EY + ey) * 64
                part = roll(by_node[first : first + 64, at], EZ * (ey - c % 4))
                joined = part if ey == 0 else jnp.where(lane2 >= EZ * ey, part, joined)
            for a in range(NODES):
                u_ref[ex, a, pl.ds(c, 8, stride=8)] = joined[8 * a : 8 * a + 8]

    for ex in range(EX):
        hx = geom_ref[ex : ex + 1]
        hy = geom_ref[2 + ex : 3 + ex]
        hz = geom_ref[4 + ex : 5 + ex]
        mass = (hx * hy * hz / 8.0)[None] * weight_ref[...]
        u_ref[ex] = mass * (u_ref[ex] + forces[ex][None])

    def free_scaled(value):
        return (value.reshape(8, 8, 8, LANES) * free[None, None]).reshape(8, 64, LANES)

    for ex in range(EX):
        u_ref[ex] = free_scaled(u_ref[ex])

    geom_copies = []
    for index, target in enumerate(targets):
        copy = pltpu.make_async_remote_copy(
            src_ref=geom_ref,
            dst_ref=recv_g.at[index],
            send_sem=g_send_sem.at[index],
            recv_sem=g_recv_sem.at[index],
            device_id=target,
            device_id_type=MESH,
        )
        geom_copies.append(copy)

    def own_pairs(ref):
        shared = ref[0, 7] + ref[1, 0]
        ref[0, 7] = shared
        ref[1, 0] = shared
        low = ref[:, :, 0:8]
        high = ref[:, :, 56:64]
        ref[:, :, 0:8] = low + jnp.where(lane >= EZ, roll(high, EZ), 0.0)
        ref[:, :, 56:64] = high + jnp.where(lane < LANES - EZ, roll(low, -EZ), 0.0)
        for ex in range(EX):
            for a in range(NODES):
                low = ref[ex, a, pl.ds(0, 8, stride=8)]
                high = ref[ex, a, pl.ds(7, 8, stride=8)]
                ref[ex, a, pl.ds(0, 8, stride=8)] = low + jnp.where(
                    z2 > 0, roll(high, 1), 0.0
                )
                ref[ex, a, pl.ds(7, 8, stride=8)] = high + jnp.where(
                    z2 < EZ - 1, roll(low, -1), 0.0
                )

    def packed_y(down_faces, up_faces):
        return jnp.where(
            lane3 < EZ,
            down_faces[0],
            jnp.where(
                lane3 < 2 * EZ,
                roll(down_faces[1], EZ),
                jnp.where(lane3 < 3 * EZ, roll(up_faces[0], -EZ), up_faces[1]),
            ),
        )

    def y_faces():
        return packed_y(
            [u_ref[ex, :, 0:8] for ex in range(EX)], [u_ref[ex, :, 56:64] for ex in range(EX)]
        )

    def weighted(parts, row):
        total = None
        for index, part in parts:
            term = part * float(stiff[row, index])
            total = term if total is None else total + term
        return total

    def send_faces(slot, planes):
        copies = [None] * 8

        def start(index, source, landing):
            copies[index] = pltpu.make_async_remote_copy(
                src_ref=source,
                dst_ref=landing,
                send_sem=send_sem.at[slot, index],
                recv_sem=recv_sem.at[slot, index],
                device_id=targets[index],
                device_id_type=MESH,
            )
            copies[index].start()

        corners = ((0, 0, 0), (1, 7, 7), (0, 0, 7), (1, 7, 0))
        if planes > 1:
            low = weighted([(a, u_ref[0, a]) for a in range(1, NODES)], 0)
            high = weighted([(a, u_ref[1, a]) for a in range(NODES - 1)], 7)
        for i, (ex, a, b) in enumerate(corners):
            ey = 0 if b == 0 else EY - 1
            line = roll(u_ref[ex, a, 8 * b : 8 * b + 8], -EZ * ey)
            if planes > 1:
                along_x = (high if ex else low)[8 * b : 8 * b + 8]
                others = [other for other in range(NODES) if other != b]
                along_y = weighted(
                    [(other, u_ref[ex, a, 8 * other : 8 * other + 8]) for other in others], b
                )
                line = jnp.where(
                    lane2 < EZ,
                    line,
                    jnp.where(
                        lane2 < 2 * EZ,
                        roll(along_x, EZ * (1 - ey)),
                        roll(along_y, EZ * (2 - ey)),
                    ),
                )
            send_c[slot, i] = line
        for i in range(4):
            start(4 + i, send_c.at[slot, i], recv_c.at[slot, i])
        send_x[slot, 0, 0] = u_ref[0, 0]
        send_x[slot, 1, 0] = u_ref[1, 7]
        if planes > 1:
            send_x[slot, 0, 1] = low
            send_x[slot, 1, 1] = high
        both = pl.ds(0, planes)
        for i in range(2):
            start(i, send_x.at[slot, i, both], recv_x.at[slot, i, both])
        send_y[slot, 0] = y_faces()
        if planes > 1:
            down_normal, up_normal = [], []
            for ex in range(EX):
                rows = [u_ref[ex, :, 8 * b : 8 * b + 8] for b in range(NODES)]
                down_normal.append(weighted([(b, rows[b]) for b in range(1, NODES)], 0))
                up_normal.append(weighted([(b, rows[b]) for b in range(NODES - 1)], 7))
            send_y[slot, 1] = packed_y(down_normal, up_normal)
        for i in range(2):
            start(2 + i, send_y.at[slot, both], recv_y.at[slot, i, both])
        return copies

    def receive_faces(slot, copies):
        for copy in copies:
            copy.wait()
        u_ref[1, 7] += recv_x[slot, FROM_RIGHT, 0]
        u_ref[0, 0] += recv_x[slot, FROM_LEFT, 0]
        add_y(u_ref, arrived_y(slot, 0))
        for index, (ex, a, first, to_ey) in enumerate(
            ((1, 7, 56, EY - 1), (0, 0, 0, 0), (1, 7, 0, 0), (0, 0, 56, EY - 1))
        ):
            u_ref[ex, a, first : first + 8] += in_slot(
                roll(recv_c[slot, index], EZ * to_ey), to_ey
            )

    def arrived_y(slot, plane):
        from_up = recv_y[slot, FROM_UP - 2, plane]
        from_down = recv_y[slot, FROM_DOWN - 2, plane]
        return roll(jnp.where(lane3 >= 2 * EZ, from_down, from_up), 2 * EZ)

    def add_y(ref, plane):
        for ex in range(EX):
            ref[ex, :, 0:8] += jnp.where(lane3 < EZ, roll(plane, -EZ * ex), 0.0)
            ref[ex, :, 56:64] += jnp.where(
                lane3 >= 3 * EZ, roll(plane, EZ * (1 - ex)), 0.0
            )

    def in_slot(value, slot):
        return jnp.where((lane2 >= EZ * slot) & (lane2 < EZ * (slot + 1)), value, 0.0)

    def outer_terms(slot):
        face = jnp.concatenate(
            [u_ref[0, 0], u_ref[1, 7], y_faces().reshape(64, LANES)], axis=1
        )
        from_left_down = recv_c[slot, FROM_LEFT_DOWN - 4]
        from_left_up = recv_c[slot, FROM_LEFT_UP - 4]
        from_right_down = recv_c[slot, FROM_RIGHT_DOWN - 4]
        from_right_up = recv_c[slot, FROM_RIGHT_UP - 4]
        sides = []
        for plane, low, high in (
            (recv_x[slot, FROM_LEFT, 1], from_left_down, from_left_up),
            (recv_x[slot, FROM_RIGHT, 1], from_right_down, from_right_up),
        ):
            sides.append(
                jnp.concatenate(
                    [
                        plane[0:8] + in_slot(roll(low, -EZ), 0),
                        plane[8:56],
                        plane[56:64] + in_slot(roll(high, 2 * EZ), 3),
                    ],
                    axis=0,
                )
            )
        normal_y = arrived_y(slot, 1)
        first = (
            normal_y[0]
            + in_slot(roll(from_left_down, -2 * EZ), 0)
            + in_slot(from_left_up, 2)
        )
        last = (
            normal_y[7]
            + in_slot(roll(from_right_down, -EZ), 1)
            + in_slot(roll(from_right_up, EZ), 3)
        )
        normal_y = jnp.concatenate([first[None], normal_y[1:7], last[None]], axis=0)
        normal = jnp.concatenate([sides[0], sides[1], normal_y.reshape(64, LANES)], axis=1)
        weight = weight_ref[0] * (1.0 / w_end)
        weight = jnp.concatenate([weight] * 3, axis=1)
        odd_ex = lax.rem(lax.div(lane2, EZ), 2) == 1
        arrived = y_faces() - send_y[slot, 0]
        arrived = jnp.concatenate(
            [
                jnp.where(odd_ex, arrived[0], 0.0)[None],
                arrived[1:7],
                jnp.where(odd_ex, 0.0, arrived[7])[None],
            ],
            axis=0,
        )
        arrived = jnp.concatenate(
            [
                u_ref[0, 0] - send_x[slot, 0, 0],
                u_ref[1, 7] - send_x[slot, 1, 0],
                arrived.reshape(64, LANES),
            ],
            axis=1,
        )
        modes = small_product(
            0, jnp.concatenate([weight * face, weight * arrived], axis=1)
        )
        width = 3 * LANES
        modes = face_lam[...] * modes[:, :width] + own_lam[...] * modes[:, width:]
        spread = small_product(1, modes)
        inward = own_normal[...] * arrived
        result = face_normal[...] * (normal + k_end * face) + w_end * weight * spread
        lines = []
        for side in range(2):
            plane = face[:, side * LANES : (side + 1) * LANES]
            value = jnp.where(lane2 < 2 * EZ, plane[0:8], plane[56:64])
            along_x = jnp.where(lane2 < 2 * EZ, sides[side][0:8], sides[side][56:64])
            edge_y = last if side else first
            along_y = jnp.where(
                lane2 < 2 * EZ,
                roll(edge_y, -EZ) if side else edge_y,
                edge_y if side else roll(edge_y, EZ),
            )
            along_z = None
            for c in range(NODES):
                term = tab_ref[38 + c] * value[c : c + 1]
                along_z = term if along_z is None else along_z + term
            lines.append(
                line_tab[side, 0] * (along_x + k_end * value)
                + line_tab[side, 1] * (along_y + k_end * value)
                + line_tab[side, 2] * along_z
            )
        return result, lines, inward

    def add_outer(result, lines, inward):
        inward_y = inward[:, 2 * LANES :].reshape(8, 8, LANES)
        for ex in range(EX):
            inward_x = inward[:, ex * LANES : (ex + 1) * LANES]
            along = jnp.where(
                lane3 < EZ,
                roll(inward_y, -EZ * ex),
                jnp.where(lane3 >= 3 * EZ, roll(inward_y, EZ * (1 - ex)), 0.0),
            )
            for a in range(NODES):
                terms = (along[a][None] * tab_ref[46:54]).reshape(64, LANES)
                w_ref[ex, a] += terms + inward_x * float(stiff[a, 7 * ex])
        for side, (ex, a) in enumerate(((0, 0), (1, 7))):
            w_ref[ex, a] += result[:, side * LANES : (side + 1) * LANES]
            w_ref[ex, a, 0:8] += in_slot(lines[side], 0)
            w_ref[ex, a, 56:64] += in_slot(lines[side], 3)
        add_y(w_ref, result[:, 2 * LANES :].reshape(8, 8, LANES))

    def small_product(which, value):
        high = value.astype(jnp.bfloat16)
        low = (value - high.astype(jnp.float32)).astype(jnp.bfloat16)
        return jnp.dot(
            plane_ref[which],
            jnp.concatenate([high, low, high], axis=0),
            preferred_element_type=jnp.float32,
        )

    def product(which, value):
        high = value.astype(jnp.bfloat16)
        low = (value - high.astype(jnp.float32)).astype(jnp.bfloat16)
        return jnp.dot(
            mat_ref[which],
            jnp.concatenate([high, low, high], axis=0),
            preferred_element_type=jnp.float32,
        )

    def flat(parts):
        return jnp.concatenate([part.reshape(256, LANES) for part in parts], axis=1)

    def element_op(fields, diag_ref):
        even, odd = [], []
        for field in fields:
            low = field[0:4]
            high = jnp.concatenate([field[7:8], field[6:7], field[5:6], field[4:5]], axis=0)
            even.append(low + high)
            odd.append(low - high)
        even = product(0, flat(even)) * flat([diag_ref[ex, 0:4] for ex in range(EX)])
        odd = product(1, flat(odd)) * flat([diag_ref[ex, 4:8] for ex in range(EX)])
        even = product(2, even)
        odd = product(3, odd)
        out = []
        for ex in range(EX):
            at = slice(ex * LANES, (ex + 1) * LANES)
            e = even[:, at].reshape(4, 64, LANES)
            o = odd[:, at].reshape(4, 64, LANES)
            diff = e - o
            out.append(
                jnp.concatenate([e + o, diff[3:4], diff[2:3], diff[1:2], diff[0:1]], axis=0)
            )
        return out

    def stiffness():
        weight = weight_ref[...]
        out = element_op([u_ref[ex] * weight for ex in range(EX)], lam_ref)
        for ex in range(EX):
            w_ref[ex] = out[ex] * weight

    def smoother(keep, take):
        out = element_op([r_ref[ex] for ex in range(EX)], inv_ref)
        for ex in range(EX):
            u_ref[ex] = (take * out[ex] + keep * u_ref[ex]) * winv_ref[...]

    wide = (levels - 1) * XCOLS
    gy_bits = n_gy.bit_length() - 1
    split = gy_bits * XCOLS

    def exchange(cycle, send_ref, recv_ref, to, send_s, recv_s):
        copies = []
        for index, target in enumerate(to):
            copy = pltpu.make_async_remote_copy(
                src_ref=send_ref,
                dst_ref=recv_ref.at[cycle, index],
                send_sem=send_s.at[index],
                recv_sem=recv_s.at[cycle, index],
                device_id=target,
                device_id_type=MESH,
            )
            copy.start()
            copies.append(copy)
        for copy in copies:
            copy.wait()

    def level_sum(own, recv_ref, cycle, count, first_level_lane):
        which = lax.broadcasted_iota(jnp.int32, own.shape, 1)
        total = own
        start = 1
        bit = 0
        while start < count:
            part = recv_ref[cycle, start - 1]
            for index in range(start + 1, 2 * start):
                part = part + recv_ref[cycle, index - 1]
            total = total + jnp.where(which >= bit * XCOLS + first_level_lane, part, 0.0)
            start *= 2
            bit += 1
        return total

    def coarse(cycle):
        sums = {}
        for ex in range(EX):
            scaled = r_ref[ex] * winv_ref[...]
            for v in range(2):
                by_v = scaled[0] * float(interp[0, v])
                for a in range(1, NODES):
                    by_v = by_v + scaled[a] * float(interp[a, v])
                by_v = by_v.reshape(8, 8, LANES)
                for u in range(2):
                    by_u = by_v[0] * float(interp[0, u])
                    for b in range(1, NODES):
                        by_u = by_u + by_v[b] * float(interp[b, u])
                    for t in range(2):
                        sums[v, u, ex, t] = jnp.sum(
                            by_u * tab_ref[36 + t], axis=0, keepdims=True
                        )
        order = [(v, u, ex) for v in range(2) for u in range(2) for ex in range(EX)]
        split_t = jnp.concatenate(
            [jnp.concatenate([sums[key + (t,)] for t in range(2)], axis=1) for key in order],
            axis=0,
        )
        vector = exact_rows(split_t, perm_ref[0])
        pieces = []
        for level in range(levels):
            rows = slice(level * XCOLS, (level + 1) * XCOLS)
            acc = None
            for q in range(8):
                term = x_factor_ref[rows, q * 256 : (q + 1) * 256] * vector[q : q + 1]
                acc = term if acc is None else acc + term
            pieces.append(acc[:, :LANES] + acc[:, LANES:])
        def row_of(parts):
            block = jnp.concatenate(parts, axis=0)
            missing = LANES - block.shape[0]
            if missing:
                block = jnp.concatenate([block, jnp.zeros((missing, LANES), jnp.float32)], axis=0)
            return jnp.sum(block.T, axis=0, keepdims=True)
        own = row_of(pieces[0:1])
        upper = jnp.concatenate(
            [row_of(pieces[i : i + 4]) for i in range(1, levels, 4)], axis=1
        )[:, :wide]
        send_one[...] = upper
        exchange(cycle, send_one, recv_one, one_targets, one_send_sem, one_recv_sem)
        upper = level_sum(upper, recv_one, cycle, n_gy, 0)
        send_two[...] = upper[:, split:]
        exchange(cycle, send_two, recv_two, two_targets, two_send_sem, two_recv_sem)
        top = level_sum(upper[:, split:], recv_two, cycle, n_gx, 0)
        upper = jnp.concatenate([upper[:, :split], top], axis=1)
        own = own * live_ref[:, 0:LANES]
        upper = upper * live_ref[:, LANES : LANES + wide]
        tail = (-wide) % LANES
        if tail:
            upper = jnp.concatenate([upper, jnp.zeros((1, tail), jnp.float32)], axis=1)
        cols = [jnp.broadcast_to(own, (LANES, LANES)).T[:XCOLS]]
        for first in range(0, wide, LANES):
            part = jnp.broadcast_to(upper[:, first : first + LANES], (LANES, LANES)).T
            cols += [part[k * XCOLS : (k + 1) * XCOLS] for k in range(LANES // XCOLS)]
        back = []
        for q in range(8):
            acc = None
            for level in range(levels):
                block = x_factor_ref[
                    level * XCOLS : (level + 1) * XCOLS, q * 256 : (q + 1) * 256
                ]
                col = cols[level]
                term = block * jnp.concatenate([col, col], axis=1)
                acc = term if acc is None else acc + term
            back.append(jnp.sum(acc, axis=0, keepdims=True))
        split_t = exact_rows(jnp.concatenate(back, axis=0), perm_ref[1])
        for ex in range(EX):
            by_v = []
            for v in range(2):
                by_u = []
                for u in range(2):
                    q = (v * 2 + u) * EX + ex
                    by_u.append(
                        split_t[q : q + 1, :LANES] * tab_ref[36]
                        + split_t[q : q + 1, LANES:] * tab_ref[37]
                    )
                by_v.append(
                    jnp.concatenate(
                        [
                            by_u[0] * float(interp[b, 0]) + by_u[1] * float(interp[b, 1])
                            for b in range(NODES)
                        ],
                        axis=0,
                    )
                )
            for a in range(NODES):
                u_ref[ex, a] = winv_ref[a] * (
                    by_v[0] * float(interp[a, 0]) + by_v[1] * float(interp[a, 1])
                )

    center = 0.5 * (bound_high + bound_low)
    radius = 0.5 * (bound_high - bound_low)
    ratio = center / radius
    rho_old = 1.0 / ratio
    rho_new = 1.0 / (2.0 * ratio - rho_old)

    own_pairs(u_ref)
    pl.semaphore_wait(barrier, len(everyone))
    copies = send_faces(1, 1)
    for copy in geom_copies:
        copy.start()
    winv_ref[...] = (edge[:, None] * edge[None] * zmask[None, None]).reshape(8, 64, LANES)
    for ex in range(EX):
        ax, ay, az = metrics(*[geom_ref[2 * dim + ex : 2 * dim + ex + 1] for dim in range(3)])
        in_x = lam_i * ax[None]
        in_y = lam_j * ay[None]
        in_z = lam_k * az
        spectrum = (in_x[:, None] + in_y[None] + in_z[None, None]).reshape(8, 64, LANES)
        shift = shift_ratio * (ax + ay + az)
        lam_ref[ex] = spectrum
        inv_ref[ex] = 1.0 / (spectrum + shift[None])
    x_ref[...] = jnp.zeros_like(x_ref)
    slots = lambda values: jnp.where(
        lane2 < EZ,
        values[0],
        jnp.where(lane2 < 2 * EZ, values[1], jnp.where(lane2 < 3 * EZ, values[2], values[3])),
    )
    own = []
    for dim in range(3):
        low, high = (geom_ref[2 * dim + ex : 2 * dim + ex + 1] for ex in range(EX))
        own.append([low, high, slots([low, roll(high, EZ), roll(low, -EZ), high])])
    for part in range(3):
        ax, ay, az = metrics(*[own[dim][part] for dim in range(3)])
        at = slice(part * LANES, (part + 1) * LANES)
        normal, along = (ay, ax) if part == 2 else (ax, ay)
        own_lam[:, at] = ((lam_j * along[None]) + (lam_k * az)[None]).reshape(64, LANES)
        own_normal[:, at] = (w_node * w_c[None] * normal[None]).reshape(64, LANES)
    receive_faces(1, copies)
    r_ref[...] = u_ref[...]
    for copy in geom_copies:
        copy.wait()

    def ghost(source, dim, ex):
        return recv_g[source, 2 * dim + ex : 2 * dim + ex + 1]

    outer = []
    for dim in range(3):
        y_side = slots(
            [
                roll(ghost(FROM_DOWN, dim, 0), EZ),
                roll(ghost(FROM_DOWN, dim, 1), 2 * EZ),
                roll(ghost(FROM_UP, dim, 0), 2 * EZ),
                roll(ghost(FROM_UP, dim, 1), 3 * EZ),
            ]
        )
        outer.append([ghost(FROM_LEFT, dim, 1), ghost(FROM_RIGHT, dim, 0), y_side])
    for part in range(3):
        ax, ay, az = metrics(*[outer[dim][part] for dim in range(3)])
        at = slice(part * LANES, (part + 1) * LANES)
        normal, along = (ay, ax) if part == 2 else (ax, ay)
        face_lam[:, at] = ((lam_j * along[None]) + (lam_k * az)[None]).reshape(64, LANES)
        face_normal[:, at] = (w_node * w_c[None] * normal[None]).reshape(64, LANES)
    for side, (low, high, ex) in enumerate(
        ((FROM_LEFT_DOWN, FROM_LEFT_UP, 1), (FROM_RIGHT_DOWN, FROM_RIGHT_UP, 0))
    ):
        lengths = [
            jnp.where(
                lane2 < 2 * EZ,
                roll(ghost(low, dim, ex), EZ),
                roll(ghost(high, dim, ex), -EZ),
            )
            for dim in range(3)
        ]
        ax, ay, az = metrics(*lengths)
        line_tab[side, 0] = w_end * w_c * ax
        line_tab[side, 1] = w_end * w_c * ay
        line_tab[side, 2] = jnp.broadcast_to(w_end * w_end * az, (8, LANES))

    for load in later_loads:
        load.wait()

    def step(index, carry):
        phase = lax.rem(index, SMOOTH)
        cycle = lax.div(index, SMOOTH)
        slot = lax.rem(index, 2)
        is_coarse = phase == 2
        second = (phase == 1) | (phase == 4)

        @pl.when(is_coarse)
        def _():
            coarse(cycle)

        @pl.when(jnp.logical_not(is_coarse))
        def _():
            keep = jnp.where(second, rho_new * rho_old, 0.0)
            take = jnp.where(second, 2.0 * rho_new / radius, 1.0 / center)
            smoother(keep, take)

        own_pairs(u_ref)
        copies = send_faces(slot, 2)

        @pl.when(index < SMOOTH * CYCLES - 1)
        def _():
            stiffness()

        receive_faces(slot, copies)
        for ex in range(EX):
            x_ref[ex] += u_ref[ex]

        @pl.when(index < SMOOTH * CYCLES - 1)
        def _():
            add_outer(*outer_terms(slot))
            own_pairs(w_ref)
            for ex in range(EX):
                r_ref[ex] -= free_scaled(w_ref[ex])

        return carry

    lax.fori_loop(0, SMOOTH * CYCLES, step, 0)

    by_node = [
        [
            jnp.concatenate(
                [x_ref[ex, a, pl.ds(c, 8, stride=8)] for a in range(NODES)], axis=0
            )
            for c in range(NODES)
        ]
        for ex in range(EX)
    ]
    rows = []
    for ex in range(EX):
        for ey in range(EY):
            halves = []
            for half in range(2):
                joined = None
                for s in range(4):
                    part = roll(by_node[ex][half * 4 + s], EZ * (s - ey))
                    joined = part if s == 0 else jnp.where(lane2 >= EZ * s, part, joined)
                halves.append(joined)
            rows.append(jnp.concatenate(halves, axis=1))
    result = exact_rows(jnp.concatenate(rows, axis=0), perm_ref[3])
    for half in range(2):
        at = slice(half * LANES, (half + 1) * LANES)
        for k in range(EX * EY):
            for a in range(NODES):
                first = k * 64 + a * 8
                w_ref[half, a, pl.ds(k, 8, stride=8)] = result[first : first + 8, at]
    for half in range(2):
        at = slice(half * LANES, (half + 1) * LANES)
        out_ref[:, :, at] = w_ref[half].reshape(128, EY, LANES)


def per_device(source, geometry, disc_mask, thrust, xxt_factor, col_count):
    n_gx = lax.axis_size("gx")
    n_gy = lax.axis_size("gy")
    levels = xxt_factor.shape[0]
    wide = (levels - 1) * XCOLS
    split = (n_gy.bit_length() - 1) * XCOLS
    matrices, plane, table, perms, interp, stiff, weights = constant_tables()
    field = (EX, NODES, 64, LANES)
    f32 = jnp.float32
    out = pl.pallas_call(
        functools.partial(kernel, n_gx, n_gy, levels, interp, stiff, weights),
        out_shape=jax.ShapeDtypeStruct((NODES * NODES * EX, EY, EZ * NODES), f32),
        in_specs=[pl.BlockSpec(memory_space=pl.ANY)] * 10,
        out_specs=pl.BlockSpec(memory_space=pltpu.VMEM),
        scratch_shapes=[
            pltpu.VMEM((NODES * NODES * EX, EY, EZ * NODES), f32),
            pltpu.VMEM(geometry.shape, f32),
            pltpu.VMEM(disc_mask.shape, jnp.int32),
            pltpu.VMEM(thrust.shape, f32),
            pltpu.VMEM((1, levels), jnp.int32),
            pltpu.VMEM(plane.shape, jnp.bfloat16),
            pltpu.VMEM(table.shape, f32),
            pltpu.VMEM(perms.shape, jnp.bfloat16),
            pltpu.VMEM((8, LANES), f32),
            pltpu.VMEM((1, LANES + wide), f32),
            pltpu.VMEM(field, f32),
            pltpu.VMEM(field, f32),
            pltpu.VMEM(field, f32),
            pltpu.VMEM(field, f32),
            pltpu.VMEM(field[1:], f32),
            pltpu.VMEM(field[1:], f32),
            pltpu.VMEM(field, f32),
            pltpu.VMEM(field, f32),
            pltpu.VMEM((64, 3 * LANES), f32),
            pltpu.VMEM((64, 3 * LANES), f32),
            pltpu.VMEM((64, 3 * LANES), f32),
            pltpu.VMEM((64, 3 * LANES), f32),
            pltpu.VMEM((2, 3, 8, LANES), f32),
            pltpu.VMEM((levels * XCOLS, xxt_factor.shape[2]), f32),
            pltpu.VMEM(matrices.shape, jnp.bfloat16),
            pltpu.VMEM((2, 2, 2, 64, LANES), f32),
            pltpu.VMEM((2, 2, 8, 8, LANES), f32),
            pltpu.VMEM((2, 4, 8, LANES), f32),
            pltpu.VMEM((2, 2, 2, 64, LANES), f32),
            pltpu.VMEM((2, 2, 2, 8, 8, LANES), f32),
            pltpu.VMEM((2, 4, 8, LANES), f32),
            pltpu.VMEM((8, 8, LANES), f32),
            pltpu.VMEM((1, wide), f32),
            pltpu.VMEM((CYCLES, n_gy - 1, 1, wide), f32),
            pltpu.VMEM((1, wide - split), f32),
            pltpu.VMEM((CYCLES, n_gx - 1, 1, wide - split), f32),
            pltpu.SemaphoreType.DMA((2, 8)),
            pltpu.SemaphoreType.DMA((2, 8)),
            pltpu.SemaphoreType.DMA((8,)),
            pltpu.SemaphoreType.DMA((8,)),
            pltpu.SemaphoreType.DMA((n_gy - 1,)),
            pltpu.SemaphoreType.DMA((CYCLES, n_gy - 1)),
            pltpu.SemaphoreType.DMA((n_gx - 1,)),
            pltpu.SemaphoreType.DMA((CYCLES, n_gx - 1)),
            pltpu.SemaphoreType.DMA((10,)),
        ],
        compiler_params=pltpu.CompilerParams(
            collective_id=0, has_side_effects=True, vmem_limit_bytes=56 * 1024 * 1024
        ),
    )(
        source.reshape(NODES * NODES * EX, EY, EZ * NODES),
        geometry,
        disc_mask,
        thrust,
        col_count.T,
        xxt_factor.reshape(levels * XCOLS, xxt_factor.shape[2]),
        jnp.asarray(matrices),
        jnp.asarray(plane),
        jnp.asarray(table),
        jnp.asarray(perms),
    )
    return out.reshape(source.shape)


def solution(mesh):
    return jax.shard_map(
        per_device,
        mesh=mesh,
        in_specs=(
            P(None, None, "gx", "gy", None),
            P(None, "gx", "gy", None),
            P("gx", "gy", None),
            P("gx", "gy", None),
            P(None, None, ("gx", "gy")),
            P(None, ("gx", "gy")),
        ),
        out_specs=P(None, None, "gx", "gy", None),
        check_vma=False,
    )
```

```python
import functools
import math

import jax
import jax.numpy as jnp
import ml_dtypes
import numpy as np
from jax import lax
from jax.experimental import pallas as pl
from jax.experimental.pallas import tpu as pltpu
from jax.sharding import PartitionSpec as P

NODES = 8
CYCLES = 2
EX = 2
EY = 4
EZ = 32
LANES = EY * EZ
XCOLS = 32
SMOOTH = 5

bound_low = 0.3
bound_high = 3.0
shift_ratio = 0.25
MESH = pl.DeviceIdType.MESH


def legendre_table(points, poly_order):
    table = [points * 0.0 + 1.0, points]
    for degree in range(2, poly_order + 1):
        table.append(
            ((2.0 * degree - 1.0) * points * table[-1] - (degree - 1.0) * table[-2]) / degree
        )
    return table


def jacobi_eigen(matrix):
    size_n = matrix.shape[0]
    current = matrix.copy()
    vectors = np.eye(size_n)
    for sweep_index in range(30):
        for first in range(size_n - 1):
            for second in range(first + 1, size_n):
                angle = 0.5 * math.atan2(
                    2.0 * float(current[first, second]),
                    float(current[second, second] - current[first, first]),
                )
                rotation = np.eye(size_n)
                rotation[first, first] = math.cos(angle)
                rotation[second, second] = math.cos(angle)
                rotation[first, second] = math.sin(angle)
                rotation[second, first] = -math.sin(angle)
                current = rotation.T @ current @ rotation
                vectors = vectors @ rotation
    values = np.array([current[index, index] for index in range(size_n)])
    order = np.argsort(values)
    return (values[order], vectors[:, order])


def gll_tables(node_count):
    poly_order = node_count - 1
    points = np.cos(np.pi * np.arange(node_count) / poly_order)
    for newton_index in range(200):
        table = legendre_table(points, poly_order)
        points = points - (points * table[poly_order] - table[poly_order - 1]) / (
            node_count * table[poly_order]
        )
    points = points[::-1].copy()
    legendre = legendre_table(points, poly_order)[poly_order]
    weights = 2.0 / (poly_order * (poly_order + 1) * legendre**2)
    identity = np.eye(node_count)
    gap_matrix = points[:, None] - points[None, :] + identity
    off_diagonal = legendre[:, None] / (legendre[None, :] * gap_matrix) * (1.0 - identity)
    end_value = poly_order * (poly_order + 1) / 4.0
    end_terms = np.concatenate([[-end_value], np.zeros(node_count - 2), [end_value]])
    derivative = off_diagonal + identity * end_terms[None, :]
    stiffness = derivative.T @ (weights[:, None] * derivative)
    root_inverse = 1.0 / np.sqrt(weights)
    symmetric = root_inverse[:, None] * stiffness * root_inverse[None, :]
    symmetric = 0.5 * (symmetric + symmetric.T)
    eigen_values, eigen_vectors = jacobi_eigen(symmetric)
    eigen_modes = root_inverse[:, None] * eigen_vectors
    vertex_interp = np.stack([(1.0 - points) / 2.0, (1.0 + points) / 2.0], axis=1)
    return weights, stiffness, eigen_modes, eigen_values, vertex_interp


def mode_order(modes):
    even = [i for i in range(NODES) if modes[0, i] * modes[NODES - 1, i] > 0.0]
    odd = [i for i in range(NODES) if i not in even]
    return even, odd


def split_pair(matrix):
    exact = matrix.astype(np.float32)
    high = exact.astype(ml_dtypes.bfloat16)
    low = (exact - high.astype(np.float32)).astype(ml_dtypes.bfloat16)
    return np.concatenate([high, high, low], axis=1)


def constant_tables():
    weights, stiffness, modes, values, interp = gll_tables(NODES)
    even, odd = mode_order(modes)
    half = NODES // 2
    mats = []
    for chosen in (even, odd):
        inverse = np.kron(modes[:half][:, chosen], np.kron(modes, modes))
        mats.append((split_pair(inverse.T), split_pair(inverse)))
    matrices = np.stack([mats[0][0], mats[1][0], mats[0][1], mats[1][1]])
    plane = np.kron(modes, modes)
    plane_matrices = np.stack([split_pair(plane.T), split_pair(plane)])
    full = np.ones((NODES, LANES))
    edge = np.ones(NODES)
    edge[0] = edge[-1] = 0.5
    ez = np.arange(LANES)[None, :] % EZ
    node = np.arange(NODES)[:, None]
    z_shared = 1.0 + ((node == 0) & (ez > 0)) + ((node == NODES - 1) & (ez < EZ - 1))
    free = 1.0 - ((node == NODES - 1) & (ez == EZ - 1))
    rows = [values[i] * full for i in even + odd]
    rows += [value * full for value in values]
    rows += [weight * full for weight in weights]
    rows += [value * full for value in edge]
    rows += [values[:, None] * full, weights[:, None] * full, free / z_shared, free * full]
    rows += [interp[:, 0:1] * full, interp[:, 1:2] * full]
    rows += [stiffness[:, c : c + 1] * full for c in range(NODES)]
    low_side = np.arange(LANES)[None, :] < LANES // 2
    rows += [
        np.where(low_side, stiffness[b, 0], stiffness[b, NODES - 1]) * full for b in range(NODES)
    ]
    table = np.stack(rows).astype(np.float32)
    perm = np.zeros((2 * LANES, 2 * LANES), np.float32)
    for t in range(2):
        for element in range(LANES):
            perm[t * LANES + element, 2 * element + t] = 1.0
    order = np.zeros((EZ * NODES, EZ * NODES), np.float32)
    for c in range(NODES):
        for element in range(EZ):
            order[element * NODES + c, c * EZ + element] = 1.0
    perms = np.stack([perm, perm.T, order, order.T]).astype(ml_dtypes.bfloat16)
    return (
        matrices,
        plane_matrices,
        table,
        perms,
        interp.astype(np.float32),
        stiffness.astype(np.float32),
        weights.astype(np.float32),
    )


def flipped(index, bits):
    out = index
    bit = 1
    while bit <= bits:
        if bits & bit:
            out = out + bit - 2 * bit * lax.rem(lax.div(index, bit), 2)
        bit *= 2
    return out


def exact_rows(value, perm):
    first = value.astype(jnp.bfloat16)
    rest = value - first.astype(jnp.float32)
    second = rest.astype(jnp.bfloat16)
    third = (rest - second.astype(jnp.float32)).astype(jnp.bfloat16)
    parts = [
        jnp.dot(part, perm, preferred_element_type=jnp.float32)
        for part in (first, second, third)
    ]
    return parts[0] + parts[1] + parts[2]


def kernel(
    n_gx,
    n_gy,
    levels,
    interp,
    stiff,
    weights,
    source_hbm,
    lengths_hbm,
    disc_hbm,
    thrust_hbm,
    count_hbm,
    x_hbm,
    mat_hbm,
    plane_hbm,
    tab_hbm,
    perm_hbm,
    out_ref,
    source_ref,
    lengths_ref,
    disc_ref,
    thrust_ref,
    count_ref,
    plane_ref,
    tab_ref,
    perm_ref,
    geom_ref,
    live_ref,
    u_ref,
    r_ref,
    w_ref,
    x_ref,
    weight_ref,
    winv_ref,
    lam_ref,
    inv_ref,
    face_lam,
    face_normal,
    own_lam,
    own_normal,
    line_tab,
    x_factor_ref,
    mat_ref,
    send_x,
    send_y,
    send_c,
    recv_x,
    recv_y,
    recv_c,
    recv_g,
    send_one,
    recv_one,
    send_two,
    recv_two,
    send_sem,
    recv_sem,
    g_send_sem,
    g_recv_sem,
    one_send_sem,
    one_recv_sem,
    two_send_sem,
    two_recv_sem,
    load_sem,
):
    me_x = lax.axis_index("gx")
    me_y = lax.axis_index("gy")
    left = lax.rem(me_x + n_gx - 1, n_gx)
    right = lax.rem(me_x + 1, n_gx)
    down = lax.rem(me_y + n_gy - 1, n_gy)
    up = lax.rem(me_y + 1, n_gy)
    targets = [
        (left, me_y),
        (right, me_y),
        (me_x, down),
        (me_x, up),
        (left, down),
        (right, up),
        (left, up),
        (right, down),
    ]
    FROM_RIGHT, FROM_LEFT, FROM_UP, FROM_DOWN = 0, 1, 2, 3
    FROM_RIGHT_UP, FROM_LEFT_DOWN, FROM_RIGHT_DOWN, FROM_LEFT_UP = 4, 5, 6, 7
    one_targets = [(me_x, flipped(me_y, off)) for off in range(1, n_gy)]
    two_targets = [(flipped(me_x, off), me_y) for off in range(1, n_gx)]
    barrier = pltpu.get_barrier_semaphore()
    everyone = targets + one_targets + two_targets
    for target in everyone:
        pl.semaphore_signal(barrier, inc=1, device_id=target, device_id_type=MESH)
    loads = [
        pltpu.make_async_copy(src, dst, load_sem.at[index])
        for index, (src, dst) in enumerate(
            (
                (tab_hbm, tab_ref),
                (source_hbm, source_ref),
                (perm_hbm, perm_ref),
                (lengths_hbm, lengths_ref),
                (disc_hbm, disc_ref),
                (thrust_hbm, thrust_ref),
                (count_hbm, count_ref),
                (mat_hbm, mat_ref),
                (plane_hbm, plane_ref),
                (x_hbm, x_factor_ref),
            )
        )
    ]
    for load in loads:
        load.start()
    first_loads, later_loads = loads[:7], loads[7:]

    lane = lax.broadcasted_iota(jnp.int32, (1, 1, 1, LANES), 3)
    lane3 = lax.broadcasted_iota(jnp.int32, (1, 1, LANES), 2)
    lane2 = lax.broadcasted_iota(jnp.int32, (1, LANES), 1)
    z2 = lax.rem(lane2, EZ)

    def roll(value, shift):
        shift = shift % LANES
        return value if shift == 0 else pltpu.roll(value, shift, value.ndim - 1)

    for load in first_loads:
        load.wait()
    for dim in range(3):
        for ex in range(EX):
            geom_ref[2 * dim + ex : 2 * dim + ex + 1] = jnp.concatenate(
                [lengths_ref[dim, ex, ey : ey + 1] for ey in range(EY)], axis=1
            )
    geom_ref[6:8] = jnp.ones((2, LANES), jnp.float32)
    forces = []
    for ex in range(EX):
        element = disc_ref[ex].astype(jnp.float32) * thrust_ref[ex]
        forces.append(
            jnp.concatenate([element[ey : ey + 1] for ey in range(EY)], axis=1)
        )
    column = lax.rem(lane2, XCOLS)
    for first in range(0, levels, LANES // XCOLS):
        chosen = [0] * 4 if first == 0 else range(first - 3, first + 1)
        count = None
        for place, level in enumerate(chosen):
            one = jnp.broadcast_to(count_ref[:, level : level + 1], (1, LANES))
            count = one if count is None else jnp.where(lane2 >= XCOLS * place, one, count)
        at = slice(first // 4 * LANES, (first // 4 + 1) * LANES)
        live_ref[:, at] = (column < count).astype(jnp.float32)
    lam_i = tab_ref[0:8]
    lam_j = tab_ref[8:16]
    w_node = tab_ref[16:24]
    edge = tab_ref[24:32]
    lam_k = tab_ref[32]
    w_c = tab_ref[33]
    zmask = tab_ref[34]
    free = tab_ref[35]
    w_end = float(weights[0])
    k_end = float(stiff[0, 0])
    weight_ref[...] = (w_node[:, None] * w_node[None] * w_c[None, None]).reshape(8, 64, LANES)

    def metrics(hx, hy, hz):
        return hy * hz / (2.0 * hx), hx * hz / (2.0 * hy), hx * hy / (2.0 * hz)

    for half in range(2):
        at = slice(half * LANES, (half + 1) * LANES)
        w_ref[half] = source_ref[:, :, at].reshape(8, 64, LANES)
    by_node = exact_rows(
        jnp.concatenate(
            [
                jnp.concatenate(
                    [w_ref[half, a, pl.ds(k, 8, stride=8)] for half in range(2)], axis=1
                )
                for k in range(EX * EY)
                for a in range(NODES)
            ],
            axis=0,
        ),
        perm_ref[2],
    )
    for ex in range(EX):
        for c in range(NODES):
            at = slice(c // 4 * LANES, (c // 4 + 1) * LANES)
            joined = None
            for ey in range(EY):
                first = (ex * EY + ey) * 64
                part = roll(by_node[first : first + 64, at], EZ * (ey - c % 4))
                joined = part if ey == 0 else jnp.where(lane2 >= EZ * ey, part, joined)
            for a in range(NODES):
                u_ref[ex, a, pl.ds(c, 8, stride=8)] = joined[8 * a : 8 * a + 8]

    for ex in range(EX):
        hx = geom_ref[ex : ex + 1]
        hy = geom_ref[2 + ex : 3 + ex]
        hz = geom_ref[4 + ex : 5 + ex]
        mass = (hx * hy * hz / 8.0)[None] * weight_ref[...]
        u_ref[ex] = mass * (u_ref[ex] + forces[ex][None])

    def free_scaled(value):
        return (value.reshape(8, 8, 8, LANES) * free[None, None]).reshape(8, 64, LANES)

    for ex in range(EX):
        u_ref[ex] = free_scaled(u_ref[ex])

    geom_copies = []
    for index, target in enumerate(targets):
        copy = pltpu.make_async_remote_copy(
            src_ref=geom_ref,
            dst_ref=recv_g.at[index],
            send_sem=g_send_sem.at[index],
            recv_sem=g_recv_sem.at[index],
            device_id=target,
            device_id_type=MESH,
        )
        geom_copies.append(copy)

    def own_pairs(ref):
        shared = ref[0, 7] + ref[1, 0]
        ref[0, 7] = shared
        ref[1, 0] = shared
        low = ref[:, :, 0:8]
        high = ref[:, :, 56:64]
        ref[:, :, 0:8] = low + jnp.where(lane >= EZ, roll(high, EZ), 0.0)
        ref[:, :, 56:64] = high + jnp.where(lane < LANES - EZ, roll(low, -EZ), 0.0)
        for ex in range(EX):
            for a in range(NODES):
                low = ref[ex, a, pl.ds(0, 8, stride=8)]
                high = ref[ex, a, pl.ds(7, 8, stride=8)]
                ref[ex, a, pl.ds(0, 8, stride=8)] = low + jnp.where(
                    z2 > 0, roll(high, 1), 0.0
                )
                ref[ex, a, pl.ds(7, 8, stride=8)] = high + jnp.where(
                    z2 < EZ - 1, roll(low, -1), 0.0
                )

    def packed_y(down_faces, up_faces):
        return jnp.where(
            lane3 < EZ,
            down_faces[0],
            jnp.where(
                lane3 < 2 * EZ,
                roll(down_faces[1], EZ),
                jnp.where(lane3 < 3 * EZ, roll(up_faces[0], -EZ), up_faces[1]),
            ),
        )

    def y_faces():
        return packed_y(
            [u_ref[ex, :, 0:8] for ex in range(EX)], [u_ref[ex, :, 56:64] for ex in range(EX)]
        )

    def weighted(parts, row):
        total = None
        for index, part in parts:
            term = part * float(stiff[row, index])
            total = term if total is None else total + term
        return total

    def send_faces(slot, planes):
        copies = [None] * 8

        def start(index, source, landing):
            copies[index] = pltpu.make_async_remote_copy(
                src_ref=source,
                dst_ref=landing,
                send_sem=send_sem.at[slot, index],
                recv_sem=recv_sem.at[slot, index],
                device_id=targets[index],
                device_id_type=MESH,
            )
            copies[index].start()

        corners = ((0, 0, 0), (1, 7, 7), (0, 0, 7), (1, 7, 0))
        if planes > 1:
            low = weighted([(a, u_ref[0, a]) for a in range(1, NODES)], 0)
            high = weighted([(a, u_ref[1, a]) for a in range(NODES - 1)], 7)
        for i, (ex, a, b) in enumerate(corners):
            ey = 0 if b == 0 else EY - 1
            line = roll(u_ref[ex, a, 8 * b : 8 * b + 8], -EZ * ey)
            if planes > 1:
                along_x = (high if ex else low)[8 * b : 8 * b + 8]
                others = [other for other in range(NODES) if other != b]
                along_y = weighted(
                    [(other, u_ref[ex, a, 8 * other : 8 * other + 8]) for other in others], b
                )
                line = jnp.where(
                    lane2 < EZ,
                    line,
                    jnp.where(
                        lane2 < 2 * EZ,
                        roll(along_x, EZ * (1 - ey)),
                        roll(along_y, EZ * (2 - ey)),
                    ),
                )
            send_c[slot, i] = line
        for i in range(4):
            start(4 + i, send_c.at[slot, i], recv_c.at[slot, i])
        send_x[slot, 0, 0] = u_ref[0, 0]
        send_x[slot, 1, 0] = u_ref[1, 7]
        if planes > 1:
            send_x[slot, 0, 1] = low
            send_x[slot, 1, 1] = high
        both = pl.ds(0, planes)
        for i in range(2):
            start(i, send_x.at[slot, i, both], recv_x.at[slot, i, both])
        send_y[slot, 0] = y_faces()
        if planes > 1:
            down_normal, up_normal = [], []
            for ex in range(EX):
                rows = [u_ref[ex, :, 8 * b : 8 * b + 8] for b in range(NODES)]
                down_normal.append(weighted([(b, rows[b]) for b in range(1, NODES)], 0))
                up_normal.append(weighted([(b, rows[b]) for b in range(NODES - 1)], 7))
            send_y[slot, 1] = packed_y(down_normal, up_normal)
        for i in range(2):
            start(2 + i, send_y.at[slot, both], recv_y.at[slot, i, both])
        return copies

    def receive_faces(slot, copies):
        for copy in copies:
            copy.wait()
        u_ref[1, 7] += recv_x[slot, FROM_RIGHT, 0]
        u_ref[0, 0] += recv_x[slot, FROM_LEFT, 0]
        add_y(u_ref, arrived_y(slot, 0))
        for index, (ex, a, first, to_ey) in enumerate(
            ((1, 7, 56, EY - 1), (0, 0, 0, 0), (1, 7, 0, 0), (0, 0, 56, EY - 1))
        ):
            u_ref[ex, a, first : first + 8] += in_slot(
                roll(recv_c[slot, index], EZ * to_ey), to_ey
            )

    def arrived_y(slot, plane):
        from_up = recv_y[slot, FROM_UP - 2, plane]
        from_down = recv_y[slot, FROM_DOWN - 2, plane]
        return roll(jnp.where(lane3 >= 2 * EZ, from_down, from_up), 2 * EZ)

    def add_y(ref, plane):
        for ex in range(EX):
            ref[ex, :, 0:8] += jnp.where(lane3 < EZ, roll(plane, -EZ * ex), 0.0)
            ref[ex, :, 56:64] += jnp.where(
                lane3 >= 3 * EZ, roll(plane, EZ * (1 - ex)), 0.0
            )

    def in_slot(value, slot):
        return jnp.where((lane2 >= EZ * slot) & (lane2 < EZ * (slot + 1)), value, 0.0)

    def outer_terms(slot):
        face = jnp.concatenate(
            [u_ref[0, 0], u_ref[1, 7], y_faces().reshape(64, LANES)], axis=1
        )
        from_left_down = recv_c[slot, FROM_LEFT_DOWN - 4]
        from_left_up = recv_c[slot, FROM_LEFT_UP - 4]
        from_right_down = recv_c[slot, FROM_RIGHT_DOWN - 4]
        from_right_up = recv_c[slot, FROM_RIGHT_UP - 4]
        sides = []
        for plane, low, high in (
            (recv_x[slot, FROM_LEFT, 1], from_left_down, from_left_up),
            (recv_x[slot, FROM_RIGHT, 1], from_right_down, from_right_up),
        ):
            sides.append(
                jnp.concatenate(
                    [
                        plane[0:8] + in_slot(roll(low, -EZ), 0),
                        plane[8:56],
                        plane[56:64] + in_slot(roll(high, 2 * EZ), 3),
                    ],
                    axis=0,
                )
            )
        normal_y = arrived_y(slot, 1)
        first = (
            normal_y[0]
            + in_slot(roll(from_left_down, -2 * EZ), 0)
            + in_slot(from_left_up, 2)
        )
        last = (
            normal_y[7]
            + in_slot(roll(from_right_down, -EZ), 1)
            + in_slot(roll(from_right_up, EZ), 3)
        )
        normal_y = jnp.concatenate([first[None], normal_y[1:7], last[None]], axis=0)
        normal = jnp.concatenate([sides[0], sides[1], normal_y.reshape(64, LANES)], axis=1)
        weight = weight_ref[0] * (1.0 / w_end)
        weight = jnp.concatenate([weight] * 3, axis=1)
        odd_ex = lax.rem(lax.div(lane2, EZ), 2) == 1
        arrived = y_faces() - send_y[slot, 0]
        arrived = jnp.concatenate(
            [
                jnp.where(odd_ex, arrived[0], 0.0)[None],
                arrived[1:7],
                jnp.where(odd_ex, 0.0, arrived[7])[None],
            ],
            axis=0,
        )
        arrived = jnp.concatenate(
            [
                u_ref[0, 0] - send_x[slot, 0, 0],
                u_ref[1, 7] - send_x[slot, 1, 0],
                arrived.reshape(64, LANES),
            ],
            axis=1,
        )
        modes = small_product(
            0, jnp.concatenate([weight * face, weight * arrived], axis=1)
        )
        width = 3 * LANES
        modes = face_lam[...] * modes[:, :width] + own_lam[...] * modes[:, width:]
        spread = small_product(1, modes)
        inward = own_normal[...] * arrived
        result = face_normal[...] * (normal + k_end * face) + w_end * weight * spread
        lines = []
        for side in range(2):
            plane = face[:, side * LANES : (side + 1) * LANES]
            value = jnp.where(lane2 < 2 * EZ, plane[0:8], plane[56:64])
            along_x = jnp.where(lane2 < 2 * EZ, sides[side][0:8], sides[side][56:64])
            edge_y = last if side else first
            along_y = jnp.where(
                lane2 < 2 * EZ,
                roll(edge_y, -EZ) if side else edge_y,
                edge_y if side else roll(edge_y, EZ),
            )
            along_z = None
            for c in range(NODES):
                term = tab_ref[38 + c] * value[c : c + 1]
                along_z = term if along_z is None else along_z + term
            lines.append(
                line_tab[side, 0] * (along_x + k_end * value)
                + line_tab[side, 1] * (along_y + k_end * value)
                + line_tab[side, 2] * along_z
            )
        return result, lines, inward

    def add_outer(result, lines, inward):
        inward_y = inward[:, 2 * LANES :].reshape(8, 8, LANES)
        for ex in range(EX):
            inward_x = inward[:, ex * LANES : (ex + 1) * LANES]
            along = jnp.where(
                lane3 < EZ,
                roll(inward_y, -EZ * ex),
                jnp.where(lane3 >= 3 * EZ, roll(inward_y, EZ * (1 - ex)), 0.0),
            )
            for a in range(NODES):
                terms = (along[a][None] * tab_ref[46:54]).reshape(64, LANES)
                w_ref[ex, a] += terms + inward_x * float(stiff[a, 7 * ex])
        for side, (ex, a) in enumerate(((0, 0), (1, 7))):
            w_ref[ex, a] += result[:, side * LANES : (side + 1) * LANES]
            w_ref[ex, a, 0:8] += in_slot(lines[side], 0)
            w_ref[ex, a, 56:64] += in_slot(lines[side], 3)
        add_y(w_ref, result[:, 2 * LANES :].reshape(8, 8, LANES))

    def small_product(which, value):
        high = value.astype(jnp.bfloat16)
        low = (value - high.astype(jnp.float32)).astype(jnp.bfloat16)
        return jnp.dot(
            plane_ref[which],
            jnp.concatenate([high, low, high], axis=0),
            preferred_element_type=jnp.float32,
        )

    def product(which, value):
        high = value.astype(jnp.bfloat16)
        low = (value - high.astype(jnp.float32)).astype(jnp.bfloat16)
        return jnp.dot(
            mat_ref[which],
            jnp.concatenate([high, low, high], axis=0),
            preferred_element_type=jnp.float32,
        )

    def flat(parts):
        return jnp.concatenate([part.reshape(256, LANES) for part in parts], axis=1)

    def element_op(fields, diag_ref):
        even, odd = [], []
        for field in fields:
            low = field[0:4]
            high = jnp.concatenate([field[7:8], field[6:7], field[5:6], field[4:5]], axis=0)
            even.append(low + high)
            odd.append(low - high)
        even = product(0, flat(even)) * flat([diag_ref[ex, 0:4] for ex in range(EX)])
        odd = product(1, flat(odd)) * flat([diag_ref[ex, 4:8] for ex in range(EX)])
        even = product(2, even)
        odd = product(3, odd)
        out = []
        for ex in range(EX):
            at = slice(ex * LANES, (ex + 1) * LANES)
            e = even[:, at].reshape(4, 64, LANES)
            o = odd[:, at].reshape(4, 64, LANES)
            diff = e - o
            out.append(
                jnp.concatenate([e + o, diff[3:4], diff[2:3], diff[1:2], diff[0:1]], axis=0)
            )
        return out

    def stiffness():
        weight = weight_ref[...]
        out = element_op([u_ref[ex] * weight for ex in range(EX)], lam_ref)
        for ex in range(EX):
            w_ref[ex] = out[ex] * weight

    def smoother(keep, take):
        out = element_op([r_ref[ex] for ex in range(EX)], inv_ref)
        for ex in range(EX):
            u_ref[ex] = (take * out[ex] + keep * u_ref[ex]) * winv_ref[...]

    wide = (levels - 1) * XCOLS
    gy_bits = n_gy.bit_length() - 1
    split = gy_bits * XCOLS

    def exchange(cycle, send_ref, recv_ref, to, send_s, recv_s):
        copies = []
        for index, target in enumerate(to):
            copy = pltpu.make_async_remote_copy(
                src_ref=send_ref,
                dst_ref=recv_ref.at[cycle, index],
                send_sem=send_s.at[index],
                recv_sem=recv_s.at[cycle, index],
                device_id=target,
                device_id_type=MESH,
            )
            copy.start()
            copies.append(copy)
        return copies

    def level_sum(own, recv_ref, cycle, count, first_level_lane):
        which = lax.broadcasted_iota(jnp.int32, own.shape, 1)
        total = own
        start = 1
        bit = 0
        while start < count:
            part = recv_ref[cycle, start - 1]
            for index in range(start + 1, 2 * start):
                part = part + recv_ref[cycle, index - 1]
            total = total + jnp.where(which >= bit * XCOLS + first_level_lane, part, 0.0)
            start *= 2
            bit += 1
        return total

    def coarse(cycle):
        sums = {}
        for ex in range(EX):
            scaled = r_ref[ex] * winv_ref[...]
            for v in range(2):
                by_v = scaled[0] * float(interp[0, v])
                for a in range(1, NODES):
                    by_v = by_v + scaled[a] * float(interp[a, v])
                by_v = by_v.reshape(8, 8, LANES)
                for u in range(2):
                    by_u = by_v[0] * float(interp[0, u])
                    for b in range(1, NODES):
                        by_u = by_u + by_v[b] * float(interp[b, u])
                    for t in range(2):
                        sums[v, u, ex, t] = jnp.sum(
                            by_u * tab_ref[36 + t], axis=0, keepdims=True
                        )
        order = [(v, u, ex) for v in range(2) for u in range(2) for ex in range(EX)]
        split_t = jnp.concatenate(
            [jnp.concatenate([sums[key + (t,)] for t in range(2)], axis=1) for key in order],
            axis=0,
        )
        vector = exact_rows(split_t, perm_ref[0])
        pieces = []
        for level in range(levels):
            rows = slice(level * XCOLS, (level + 1) * XCOLS)
            acc = None
            for q in range(8):
                term = x_factor_ref[rows, q * 256 : (q + 1) * 256] * vector[q : q + 1]
                acc = term if acc is None else acc + term
            pieces.append(acc[:, :LANES] + acc[:, LANES:])
        def row_of(parts):
            block = jnp.concatenate(parts, axis=0)
            missing = LANES - block.shape[0]
            if missing:
                block = jnp.concatenate([block, jnp.zeros((missing, LANES), jnp.float32)], axis=0)
            return jnp.sum(block.T, axis=0, keepdims=True)
        own = row_of(pieces[0:1])
        upper = jnp.concatenate(
            [row_of(pieces[i : i + 4]) for i in range(1, levels, 4)], axis=1
        )[:, :wide]
        back = [None] * 8

        def spread(first_level, row):
            part = jnp.broadcast_to(row, (LANES, LANES)).T
            for q in range(8):
                for k in range(row_levels[first_level]):
                    level = first_level + k
                    col = part[k * XCOLS : (k + 1) * XCOLS]
                    block = x_factor_ref[
                        level * XCOLS : (level + 1) * XCOLS, q * 256 : (q + 1) * 256
                    ]
                    term = block * jnp.concatenate([col, col], axis=1)
                    back[q] = term if back[q] is None else back[q] + term

        def tiles(row):
            return [row[:, i : i + LANES] for i in range(0, row.shape[1], LANES)]

        row_levels = {0: 1}
        row_levels.update({level: 4 for level in range(1, levels, 4)})
        send_one[...] = upper
        copies = exchange(cycle, send_one, recv_one, one_targets, one_send_sem, one_recv_sem)
        spread(0, own * live_ref[:, 0:LANES])
        for copy in copies:
            copy.wait()
        upper = level_sum(upper, recv_one, cycle, n_gy, 0)
        send_two[...] = upper[:, split:]
        copies = exchange(cycle, send_two, recv_two, two_targets, two_send_sem, two_recv_sem)
        for i, row in enumerate(tiles(upper[:, :split] * live_ref[:, LANES : LANES + split])):
            spread(1 + 4 * i, row)
        for copy in copies:
            copy.wait()
        top = level_sum(upper[:, split:], recv_two, cycle, n_gx, 0)
        for i, row in enumerate(tiles(top * live_ref[:, LANES + split : LANES + wide])):
            spread(1 + split // XCOLS + 4 * i, row)
        back = [jnp.sum(total, axis=0, keepdims=True) for total in back]
        split_t = exact_rows(jnp.concatenate(back, axis=0), perm_ref[1])
        for ex in range(EX):
            by_v = []
            for v in range(2):
                by_u = []
                for u in range(2):
                    q = (v * 2 + u) * EX + ex
                    by_u.append(
                        split_t[q : q + 1, :LANES] * tab_ref[36]
                        + split_t[q : q + 1, LANES:] * tab_ref[37]
                    )
                by_v.append(
                    jnp.concatenate(
                        [
                            by_u[0] * float(interp[b, 0]) + by_u[1] * float(interp[b, 1])
                            for b in range(NODES)
                        ],
                        axis=0,
                    )
                )
            for a in range(NODES):
                u_ref[ex, a] = winv_ref[a] * (
                    by_v[0] * float(interp[a, 0]) + by_v[1] * float(interp[a, 1])
                )

    center = 0.5 * (bound_high + bound_low)
    radius = 0.5 * (bound_high - bound_low)
    ratio = center / radius
    rho_old = 1.0 / ratio
    rho_new = 1.0 / (2.0 * ratio - rho_old)

    own_pairs(u_ref)
    pl.semaphore_wait(barrier, len(everyone))
    copies = send_faces(1, 1)
    for copy in geom_copies:
        copy.start()
    winv_ref[...] = (edge[:, None] * edge[None] * zmask[None, None]).reshape(8, 64, LANES)
    for ex in range(EX):
        ax, ay, az = metrics(*[geom_ref[2 * dim + ex : 2 * dim + ex + 1] for dim in range(3)])
        in_x = lam_i * ax[None]
        in_y = lam_j * ay[None]
        in_z = lam_k * az
        spectrum = (in_x[:, None] + in_y[None] + in_z[None, None]).reshape(8, 64, LANES)
        shift = shift_ratio * (ax + ay + az)
        lam_ref[ex] = spectrum
        inv_ref[ex] = 1.0 / (spectrum + shift[None])
    x_ref[...] = jnp.zeros_like(x_ref)
    slots = lambda values: jnp.where(
        lane2 < EZ,
        values[0],
        jnp.where(lane2 < 2 * EZ, values[1], jnp.where(lane2 < 3 * EZ, values[2], values[3])),
    )
    own = []
    for dim in range(3):
        low, high = (geom_ref[2 * dim + ex : 2 * dim + ex + 1] for ex in range(EX))
        own.append([low, high, slots([low, roll(high, EZ), roll(low, -EZ), high])])
    for part in range(3):
        ax, ay, az = metrics(*[own[dim][part] for dim in range(3)])
        at = slice(part * LANES, (part + 1) * LANES)
        normal, along = (ay, ax) if part == 2 else (ax, ay)
        own_lam[:, at] = ((lam_j * along[None]) + (lam_k * az)[None]).reshape(64, LANES)
        own_normal[:, at] = (w_node * w_c[None] * normal[None]).reshape(64, LANES)
    receive_faces(1, copies)
    r_ref[...] = u_ref[...]
    for copy in geom_copies:
        copy.wait()

    def ghost(source, dim, ex):
        return recv_g[source, 2 * dim + ex : 2 * dim + ex + 1]

    outer = []
    for dim in range(3):
        y_side = slots(
            [
                roll(ghost(FROM_DOWN, dim, 0), EZ),
                roll(ghost(FROM_DOWN, dim, 1), 2 * EZ),
                roll(ghost(FROM_UP, dim, 0), 2 * EZ),
                roll(ghost(FROM_UP, dim, 1), 3 * EZ),
            ]
        )
        outer.append([ghost(FROM_LEFT, dim, 1), ghost(FROM_RIGHT, dim, 0), y_side])
    for part in range(3):
        ax, ay, az = metrics(*[outer[dim][part] for dim in range(3)])
        at = slice(part * LANES, (part + 1) * LANES)
        normal, along = (ay, ax) if part == 2 else (ax, ay)
        face_lam[:, at] = ((lam_j * along[None]) + (lam_k * az)[None]).reshape(64, LANES)
        face_normal[:, at] = (w_node * w_c[None] * normal[None]).reshape(64, LANES)
    for side, (low, high, ex) in enumerate(
        ((FROM_LEFT_DOWN, FROM_LEFT_UP, 1), (FROM_RIGHT_DOWN, FROM_RIGHT_UP, 0))
    ):
        lengths = [
            jnp.where(
                lane2 < 2 * EZ,
                roll(ghost(low, dim, ex), EZ),
                roll(ghost(high, dim, ex), -EZ),
            )
            for dim in range(3)
        ]
        ax, ay, az = metrics(*lengths)
        line_tab[side, 0] = w_end * w_c * ax
        line_tab[side, 1] = w_end * w_c * ay
        line_tab[side, 2] = jnp.broadcast_to(w_end * w_end * az, (8, LANES))

    for load in later_loads:
        load.wait()

    def step(index, carry):
        phase = lax.rem(index, SMOOTH)
        cycle = lax.div(index, SMOOTH)
        slot = lax.rem(index, 2)
        is_coarse = phase == 2
        second = (phase == 1) | (phase == 4)

        @pl.when(is_coarse)
        def _():
            coarse(cycle)

        @pl.when(jnp.logical_not(is_coarse))
        def _():
            keep = jnp.where(second, rho_new * rho_old, 0.0)
            take = jnp.where(second, 2.0 * rho_new / radius, 1.0 / center)
            smoother(keep, take)

        own_pairs(u_ref)
        copies = send_faces(slot, 2)

        stiffness()
        receive_faces(slot, copies)
        for ex in range(EX):
            x_ref[ex] += u_ref[ex]
        add_outer(*outer_terms(slot))
        own_pairs(w_ref)
        for ex in range(EX):
            r_ref[ex] -= free_scaled(w_ref[ex])
        return carry

    last = SMOOTH * CYCLES - 1
    lax.fori_loop(0, last, step, 0)
    smoother(rho_new * rho_old, 2.0 * rho_new / radius)
    own_pairs(u_ref)
    receive_faces(last % 2, send_faces(last % 2, 1))
    for ex in range(EX):
        x_ref[ex] += u_ref[ex]

    by_node = [
        [
            jnp.concatenate(
                [x_ref[ex, a, pl.ds(c, 8, stride=8)] for a in range(NODES)], axis=0
            )
            for c in range(NODES)
        ]
        for ex in range(EX)
    ]
    rows = []
    for ex in range(EX):
        for ey in range(EY):
            halves = []
            for half in range(2):
                joined = None
                for s in range(4):
                    part = roll(by_node[ex][half * 4 + s], EZ * (s - ey))
                    joined = part if s == 0 else jnp.where(lane2 >= EZ * s, part, joined)
                halves.append(joined)
            rows.append(jnp.concatenate(halves, axis=1))
    result = exact_rows(jnp.concatenate(rows, axis=0), perm_ref[3])
    for half in range(2):
        at = slice(half * LANES, (half + 1) * LANES)
        for k in range(EX * EY):
            for a in range(NODES):
                first = k * 64 + a * 8
                w_ref[half, a, pl.ds(k, 8, stride=8)] = result[first : first + 8, at]
    for half in range(2):
        at = slice(half * LANES, (half + 1) * LANES)
        out_ref[:, :, at] = w_ref[half].reshape(128, EY, LANES)


def per_device(source, geometry, disc_mask, thrust, xxt_factor, col_count):
    n_gx = lax.axis_size("gx")
    n_gy = lax.axis_size("gy")
    levels = xxt_factor.shape[0]
    wide = (levels - 1) * XCOLS
    split = (n_gy.bit_length() - 1) * XCOLS
    matrices, plane, table, perms, interp, stiff, weights = constant_tables()
    field = (EX, NODES, 64, LANES)
    f32 = jnp.float32
    out = pl.pallas_call(
        functools.partial(kernel, n_gx, n_gy, levels, interp, stiff, weights),
        out_shape=jax.ShapeDtypeStruct((NODES * NODES * EX, EY, EZ * NODES), f32),
        in_specs=[pl.BlockSpec(memory_space=pl.ANY)] * 10,
        out_specs=pl.BlockSpec(memory_space=pltpu.VMEM),
        scratch_shapes=[
            pltpu.VMEM((NODES * NODES * EX, EY, EZ * NODES), f32),
            pltpu.VMEM(geometry.shape, f32),
            pltpu.VMEM(disc_mask.shape, jnp.int32),
            pltpu.VMEM(thrust.shape, f32),
            pltpu.VMEM((1, levels), jnp.int32),
            pltpu.VMEM(plane.shape, jnp.bfloat16),
            pltpu.VMEM(table.shape, f32),
            pltpu.VMEM(perms.shape, jnp.bfloat16),
            pltpu.VMEM((8, LANES), f32),
            pltpu.VMEM((1, LANES + wide), f32),
            pltpu.VMEM(field, f32),
            pltpu.VMEM(field, f32),
            pltpu.VMEM(field, f32),
            pltpu.VMEM(field, f32),
            pltpu.VMEM(field[1:], f32),
            pltpu.VMEM(field[1:], f32),
            pltpu.VMEM(field, f32),
            pltpu.VMEM(field, f32),
            pltpu.VMEM((64, 3 * LANES), f32),
            pltpu.VMEM((64, 3 * LANES), f32),
            pltpu.VMEM((64, 3 * LANES), f32),
            pltpu.VMEM((64, 3 * LANES), f32),
            pltpu.VMEM((2, 3, 8, LANES), f32),
            pltpu.VMEM((levels * XCOLS, xxt_factor.shape[2]), f32),
            pltpu.VMEM(matrices.shape, jnp.bfloat16),
            pltpu.VMEM((2, 2, 2, 64, LANES), f32),
            pltpu.VMEM((2, 2, 8, 8, LANES), f32),
            pltpu.VMEM((2, 4, 8, LANES), f32),
            pltpu.VMEM((2, 2, 2, 64, LANES), f32),
            pltpu.VMEM((2, 2, 2, 8, 8, LANES), f32),
            pltpu.VMEM((2, 4, 8, LANES), f32),
            pltpu.VMEM((8, 8, LANES), f32),
            pltpu.VMEM((1, wide), f32),
            pltpu.VMEM((CYCLES, n_gy - 1, 1, wide), f32),
            pltpu.VMEM((1, wide - split), f32),
            pltpu.VMEM((CYCLES, n_gx - 1, 1, wide - split), f32),
            pltpu.SemaphoreType.DMA((2, 8)),
            pltpu.SemaphoreType.DMA((2, 8)),
            pltpu.SemaphoreType.DMA((8,)),
            pltpu.SemaphoreType.DMA((8,)),
            pltpu.SemaphoreType.DMA((n_gy - 1,)),
            pltpu.SemaphoreType.DMA((CYCLES, n_gy - 1)),
            pltpu.SemaphoreType.DMA((n_gx - 1,)),
            pltpu.SemaphoreType.DMA((CYCLES, n_gx - 1)),
            pltpu.SemaphoreType.DMA((10,)),
        ],
        compiler_params=pltpu.CompilerParams(
            collective_id=0, has_side_effects=True, vmem_limit_bytes=56 * 1024 * 1024
        ),
    )(
        source.reshape(NODES * NODES * EX, EY, EZ * NODES),
        geometry,
        disc_mask,
        thrust,
        col_count.T,
        xxt_factor.reshape(levels * XCOLS, xxt_factor.shape[2]),
        jnp.asarray(matrices),
        jnp.asarray(plane),
        jnp.asarray(table),
        jnp.asarray(perms),
    )
    return out.reshape(source.shape)


def solution(mesh):
    return jax.shard_map(
        per_device,
        mesh=mesh,
        in_specs=(
            P(None, None, "gx", "gy", None),
            P(None, "gx", "gy", None),
            P("gx", "gy", None),
            P("gx", "gy", None),
            P(None, None, ("gx", "gy")),
            P(None, ("gx", "gy")),
        ),
        out_specs=P(None, None, "gx", "gy", None),
        check_vma=False,
    )
```

```python
import functools
import math

import jax
import jax.numpy as jnp
import ml_dtypes
import numpy as np
from jax import lax
from jax.experimental import pallas as pl
from jax.experimental.pallas import tpu as pltpu
from jax.sharding import PartitionSpec as P

NODES = 8
CYCLES = 2
EX = 2
EY = 4
EZ = 32
LANES = EY * EZ
XCOLS = 32
SMOOTH = 5

bound_low = 0.3
bound_high = 3.0
shift_ratio = 0.25
MESH = pl.DeviceIdType.MESH


def legendre_table(points, poly_order):
    table = [points * 0.0 + 1.0, points]
    for degree in range(2, poly_order + 1):
        table.append(
            ((2.0 * degree - 1.0) * points * table[-1] - (degree - 1.0) * table[-2]) / degree
        )
    return table


def jacobi_eigen(matrix):
    size_n = matrix.shape[0]
    current = matrix.copy()
    vectors = np.eye(size_n)
    for sweep_index in range(30):
        for first in range(size_n - 1):
            for second in range(first + 1, size_n):
                angle = 0.5 * math.atan2(
                    2.0 * float(current[first, second]),
                    float(current[second, second] - current[first, first]),
                )
                rotation = np.eye(size_n)
                rotation[first, first] = math.cos(angle)
                rotation[second, second] = math.cos(angle)
                rotation[first, second] = math.sin(angle)
                rotation[second, first] = -math.sin(angle)
                current = rotation.T @ current @ rotation
                vectors = vectors @ rotation
    values = np.array([current[index, index] for index in range(size_n)])
    order = np.argsort(values)
    return (values[order], vectors[:, order])


def gll_tables(node_count):
    poly_order = node_count - 1
    points = np.cos(np.pi * np.arange(node_count) / poly_order)
    for newton_index in range(200):
        table = legendre_table(points, poly_order)
        points = points - (points * table[poly_order] - table[poly_order - 1]) / (
            node_count * table[poly_order]
        )
    points = points[::-1].copy()
    legendre = legendre_table(points, poly_order)[poly_order]
    weights = 2.0 / (poly_order * (poly_order + 1) * legendre**2)
    identity = np.eye(node_count)
    gap_matrix = points[:, None] - points[None, :] + identity
    off_diagonal = legendre[:, None] / (legendre[None, :] * gap_matrix) * (1.0 - identity)
    end_value = poly_order * (poly_order + 1) / 4.0
    end_terms = np.concatenate([[-end_value], np.zeros(node_count - 2), [end_value]])
    derivative = off_diagonal + identity * end_terms[None, :]
    stiffness = derivative.T @ (weights[:, None] * derivative)
    root_inverse = 1.0 / np.sqrt(weights)
    symmetric = root_inverse[:, None] * stiffness * root_inverse[None, :]
    symmetric = 0.5 * (symmetric + symmetric.T)
    eigen_values, eigen_vectors = jacobi_eigen(symmetric)
    eigen_modes = root_inverse[:, None] * eigen_vectors
    vertex_interp = np.stack([(1.0 - points) / 2.0, (1.0 + points) / 2.0], axis=1)
    return weights, stiffness, eigen_modes, eigen_values, vertex_interp


def mode_order(modes):
    even = [i for i in range(NODES) if modes[0, i] * modes[NODES - 1, i] > 0.0]
    odd = [i for i in range(NODES) if i not in even]
    return even, odd


def split_pair(matrix):
    exact = matrix.astype(np.float32)
    high = exact.astype(ml_dtypes.bfloat16)
    low = (exact - high.astype(np.float32)).astype(ml_dtypes.bfloat16)
    return np.concatenate([high, high, low], axis=1)


def constant_tables():
    weights, stiffness, modes, values, interp = gll_tables(NODES)
    even, odd = mode_order(modes)
    half = NODES // 2
    mats = []
    for chosen in (even, odd):
        inverse = np.kron(modes[:half][:, chosen], np.kron(modes, modes))
        mats.append((split_pair(inverse.T), split_pair(inverse)))
    matrices = np.stack([mats[0][0], mats[1][0], mats[0][1], mats[1][1]])
    plane = np.kron(modes, modes)
    plane_matrices = np.stack([split_pair(plane.T), split_pair(plane)])
    full = np.ones((NODES, LANES))
    edge = np.ones(NODES)
    edge[0] = edge[-1] = 0.5
    ez = np.arange(LANES)[None, :] % EZ
    node = np.arange(NODES)[:, None]
    z_shared = 1.0 + ((node == 0) & (ez > 0)) + ((node == NODES - 1) & (ez < EZ - 1))
    free = 1.0 - ((node == NODES - 1) & (ez == EZ - 1))
    rows = [values[i] * full for i in even + odd]
    rows += [value * full for value in values]
    rows += [weight * full for weight in weights]
    rows += [value * full for value in edge]
    rows += [values[:, None] * full, weights[:, None] * full, free / z_shared, free * full]
    rows += [interp[:, 0:1] * full, interp[:, 1:2] * full]
    rows += [stiffness[:, c : c + 1] * full for c in range(NODES)]
    low_side = np.arange(LANES)[None, :] < LANES // 2
    rows += [
        np.where(low_side, stiffness[b, 0], stiffness[b, NODES - 1]) * full for b in range(NODES)
    ]
    table = np.stack(rows).astype(np.float32)
    perm = np.zeros((2 * LANES, 2 * LANES), np.float32)
    for t in range(2):
        for element in range(LANES):
            perm[t * LANES + element, 2 * element + t] = 1.0
    order = np.zeros((EZ * NODES, EZ * NODES), np.float32)
    for c in range(NODES):
        for element in range(EZ):
            order[element * NODES + c, c * EZ + element] = 1.0
    perms = np.stack([perm, perm.T, order, order.T]).astype(ml_dtypes.bfloat16)
    return (
        matrices,
        plane_matrices,
        table,
        perms,
        interp.astype(np.float32),
        stiffness.astype(np.float32),
        weights.astype(np.float32),
    )


def flipped(index, bits):
    out = index
    bit = 1
    while bit <= bits:
        if bits & bit:
            out = out + bit - 2 * bit * lax.rem(lax.div(index, bit), 2)
        bit *= 2
    return out


def exact_rows(value, perm):
    first = value.astype(jnp.bfloat16)
    rest = value - first.astype(jnp.float32)
    second = rest.astype(jnp.bfloat16)
    third = (rest - second.astype(jnp.float32)).astype(jnp.bfloat16)
    parts = [
        jnp.dot(part, perm, preferred_element_type=jnp.float32)
        for part in (first, second, third)
    ]
    return parts[0] + parts[1] + parts[2]


def kernel(
    n_gx,
    n_gy,
    levels,
    interp,
    stiff,
    weights,
    source_hbm,
    lengths_hbm,
    disc_hbm,
    thrust_hbm,
    count_hbm,
    x_hbm,
    mat_hbm,
    plane_hbm,
    tab_hbm,
    perm_hbm,
    out_ref,
    source_ref,
    lengths_ref,
    disc_ref,
    thrust_ref,
    count_ref,
    plane_ref,
    tab_ref,
    perm_ref,
    geom_ref,
    live_ref,
    u_ref,
    r_ref,
    w_ref,
    x_ref,
    weight_ref,
    winv_ref,
    lam_ref,
    inv_ref,
    face_lam,
    face_normal,
    own_lam,
    own_normal,
    line_tab,
    x_factor_ref,
    mat_ref,
    send_x,
    send_y,
    send_c,
    recv_x,
    recv_y,
    recv_c,
    recv_g,
    send_one,
    recv_one,
    send_two,
    recv_two,
    send_sem,
    recv_sem,
    g_send_sem,
    g_recv_sem,
    one_send_sem,
    one_recv_sem,
    two_send_sem,
    two_recv_sem,
    load_sem,
):
    me_x = lax.axis_index("gx")
    me_y = lax.axis_index("gy")
    left = lax.rem(me_x + n_gx - 1, n_gx)
    right = lax.rem(me_x + 1, n_gx)
    down = lax.rem(me_y + n_gy - 1, n_gy)
    up = lax.rem(me_y + 1, n_gy)
    targets = [
        (left, me_y),
        (right, me_y),
        (me_x, down),
        (me_x, up),
        (left, down),
        (right, up),
        (left, up),
        (right, down),
    ]
    FROM_RIGHT, FROM_LEFT, FROM_UP, FROM_DOWN = 0, 1, 2, 3
    FROM_RIGHT_UP, FROM_LEFT_DOWN, FROM_RIGHT_DOWN, FROM_LEFT_UP = 4, 5, 6, 7
    one_targets = [(me_x, flipped(me_y, off)) for off in range(1, n_gy)]
    two_targets = [(flipped(me_x, off), me_y) for off in range(1, n_gx)]
    barrier = pltpu.get_barrier_semaphore()
    everyone = targets + one_targets + two_targets
    for target in everyone:
        pl.semaphore_signal(barrier, inc=1, device_id=target, device_id_type=MESH)
    loads = [
        pltpu.make_async_copy(src, dst, load_sem.at[index])
        for index, (src, dst) in enumerate(
            (
                (tab_hbm, tab_ref),
                (source_hbm, source_ref),
                (perm_hbm, perm_ref),
                (lengths_hbm, lengths_ref),
                (disc_hbm, disc_ref),
                (thrust_hbm, thrust_ref),
                (count_hbm, count_ref),
                (mat_hbm, mat_ref),
                (plane_hbm, plane_ref),
                (x_hbm, x_factor_ref),
            )
        )
    ]
    for load in loads:
        load.start()
    first_loads, later_loads = loads[:7], loads[7:]

    lane = lax.broadcasted_iota(jnp.int32, (1, 1, 1, LANES), 3)
    lane3 = lax.broadcasted_iota(jnp.int32, (1, 1, LANES), 2)
    lane2 = lax.broadcasted_iota(jnp.int32, (1, LANES), 1)
    z2 = lax.rem(lane2, EZ)

    def roll(value, shift):
        shift = shift % LANES
        return value if shift == 0 else pltpu.roll(value, shift, value.ndim - 1)

    for load in first_loads:
        load.wait()
    for dim in range(3):
        for ex in range(EX):
            geom_ref[2 * dim + ex : 2 * dim + ex + 1] = jnp.concatenate(
                [lengths_ref[dim, ex, ey : ey + 1] for ey in range(EY)], axis=1
            )
    geom_ref[6:8] = jnp.ones((2, LANES), jnp.float32)
    forces = []
    for ex in range(EX):
        element = disc_ref[ex].astype(jnp.float32) * thrust_ref[ex]
        forces.append(
            jnp.concatenate([element[ey : ey + 1] for ey in range(EY)], axis=1)
        )
    column = lax.rem(lane2, XCOLS)
    for first in range(0, levels, LANES // XCOLS):
        chosen = [0] * 4 if first == 0 else range(first - 3, first + 1)
        count = None
        for place, level in enumerate(chosen):
            one = jnp.broadcast_to(count_ref[:, level : level + 1], (1, LANES))
            count = one if count is None else jnp.where(lane2 >= XCOLS * place, one, count)
        at = slice(first // 4 * LANES, (first // 4 + 1) * LANES)
        live_ref[:, at] = (column < count).astype(jnp.float32)
    lam_i = tab_ref[0:8]
    lam_j = tab_ref[8:16]
    w_node = tab_ref[16:24]
    edge = tab_ref[24:32]
    lam_k = tab_ref[32]
    w_c = tab_ref[33]
    zmask = tab_ref[34]
    free = tab_ref[35]
    w_end = float(weights[0])
    k_end = float(stiff[0, 0])
    weight_ref[...] = (w_node[:, None] * w_node[None] * w_c[None, None]).reshape(8, 64, LANES)

    def metrics(hx, hy, hz):
        return hy * hz / (2.0 * hx), hx * hz / (2.0 * hy), hx * hy / (2.0 * hz)

    for half in range(2):
        at = slice(half * LANES, (half + 1) * LANES)
        w_ref[half] = source_ref[:, :, at].reshape(8, 64, LANES)
    by_node = exact_rows(
        jnp.concatenate(
            [
                jnp.concatenate(
                    [w_ref[half, a, pl.ds(k, 8, stride=8)] for half in range(2)], axis=1
                )
                for k in range(EX * EY)
                for a in range(NODES)
            ],
            axis=0,
        ),
        perm_ref[2],
    )
    for ex in range(EX):
        for c in range(NODES):
            at = slice(c // 4 * LANES, (c // 4 + 1) * LANES)
            joined = None
            for ey in range(EY):
                first = (ex * EY + ey) * 64
                part = roll(by_node[first : first + 64, at], EZ * (ey - c % 4))
                joined = part if ey == 0 else jnp.where(lane2 >= EZ * ey, part, joined)
            for a in range(NODES):
                u_ref[ex, a, pl.ds(c, 8, stride=8)] = joined[8 * a : 8 * a + 8]

    for ex in range(EX):
        hx = geom_ref[ex : ex + 1]
        hy = geom_ref[2 + ex : 3 + ex]
        hz = geom_ref[4 + ex : 5 + ex]
        mass = (hx * hy * hz / 8.0)[None] * weight_ref[...]
        u_ref[ex] = mass * (u_ref[ex] + forces[ex][None])

    def free_scaled(value):
        return (value.reshape(8, 8, 8, LANES) * free[None, None]).reshape(8, 64, LANES)

    for ex in range(EX):
        u_ref[ex] = free_scaled(u_ref[ex])

    geom_copies = []
    for index, target in enumerate(targets):
        copy = pltpu.make_async_remote_copy(
            src_ref=geom_ref,
            dst_ref=recv_g.at[index],
            send_sem=g_send_sem.at[index],
            recv_sem=g_recv_sem.at[index],
            device_id=target,
            device_id_type=MESH,
        )
        geom_copies.append(copy)

    def own_pairs(ref):
        shared = ref[0, 7] + ref[1, 0]
        ref[0, 7] = shared
        ref[1, 0] = shared
        low = ref[:, :, 0:8]
        high = ref[:, :, 56:64]
        ref[:, :, 0:8] = low + jnp.where(lane >= EZ, roll(high, EZ), 0.0)
        ref[:, :, 56:64] = high + jnp.where(lane < LANES - EZ, roll(low, -EZ), 0.0)
        for ex in range(EX):
            for a in range(NODES):
                low = ref[ex, a, pl.ds(0, 8, stride=8)]
                high = ref[ex, a, pl.ds(7, 8, stride=8)]
                ref[ex, a, pl.ds(0, 8, stride=8)] = low + jnp.where(
                    z2 > 0, roll(high, 1), 0.0
                )
                ref[ex, a, pl.ds(7, 8, stride=8)] = high + jnp.where(
                    z2 < EZ - 1, roll(low, -1), 0.0
                )

    def packed_y(down_faces, up_faces):
        return jnp.where(
            lane3 < EZ,
            down_faces[0],
            jnp.where(
                lane3 < 2 * EZ,
                roll(down_faces[1], EZ),
                jnp.where(lane3 < 3 * EZ, roll(up_faces[0], -EZ), up_faces[1]),
            ),
        )

    def y_faces():
        return packed_y(
            [u_ref[ex, :, 0:8] for ex in range(EX)], [u_ref[ex, :, 56:64] for ex in range(EX)]
        )

    def weighted(parts, row):
        total = None
        for index, part in parts:
            term = part * float(stiff[row, index])
            total = term if total is None else total + term
        return total

    def send_faces(slot, planes):
        copies = [None] * 8

        def start(index, source, landing):
            copies[index] = pltpu.make_async_remote_copy(
                src_ref=source,
                dst_ref=landing,
                send_sem=send_sem.at[slot, index],
                recv_sem=recv_sem.at[slot, index],
                device_id=targets[index],
                device_id_type=MESH,
            )
            copies[index].start()

        corners = ((0, 0, 0), (1, 7, 7), (0, 0, 7), (1, 7, 0))
        if planes > 1:
            low = weighted([(a, u_ref[0, a]) for a in range(1, NODES)], 0)
            high = weighted([(a, u_ref[1, a]) for a in range(NODES - 1)], 7)
        for i, (ex, a, b) in enumerate(corners):
            ey = 0 if b == 0 else EY - 1
            line = roll(u_ref[ex, a, 8 * b : 8 * b + 8], -EZ * ey)
            if planes > 1:
                along_x = (high if ex else low)[8 * b : 8 * b + 8]
                others = [other for other in range(NODES) if other != b]
                along_y = weighted(
                    [(other, u_ref[ex, a, 8 * other : 8 * other + 8]) for other in others], b
                )
                line = jnp.where(
                    lane2 < EZ,
                    line,
                    jnp.where(
                        lane2 < 2 * EZ,
                        roll(along_x, EZ * (1 - ey)),
                        roll(along_y, EZ * (2 - ey)),
                    ),
                )
            send_c[slot, i] = line
        for i in range(4):
            start(4 + i, send_c.at[slot, i], recv_c.at[slot, i])
        send_x[slot, 0, 0] = u_ref[0, 0]
        send_x[slot, 1, 0] = u_ref[1, 7]
        if planes > 1:
            send_x[slot, 0, 1] = low
            send_x[slot, 1, 1] = high
        both = pl.ds(0, planes)
        for i in range(2):
            start(i, send_x.at[slot, i, both], recv_x.at[slot, i, both])
        send_y[slot, 0] = y_faces()
        if planes > 1:
            down_normal, up_normal = [], []
            for ex in range(EX):
                rows = [u_ref[ex, :, 8 * b : 8 * b + 8] for b in range(NODES)]
                down_normal.append(weighted([(b, rows[b]) for b in range(1, NODES)], 0))
                up_normal.append(weighted([(b, rows[b]) for b in range(NODES - 1)], 7))
            send_y[slot, 1] = packed_y(down_normal, up_normal)
        for i in range(2):
            start(2 + i, send_y.at[slot, both], recv_y.at[slot, i, both])
        return copies

    def receive_faces(slot, copies, refs):
        for copy in copies[2:4]:
            copy.wait()
        for ref in refs:
            add_y(ref, arrived_y(slot, 0))
        for copy in copies[0:2]:
            copy.wait()
        for ref in refs:
            ref[1, 7] += recv_x[slot, FROM_RIGHT, 0]
            ref[0, 0] += recv_x[slot, FROM_LEFT, 0]
        for copy in copies[4:8]:
            copy.wait()
        for index, (ex, a, first, to_ey) in enumerate(
            ((1, 7, 56, EY - 1), (0, 0, 0, 0), (1, 7, 0, 0), (0, 0, 56, EY - 1))
        ):
            line = in_slot(roll(recv_c[slot, index], EZ * to_ey), to_ey)
            for ref in refs:
                ref[ex, a, first : first + 8] += line

    def arrived_y(slot, plane):
        from_up = recv_y[slot, FROM_UP - 2, plane]
        from_down = recv_y[slot, FROM_DOWN - 2, plane]
        return roll(jnp.where(lane3 >= 2 * EZ, from_down, from_up), 2 * EZ)

    def add_y(ref, plane):
        for ex in range(EX):
            ref[ex, :, 0:8] += jnp.where(lane3 < EZ, roll(plane, -EZ * ex), 0.0)
            ref[ex, :, 56:64] += jnp.where(
                lane3 >= 3 * EZ, roll(plane, EZ * (1 - ex)), 0.0
            )

    def in_slot(value, slot):
        return jnp.where((lane2 >= EZ * slot) & (lane2 < EZ * (slot + 1)), value, 0.0)

    def outer_terms(slot):
        face = jnp.concatenate(
            [u_ref[0, 0], u_ref[1, 7], y_faces().reshape(64, LANES)], axis=1
        )
        from_left_down = recv_c[slot, FROM_LEFT_DOWN - 4]
        from_left_up = recv_c[slot, FROM_LEFT_UP - 4]
        from_right_down = recv_c[slot, FROM_RIGHT_DOWN - 4]
        from_right_up = recv_c[slot, FROM_RIGHT_UP - 4]
        sides = []
        for plane, low, high in (
            (recv_x[slot, FROM_LEFT, 1], from_left_down, from_left_up),
            (recv_x[slot, FROM_RIGHT, 1], from_right_down, from_right_up),
        ):
            sides.append(
                jnp.concatenate(
                    [
                        plane[0:8] + in_slot(roll(low, -EZ), 0),
                        plane[8:56],
                        plane[56:64] + in_slot(roll(high, 2 * EZ), 3),
                    ],
                    axis=0,
                )
            )
        normal_y = arrived_y(slot, 1)
        first = (
            normal_y[0]
            + in_slot(roll(from_left_down, -2 * EZ), 0)
            + in_slot(from_left_up, 2)
        )
        last = (
            normal_y[7]
            + in_slot(roll(from_right_down, -EZ), 1)
            + in_slot(roll(from_right_up, EZ), 3)
        )
        normal_y = jnp.concatenate([first[None], normal_y[1:7], last[None]], axis=0)
        normal = jnp.concatenate([sides[0], sides[1], normal_y.reshape(64, LANES)], axis=1)
        weight = weight_ref[0] * (1.0 / w_end)
        weight = jnp.concatenate([weight] * 3, axis=1)
        odd_ex = lax.rem(lax.div(lane2, EZ), 2) == 1
        arrived = y_faces() - send_y[slot, 0]
        arrived = jnp.concatenate(
            [
                jnp.where(odd_ex, arrived[0], 0.0)[None],
                arrived[1:7],
                jnp.where(odd_ex, 0.0, arrived[7])[None],
            ],
            axis=0,
        )
        arrived = jnp.concatenate(
            [
                u_ref[0, 0] - send_x[slot, 0, 0],
                u_ref[1, 7] - send_x[slot, 1, 0],
                arrived.reshape(64, LANES),
            ],
            axis=1,
        )
        modes = small_product(
            0, jnp.concatenate([weight * face, weight * arrived], axis=1)
        )
        width = 3 * LANES
        modes = face_lam[...] * modes[:, :width] + own_lam[...] * modes[:, width:]
        spread = small_product(1, modes)
        inward = own_normal[...] * arrived
        result = face_normal[...] * (normal + k_end * face) + w_end * weight * spread
        lines = []
        for side in range(2):
            plane = face[:, side * LANES : (side + 1) * LANES]
            value = jnp.where(lane2 < 2 * EZ, plane[0:8], plane[56:64])
            along_x = jnp.where(lane2 < 2 * EZ, sides[side][0:8], sides[side][56:64])
            edge_y = last if side else first
            along_y = jnp.where(
                lane2 < 2 * EZ,
                roll(edge_y, -EZ) if side else edge_y,
                edge_y if side else roll(edge_y, EZ),
            )
            along_z = None
            for c in range(NODES):
                term = tab_ref[38 + c] * value[c : c + 1]
                along_z = term if along_z is None else along_z + term
            lines.append(
                line_tab[side, 0] * (along_x + k_end * value)
                + line_tab[side, 1] * (along_y + k_end * value)
                + line_tab[side, 2] * along_z
            )
        return result, lines, inward

    def add_outer(result, lines, inward):
        inward_y = inward[:, 2 * LANES :].reshape(8, 8, LANES)
        for ex in range(EX):
            inward_x = inward[:, ex * LANES : (ex + 1) * LANES]
            along = jnp.where(
                lane3 < EZ,
                roll(inward_y, -EZ * ex),
                jnp.where(lane3 >= 3 * EZ, roll(inward_y, EZ * (1 - ex)), 0.0),
            )
            for a in range(NODES):
                terms = (along[a][None] * tab_ref[46:54]).reshape(64, LANES)
                w_ref[ex, a] += terms + inward_x * float(stiff[a, 7 * ex])
        for side, (ex, a) in enumerate(((0, 0), (1, 7))):
            w_ref[ex, a] += result[:, side * LANES : (side + 1) * LANES]
            w_ref[ex, a, 0:8] += in_slot(lines[side], 0)
            w_ref[ex, a, 56:64] += in_slot(lines[side], 3)
        add_y(w_ref, result[:, 2 * LANES :].reshape(8, 8, LANES))

    def small_product(which, value):
        high = value.astype(jnp.bfloat16)
        low = (value - high.astype(jnp.float32)).astype(jnp.bfloat16)
        return jnp.dot(
            plane_ref[which],
            jnp.concatenate([high, low, high], axis=0),
            preferred_element_type=jnp.float32,
        )

    def product(which, value):
        high = value.astype(jnp.bfloat16)
        low = (value - high.astype(jnp.float32)).astype(jnp.bfloat16)
        return jnp.dot(
            mat_ref[which],
            jnp.concatenate([high, low, high], axis=0),
            preferred_element_type=jnp.float32,
        )

    def flat(parts):
        return jnp.concatenate([part.reshape(256, LANES) for part in parts], axis=1)

    def element_op(fields, diag_ref):
        even, odd = [], []
        for field in fields:
            low = field[0:4]
            high = jnp.concatenate([field[7:8], field[6:7], field[5:6], field[4:5]], axis=0)
            even.append(low + high)
            odd.append(low - high)
        even = product(0, flat(even)) * flat([diag_ref[ex, 0:4] for ex in range(EX)])
        odd = product(1, flat(odd)) * flat([diag_ref[ex, 4:8] for ex in range(EX)])
        even = product(2, even)
        odd = product(3, odd)
        out = []
        for ex in range(EX):
            at = slice(ex * LANES, (ex + 1) * LANES)
            e = even[:, at].reshape(4, 64, LANES)
            o = odd[:, at].reshape(4, 64, LANES)
            diff = e - o
            out.append(
                jnp.concatenate([e + o, diff[3:4], diff[2:3], diff[1:2], diff[0:1]], axis=0)
            )
        return out

    def stiffness():
        weight = weight_ref[...]
        out = element_op([u_ref[ex] * weight for ex in range(EX)], lam_ref)
        for ex in range(EX):
            w_ref[ex] = out[ex] * weight

    def smoother(keep, take):
        out = element_op([r_ref[ex] for ex in range(EX)], inv_ref)
        for ex in range(EX):
            u_ref[ex] = (take * out[ex] + keep * u_ref[ex]) * winv_ref[...]

    wide = (levels - 1) * XCOLS
    gy_bits = n_gy.bit_length() - 1
    split = gy_bits * XCOLS

    def exchange(cycle, send_ref, recv_ref, to, send_s, recv_s):
        copies = []
        for index, target in enumerate(to):
            copy = pltpu.make_async_remote_copy(
                src_ref=send_ref,
                dst_ref=recv_ref.at[cycle, index],
                send_sem=send_s.at[index],
                recv_sem=recv_s.at[cycle, index],
                device_id=target,
                device_id_type=MESH,
            )
            copy.start()
            copies.append(copy)
        return copies

    def level_sum(own, recv_ref, cycle, count, first_level_lane):
        which = lax.broadcasted_iota(jnp.int32, own.shape, 1)
        total = own
        start = 1
        bit = 0
        while start < count:
            part = recv_ref[cycle, start - 1]
            for index in range(start + 1, 2 * start):
                part = part + recv_ref[cycle, index - 1]
            total = total + jnp.where(which >= bit * XCOLS + first_level_lane, part, 0.0)
            start *= 2
            bit += 1
        return total

    def coarse(cycle):
        sums = {}
        for ex in range(EX):
            scaled = r_ref[ex] * winv_ref[...]
            for v in range(2):
                by_v = scaled[0] * float(interp[0, v])
                for a in range(1, NODES):
                    by_v = by_v + scaled[a] * float(interp[a, v])
                by_v = by_v.reshape(8, 8, LANES)
                for u in range(2):
                    by_u = by_v[0] * float(interp[0, u])
                    for b in range(1, NODES):
                        by_u = by_u + by_v[b] * float(interp[b, u])
                    for t in range(2):
                        sums[v, u, ex, t] = jnp.sum(
                            by_u * tab_ref[36 + t], axis=0, keepdims=True
                        )
        order = [(v, u, ex) for v in range(2) for u in range(2) for ex in range(EX)]
        split_t = jnp.concatenate(
            [jnp.concatenate([sums[key + (t,)] for t in range(2)], axis=1) for key in order],
            axis=0,
        )
        vector = exact_rows(split_t, perm_ref[0])
        pieces = []
        for level in range(levels):
            rows = slice(level * XCOLS, (level + 1) * XCOLS)
            acc = None
            for q in range(8):
                term = x_factor_ref[rows, q * 256 : (q + 1) * 256] * vector[q : q + 1]
                acc = term if acc is None else acc + term
            pieces.append(acc[:, :LANES] + acc[:, LANES:])
        def row_of(parts):
            block = jnp.concatenate(parts, axis=0)
            missing = LANES - block.shape[0]
            if missing:
                block = jnp.concatenate([block, jnp.zeros((missing, LANES), jnp.float32)], axis=0)
            return jnp.sum(block.T, axis=0, keepdims=True)
        own = row_of(pieces[0:1])
        upper = jnp.concatenate(
            [row_of(pieces[i : i + 4]) for i in range(1, levels, 4)], axis=1
        )[:, :wide]
        back = [None] * 8

        def spread(first_level, row):
            part = jnp.broadcast_to(row, (LANES, LANES)).T
            for q in range(8):
                for k in range(row_levels[first_level]):
                    level = first_level + k
                    col = part[k * XCOLS : (k + 1) * XCOLS]
                    block = x_factor_ref[
                        level * XCOLS : (level + 1) * XCOLS, q * 256 : (q + 1) * 256
                    ]
                    term = block * jnp.concatenate([col, col], axis=1)
                    back[q] = term if back[q] is None else back[q] + term

        def tiles(row):
            return [row[:, i : i + LANES] for i in range(0, row.shape[1], LANES)]

        row_levels = {0: 1}
        row_levels.update({level: 4 for level in range(1, levels, 4)})
        send_one[...] = upper
        copies = exchange(cycle, send_one, recv_one, one_targets, one_send_sem, one_recv_sem)
        spread(0, own * live_ref[:, 0:LANES])
        for copy in copies:
            copy.wait()
        upper = level_sum(upper, recv_one, cycle, n_gy, 0)
        send_two[...] = upper[:, split:]
        copies = exchange(cycle, send_two, recv_two, two_targets, two_send_sem, two_recv_sem)
        for i, row in enumerate(tiles(upper[:, :split] * live_ref[:, LANES : LANES + split])):
            spread(1 + 4 * i, row)
        for copy in copies:
            copy.wait()
        top = level_sum(upper[:, split:], recv_two, cycle, n_gx, 0)
        for i, row in enumerate(tiles(top * live_ref[:, LANES + split : LANES + wide])):
            spread(1 + split // XCOLS + 4 * i, row)
        back = [jnp.sum(total, axis=0, keepdims=True) for total in back]
        split_t = exact_rows(jnp.concatenate(back, axis=0), perm_ref[1])
        for ex in range(EX):
            by_v = []
            for v in range(2):
                by_u = []
                for u in range(2):
                    q = (v * 2 + u) * EX + ex
                    by_u.append(
                        split_t[q : q + 1, :LANES] * tab_ref[36]
                        + split_t[q : q + 1, LANES:] * tab_ref[37]
                    )
                by_v.append(
                    jnp.concatenate(
                        [
                            by_u[0] * float(interp[b, 0]) + by_u[1] * float(interp[b, 1])
                            for b in range(NODES)
                        ],
                        axis=0,
                    )
                )
            for a in range(NODES):
                u_ref[ex, a] = winv_ref[a] * (
                    by_v[0] * float(interp[a, 0]) + by_v[1] * float(interp[a, 1])
                )

    center = 0.5 * (bound_high + bound_low)
    radius = 0.5 * (bound_high - bound_low)
    ratio = center / radius
    rho_old = 1.0 / ratio
    rho_new = 1.0 / (2.0 * ratio - rho_old)

    own_pairs(u_ref)
    pl.semaphore_wait(barrier, len(everyone))
    copies = send_faces(1, 1)
    for copy in geom_copies:
        copy.start()
    winv_ref[...] = (edge[:, None] * edge[None] * zmask[None, None]).reshape(8, 64, LANES)
    for ex in range(EX):
        ax, ay, az = metrics(*[geom_ref[2 * dim + ex : 2 * dim + ex + 1] for dim in range(3)])
        in_x = lam_i * ax[None]
        in_y = lam_j * ay[None]
        in_z = lam_k * az
        spectrum = (in_x[:, None] + in_y[None] + in_z[None, None]).reshape(8, 64, LANES)
        shift = shift_ratio * (ax + ay + az)
        lam_ref[ex] = spectrum
        inv_ref[ex] = 1.0 / (spectrum + shift[None])
    x_ref[...] = jnp.zeros_like(x_ref)
    slots = lambda values: jnp.where(
        lane2 < EZ,
        values[0],
        jnp.where(lane2 < 2 * EZ, values[1], jnp.where(lane2 < 3 * EZ, values[2], values[3])),
    )
    own = []
    for dim in range(3):
        low, high = (geom_ref[2 * dim + ex : 2 * dim + ex + 1] for ex in range(EX))
        own.append([low, high, slots([low, roll(high, EZ), roll(low, -EZ), high])])
    for part in range(3):
        ax, ay, az = metrics(*[own[dim][part] for dim in range(3)])
        at = slice(part * LANES, (part + 1) * LANES)
        normal, along = (ay, ax) if part == 2 else (ax, ay)
        own_lam[:, at] = ((lam_j * along[None]) + (lam_k * az)[None]).reshape(64, LANES)
        own_normal[:, at] = (w_node * w_c[None] * normal[None]).reshape(64, LANES)
    receive_faces(1, copies, (u_ref,))
    r_ref[...] = u_ref[...]
    for copy in geom_copies:
        copy.wait()

    def ghost(source, dim, ex):
        return recv_g[source, 2 * dim + ex : 2 * dim + ex + 1]

    outer = []
    for dim in range(3):
        y_side = slots(
            [
                roll(ghost(FROM_DOWN, dim, 0), EZ),
                roll(ghost(FROM_DOWN, dim, 1), 2 * EZ),
                roll(ghost(FROM_UP, dim, 0), 2 * EZ),
                roll(ghost(FROM_UP, dim, 1), 3 * EZ),
            ]
        )
        outer.append([ghost(FROM_LEFT, dim, 1), ghost(FROM_RIGHT, dim, 0), y_side])
    for part in range(3):
        ax, ay, az = metrics(*[outer[dim][part] for dim in range(3)])
        at = slice(part * LANES, (part + 1) * LANES)
        normal, along = (ay, ax) if part == 2 else (ax, ay)
        face_lam[:, at] = ((lam_j * along[None]) + (lam_k * az)[None]).reshape(64, LANES)
        face_normal[:, at] = (w_node * w_c[None] * normal[None]).reshape(64, LANES)
    for side, (low, high, ex) in enumerate(
        ((FROM_LEFT_DOWN, FROM_LEFT_UP, 1), (FROM_RIGHT_DOWN, FROM_RIGHT_UP, 0))
    ):
        lengths = [
            jnp.where(
                lane2 < 2 * EZ,
                roll(ghost(low, dim, ex), EZ),
                roll(ghost(high, dim, ex), -EZ),
            )
            for dim in range(3)
        ]
        ax, ay, az = metrics(*lengths)
        line_tab[side, 0] = w_end * w_c * ax
        line_tab[side, 1] = w_end * w_c * ay
        line_tab[side, 2] = jnp.broadcast_to(w_end * w_end * az, (8, LANES))

    for load in later_loads:
        load.wait()

    def step(index, carry):
        phase = lax.rem(index, SMOOTH)
        cycle = lax.div(index, SMOOTH)
        slot = lax.rem(index, 2)
        is_coarse = phase == 2
        second = (phase == 1) | (phase == 4)

        @pl.when(is_coarse)
        def _():
            coarse(cycle)

        @pl.when(jnp.logical_not(is_coarse))
        def _():
            keep = jnp.where(second, rho_new * rho_old, 0.0)
            take = jnp.where(second, 2.0 * rho_new / radius, 1.0 / center)
            smoother(keep, take)

        own_pairs(u_ref)
        copies = send_faces(slot, 2)

        stiffness()
        for ex in range(EX):
            x_ref[ex] += u_ref[ex]
        receive_faces(slot, copies, (u_ref, x_ref))
        add_outer(*outer_terms(slot))
        own_pairs(w_ref)
        for ex in range(EX):
            r_ref[ex] -= free_scaled(w_ref[ex])
        return carry

    last = SMOOTH * CYCLES - 1
    lax.fori_loop(0, last, step, 0)
    smoother(rho_new * rho_old, 2.0 * rho_new / radius)
    own_pairs(u_ref)
    copies = send_faces(last % 2, 1)
    for ex in range(EX):
        x_ref[ex] += u_ref[ex]
    receive_faces(last % 2, copies, (x_ref,))

    by_node = [
        [
            jnp.concatenate(
                [x_ref[ex, a, pl.ds(c, 8, stride=8)] for a in range(NODES)], axis=0
            )
            for c in range(NODES)
        ]
        for ex in range(EX)
    ]
    rows = []
    for ex in range(EX):
        for ey in range(EY):
            halves = []
            for half in range(2):
                joined = None
                for s in range(4):
                    part = roll(by_node[ex][half * 4 + s], EZ * (s - ey))
                    joined = part if s == 0 else jnp.where(lane2 >= EZ * s, part, joined)
                halves.append(joined)
            rows.append(jnp.concatenate(halves, axis=1))
    result = exact_rows(jnp.concatenate(rows, axis=0), perm_ref[3])
    for half in range(2):
        at = slice(half * LANES, (half + 1) * LANES)
        for k in range(EX * EY):
            for a in range(NODES):
                first = k * 64 + a * 8
                w_ref[half, a, pl.ds(k, 8, stride=8)] = result[first : first + 8, at]
    for half in range(2):
        at = slice(half * LANES, (half + 1) * LANES)
        out_ref[:, :, at] = w_ref[half].reshape(128, EY, LANES)


def per_device(source, geometry, disc_mask, thrust, xxt_factor, col_count):
    n_gx = lax.axis_size("gx")
    n_gy = lax.axis_size("gy")
    levels = xxt_factor.shape[0]
    wide = (levels - 1) * XCOLS
    split = (n_gy.bit_length() - 1) * XCOLS
    matrices, plane, table, perms, interp, stiff, weights = constant_tables()
    field = (EX, NODES, 64, LANES)
    f32 = jnp.float32
    out = pl.pallas_call(
        functools.partial(kernel, n_gx, n_gy, levels, interp, stiff, weights),
        out_shape=jax.ShapeDtypeStruct((NODES * NODES * EX, EY, EZ * NODES), f32),
        in_specs=[pl.BlockSpec(memory_space=pl.ANY)] * 10,
        out_specs=pl.BlockSpec(memory_space=pltpu.VMEM),
        scratch_shapes=[
            pltpu.VMEM((NODES * NODES * EX, EY, EZ * NODES), f32),
            pltpu.VMEM(geometry.shape, f32),
            pltpu.VMEM(disc_mask.shape, jnp.int32),
            pltpu.VMEM(thrust.shape, f32),
            pltpu.VMEM((1, levels), jnp.int32),
            pltpu.VMEM(plane.shape, jnp.bfloat16),
            pltpu.VMEM(table.shape, f32),
            pltpu.VMEM(perms.shape, jnp.bfloat16),
            pltpu.VMEM((8, LANES), f32),
            pltpu.VMEM((1, LANES + wide), f32),
            pltpu.VMEM(field, f32),
            pltpu.VMEM(field, f32),
            pltpu.VMEM(field, f32),
            pltpu.VMEM(field, f32),
            pltpu.VMEM(field[1:], f32),
            pltpu.VMEM(field[1:], f32),
            pltpu.VMEM(field, f32),
            pltpu.VMEM(field, f32),
            pltpu.VMEM((64, 3 * LANES), f32),
            pltpu.VMEM((64, 3 * LANES), f32),
            pltpu.VMEM((64, 3 * LANES), f32),
            pltpu.VMEM((64, 3 * LANES), f32),
            pltpu.VMEM((2, 3, 8, LANES), f32),
            pltpu.VMEM((levels * XCOLS, xxt_factor.shape[2]), f32),
            pltpu.VMEM(matrices.shape, jnp.bfloat16),
            pltpu.VMEM((2, 2, 2, 64, LANES), f32),
            pltpu.VMEM((2, 2, 8, 8, LANES), f32),
            pltpu.VMEM((2, 4, 8, LANES), f32),
            pltpu.VMEM((2, 2, 2, 64, LANES), f32),
            pltpu.VMEM((2, 2, 2, 8, 8, LANES), f32),
            pltpu.VMEM((2, 4, 8, LANES), f32),
            pltpu.VMEM((8, 8, LANES), f32),
            pltpu.VMEM((1, wide), f32),
            pltpu.VMEM((CYCLES, n_gy - 1, 1, wide), f32),
            pltpu.VMEM((1, wide - split), f32),
            pltpu.VMEM((CYCLES, n_gx - 1, 1, wide - split), f32),
            pltpu.SemaphoreType.DMA((2, 8)),
            pltpu.SemaphoreType.DMA((2, 8)),
            pltpu.SemaphoreType.DMA((8,)),
            pltpu.SemaphoreType.DMA((8,)),
            pltpu.SemaphoreType.DMA((n_gy - 1,)),
            pltpu.SemaphoreType.DMA((CYCLES, n_gy - 1)),
            pltpu.SemaphoreType.DMA((n_gx - 1,)),
            pltpu.SemaphoreType.DMA((CYCLES, n_gx - 1)),
            pltpu.SemaphoreType.DMA((10,)),
        ],
        compiler_params=pltpu.CompilerParams(
            collective_id=0, has_side_effects=True, vmem_limit_bytes=56 * 1024 * 1024
        ),
    )(
        source.reshape(NODES * NODES * EX, EY, EZ * NODES),
        geometry,
        disc_mask,
        thrust,
        col_count.T,
        xxt_factor.reshape(levels * XCOLS, xxt_factor.shape[2]),
        jnp.asarray(matrices),
        jnp.asarray(plane),
        jnp.asarray(table),
        jnp.asarray(perms),
    )
    return out.reshape(source.shape)


def solution(mesh):
    return jax.shard_map(
        per_device,
        mesh=mesh,
        in_specs=(
            P(None, None, "gx", "gy", None),
            P(None, "gx", "gy", None),
            P("gx", "gy", None),
            P("gx", "gy", None),
            P(None, None, ("gx", "gy")),
            P(None, ("gx", "gy")),
        ),
        out_specs=P(None, None, "gx", "gy", None),
        check_vma=False,
    )
```
